32 devices in a mesh: dp: 8 (over z, y), seq: 4 (over x, core).
Axes of the slice: x: 2, y: 2, z: 4, core: 2. Of those that a mesh axis runs over, the one named last changes fastest.
Arguments:
- tokens: bfloat16 [16, 1024, 768], P('dp', 'seq'), may hold values from -6 to 6
- segment_ids: int32 [16, 1024], P('dp'), may hold values from 0 to 7, never falling along the last dimension, each value on 1 to 512 neighbouring positions
- w_qkv: bfloat16 [768, 2304], P(('dp', 'seq')), may hold values from -0.21875 to 0.21875
- b_qkv: bfloat16 [2304], P(('dp', 'seq')), may hold values from -1.796875 to 1.796875
- w_out: bfloat16 [768, 768], P(('dp', 'seq')), may hold values from -0.625 to 0.625
- b_out: bfloat16 [768], P(('dp', 'seq')), may hold values from -4 to 4
- ln1_gain: bfloat16 [768], P(('dp', 'seq')), may hold values from 0.25 to 1.75
- ln1_bias: bfloat16 [768], P(('dp', 'seq')), may hold values from -1.796875 to 1.796875
- w_in: bfloat16 [768, 3072], P(('dp', 'seq')), may hold values from -0.21875 to 0.21875
- b_in: bfloat16 [3072], P(('dp', 'seq')), may hold values from -1.796875 to 1.796875
- w_back: bfloat16 [3072, 768], P(('dp', 'seq')), may hold values from -0.15625 to 0.15625
- b_back: bfloat16 [768], P(('dp', 'seq')), may hold values from -1.796875 to 1.796875
- ln2_gain: bfloat16 [768], P(('dp', 'seq')), may hold values from 0.25 to 1.75
- ln2_bias: bfloat16 [768], P(('dp', 'seq')), may hold values from -1.796875 to 1.796875
- out_grad: bfloat16 [16, 1024, 768], P('dp', 'seq'), may hold values from -6 to 6
Outputs:
- layer_out: bfloat16 [16, 1024, 768], P('dp', 'seq')
- input_grad: float32 [16, 1024, 768], P('dp', 'seq')
- w_qkv_grad: float32 [768, 2304], P(('dp', 'seq'))
- b_qkv_grad: float32 [2304], P(('dp', 'seq'))
- w_out_grad: float32 [768, 768], P(('dp', 'seq'))
- b_out_grad: float32 [768], P(('dp', 'seq'))
- ln1_gain_grad: float32 [768], P(('dp', 'seq'))
- ln1_bias_grad: float32 [768], P(('dp', 'seq'))
- w_in_grad: float32 [768, 3072], P(('dp', 'seq'))
- b_in_grad: float32 [3072], P(('dp', 'seq'))
- w_back_grad: float32 [3072, 768], P(('dp', 'seq'))
- b_back_grad: float32 [768], P(('dp', 'seq'))
- ln2_gain_grad: float32 [768], P(('dp', 'seq'))
- ln2_bias_grad: float32 [768], P(('dp', 'seq'))
The draws below stay inside these ranges and needn't reach their ends.
Inputs may be any that keep to these rules, and one draw needn't show every extreme that they name: `segment_ids`: along each sequence the ids never fall; a document holds 1 to 512 tokens, and in every sequence one holds exactly 512.
All inputs are finite; a program needn't handle non-finite values.
Results may differ from the reference program's by a relative error of at most 0.034.
Values may be sent and summed in bfloat16 or wider, within the bound.
A program may use at most 320 MiB of HBM per device.

```python
import math
from functools import partial
import jax
import jax.numpy as jnp
import numpy as np
from jax import lax

D = 768
HEADS = 12
HD = 64
FF = 3072
DOCS = 8
LEN = 1024
SEQS = 16
LONGEST = 512


def raised(drawn, stream_key, source, target, parts, factor):
    def block_of(dim):
        return (jnp.arange(drawn.shape[dim]) // (drawn.shape[dim] // parts)).reshape((-1,) + (1,) * (drawn.ndim - 1 - dim))

    one_side = jax.random.permutation(stream_key, parts)[block_of(target)]
    other_side = (block_of(target) + parts // 2) % parts
    return jnp.where((block_of(source) == one_side) | (block_of(source) == other_side), factor * drawn, drawn)


def level_of(own_key, shape, shards, least, largest):
    level = 1.0
    for axis_at, blocks in shards:
        draws = jax.random.uniform(jax.random.fold_in(jax.random.fold_in(own_key, 6), axis_at), (blocks,), jnp.float32, least / len(shards), largest / len(shards))
        level = level * jnp.repeat(jnp.exp(draws), shape[axis_at] // blocks).reshape((-1,) + (1,) * (len(shape) - 1 - axis_at))
    return level


def split_up(count, total, bound, skew):
    loads = [(1 << 20) // math.isqrt(rank ** skew) + 1 for rank in range(2, count + 1)]
    rest, counts = total - bound - (count - 1), [1] * (count - 1)
    while rest > 0:
        candidates = [i for i in range(count - 1) if counts[i] < bound]
        pool, remaining = sum([loads[i] for i in candidates]), rest
        for i in candidates:
            more = min(bound - counts[i], max(1, remaining * loads[i] // pool), rest)
            counts[i] = counts[i] + more
            rest = rest - more
    return np.array([bound] + counts)


def uneven_parts(rng, number_of, total, bound, slope):
    if number_of == 2:
        one = jax.random.randint(rng, (), max(1, total - bound), min(bound, total - 1) + 1)
        return jnp.stack([one, total - one])
    tallies = jnp.asarray(split_up(number_of, total, bound, slope), jnp.int32)
    couples = (number_of - 1) // 2
    source_of, taker = tallies[1:1 + 2 * couples:2], tallies[2:2 + 2 * couples:2]
    margin = jnp.minimum(source_of - 1, bound - taker)
    passed = jax.random.randint(jax.random.fold_in(rng, 1), (couples,), 0, 1 << 20) % (margin + 1)
    tallies = tallies.at[1:1 + 2 * couples:2].set(source_of - passed).at[2:2 + 2 * couples:2].set(taker + passed)
    return tallies[jax.random.permutation(jax.random.fold_in(rng, 2), number_of)]


def noise(stream_key, shape, scale, bound, split=(), held_as=jnp.bfloat16):
    array = scale * jax.random.normal(stream_key, shape, jnp.float32)
    if split:
        array = array * level_of(stream_key, shape, split, -0.22, 0.18)
    return jnp.clip(array, -bound, bound).astype(held_as)


def gaussian_with(own_key, shape, width, reach, shards, heavy, kind=jnp.bfloat16):
    drawn = width * jax.random.normal(own_key, shape, jnp.float32)
    if shards:
        drawn = drawn * level_of(own_key, shape, shards, -0.22, 0.18)
    return jnp.clip(raised(drawn, jax.random.fold_in(own_key, 3), *heavy), -reach, reach).astype(kind)


def setup_inputs(seed: int = 0) -> dict:
    key_of = jax.random.split(jax.random.key(seed), 16)
    tokens = gaussian_with(key_of[0], (SEQS, LEN, D), 1.0, 6.0, ((0, 8), (1, 4)), (1, 2, 4, 2.0))
    segment_ids = jax.vmap(lambda own: jnp.searchsorted(jnp.cumsum(uneven_parts(own, DOCS, LEN, LONGEST, 2)), jnp.arange(LEN), side="right"))(jax.random.split(key_of[1], SEQS)).reshape((SEQS, LEN)).astype(jnp.int32)
    w_qkv = noise(key_of[2], (D, 3 * D), D ** -0.5, 0.21875, ((0, 32),))
    b_qkv = noise(key_of[3], (3 * D,), 0.3, 1.796875, ((0, 32),))
    w_out = noise(key_of[4], (D, D), (D // 8) ** -0.5, 0.625, ((0, 32),))
    b_out = noise(key_of[5], (D,), 1.0, 4.0, ((0, 32),))
    ln1_gain = jnp.clip(1.0 + 0.15 * jax.random.normal(key_of[6], (D,), jnp.float32), 0.25, 1.75).astype(jnp.bfloat16)
    ln1_bias = noise(key_of[7], (D,), 0.3, 1.796875, ((0, 32),))
    w_in = noise(key_of[8], (D, FF), D ** -0.5, 0.21875, ((0, 32),))
    b_in = noise(key_of[9], (FF,), 0.3, 1.796875, ((0, 32),))
    w_back = noise(key_of[10], (FF, D), (FF // 2) ** -0.5, 0.15625, ((0, 32),))
    b_back = noise(key_of[11], (D,), 0.3, 1.796875, ((0, 32),))
    ln2_gain = jnp.clip(1.0 + 0.15 * jax.random.normal(key_of[12], (D,), jnp.float32), 0.25, 1.75).astype(jnp.bfloat16)
    ln2_bias = noise(key_of[13], (D,), 0.3, 1.796875, ((0, 32),))
    out_grad = noise(key_of[14], (SEQS, LEN, D), 1.0, 6.0, ((0, 8), (1, 4)))
    return {"tokens": tokens, "segment_ids": segment_ids, "w_qkv": w_qkv, "b_qkv": b_qkv, "w_out": w_out, "b_out": b_out, "ln1_gain": ln1_gain, "ln1_bias": ln1_bias, "w_in": w_in, "b_in": b_in, "w_back": w_back, "b_back": b_back, "ln2_gain": ln2_gain, "ln2_bias": ln2_bias, "out_grad": out_grad}


@jax.custom_vjp
def low(v):
    return lax.optimization_barrier(v.astype(jnp.bfloat16)).astype(jnp.float32)

@jax.custom_vjp
def low_back(v):
    return v

def low_keep(v):
    return (low(v), None)

def low_pass(kept, grad):
    return (grad,)

def back_keep(v):
    return (v, None)

def back_low(kept, grad):
    return (low(grad),)
low.defvjp(low_keep, low_pass)
low_back.defvjp(back_keep, back_low)
EPSILON = 1e-06
HIGH = lax.Precision.HIGHEST

def layer_norm(values, gain_vec, shift_vec):
    center = values - lax.optimization_barrier(jnp.mean(values, axis=-1, keepdims=True))
    spread = lax.optimization_barrier(jnp.mean(center * center, axis=-1, keepdims=True))
    return center * lax.rsqrt(spread + EPSILON) * gain_vec + shift_vec

def gelu_exact(values):
    return jax.nn.gelu(values, approximate=False)

def rotary_tables(segments):
    length = segments.shape[0]
    places = jnp.arange(length, dtype=jnp.int32)
    change = jnp.concatenate([jnp.ones((1,), dtype=bool), segments[1:] != segments[:-1]])
    starts = lax.cummax(jnp.where(change, places, jnp.zeros_like(places)), axis=0)
    position = (places - starts).astype(jnp.float32)
    half_size = HD // 2
    inverse = 10000.0 ** (-2.0 * jnp.arange(half_size, dtype=jnp.float32) / HD)
    angles = position[:, None] * inverse[None, :]
    return (jnp.cos(angles), jnp.sin(angles))

def rotate(values, cos_part, sin_part):
    row_count = values.shape[0]
    paired = values.reshape(row_count, HEADS, HD // 2, 2)
    even_part = paired[..., 0]
    odd_part = paired[..., 1]
    cos_wide = cos_part[:, None, :]
    sin_wide = sin_part[:, None, :]
    turned = jnp.stack([even_part * cos_wide - odd_part * sin_wide, even_part * sin_wide + odd_part * cos_wide], axis=-1)
    return turned.reshape(row_count, HEADS * HD)

def attend_block(query_block, key_rot, value_rot, segments):
    query_part, seg_part = query_block
    raw_scores = low_back(jnp.einsum('qhd,khd->hqk', query_part, key_rot, precision=HIGH))
    same_doc = seg_part[:, None] == segments[None, :]
    scores = jnp.where(same_doc[None], raw_scores * HD ** (-0.5), -1e+30)
    highest = lax.optimization_barrier(jnp.max(scores, axis=-1, keepdims=True))
    exponent = jnp.exp(scores - highest)
    attention = exponent / lax.optimization_barrier(jnp.sum(exponent, axis=-1, keepdims=True))
    return jnp.einsum('hqk,khd->qhd', low(attention), value_rot, precision=HIGH)

def layer_forward(tokens_f, segments, w_qkv, b_qkv, w_out, b_out, gain_one, shift_one, w_in, b_in, w_back, b_back, gain_two, shift_two):
    length = tokens_f.shape[0]
    cos_part, sin_part = rotary_tables(segments)
    joined_qkv = low_back(jnp.dot(tokens_f, w_qkv, precision=HIGH) + b_qkv)
    query_rot = low(rotate(joined_qkv[:, :D], cos_part, sin_part)).reshape(length, HEADS, HD)
    key_rot = low(rotate(joined_qkv[:, D:2 * D], cos_part, sin_part)).reshape(length, HEADS, HD)
    value_rot = low(joined_qkv[:, 2 * D:]).reshape(length, HEADS, HD)
    block_rows = min(512, length)
    blocks = length // block_rows
    attend = jax.checkpoint(partial(attend_block, key_rot=key_rot, value_rot=value_rot, segments=segments))
    mixed_out = lax.map(attend, (query_rot.reshape(blocks, block_rows, HEADS, HD), segments.reshape(blocks, block_rows)))
    mixed_out = low(low_back(mixed_out.reshape(length, D)))
    branch = low_back(jnp.dot(mixed_out, w_out, precision=HIGH) + b_out)
    normed = layer_norm(tokens_f + branch, gain_one, shift_one)
    inner_act = low_back(jnp.dot(low(normed), w_in, precision=HIGH) + b_in)
    active = low(gelu_exact(inner_act))
    second = low_back(jnp.dot(active, w_back, precision=HIGH) + b_back)
    return layer_norm(normed + second, gain_two, shift_two)

def reference(tokens, segment_ids, w_qkv, b_qkv, w_out, b_out, ln1_gain, ln1_bias, w_in, b_in, w_back, b_back, ln2_gain, ln2_bias, out_grad):
    params = tuple((weight_item.astype(jnp.float32) for weight_item in (w_qkv, b_qkv, w_out, b_out, ln1_gain, ln1_bias, w_in, b_in, w_back, b_back, ln2_gain, ln2_bias)))

    def one_sequence(totals, inputs):
        seq_tokens, seq_ids, seq_grad = inputs

        def forward(tokens_f, *weights):
            return layer_forward(tokens_f, seq_ids, *weights)
        result, pull_back = jax.vjp(forward, seq_tokens.astype(jnp.float32), *params)
        grad_set = pull_back(seq_grad.astype(jnp.float32))
        totals = jax.tree.map(jnp.add, totals, tuple(grad_set[1:]))
        return (totals, (result.astype(jnp.bfloat16), grad_set[0]))
    zeros_set = tuple((jnp.zeros(weight_item.shape, jnp.float32) for weight_item in params))
    sums_all, outputs = lax.scan(one_sequence, zeros_set, (tokens, segment_ids, out_grad))
    layer_out, input_grad = outputs
    return (layer_out, input_grad, sums_all[0], sums_all[1], sums_all[2], sums_all[3], sums_all[4], sums_all[5], sums_all[6], sums_all[7], sums_all[8], sums_all[9], sums_all[10], sums_all[11])
```

```python
import jax
import jax.numpy as jnp
from jax import lax
from jax.sharding import PartitionSpec as P

D = 768
HEADS = 12
HD = 64
FF = 3072
EPSILON = 1e-06
ALL = ("dp", "seq")
BF = jnp.bfloat16
F32 = jnp.float32
SMALL = (3 * D, D, D, D, FF, D, D, D)


def mm(a, b):
    return jnp.dot(a, b, preferred_element_type=F32)


def layer_norm(values, gain_vec, shift_vec):
    center = values - jnp.mean(values, axis=-1, keepdims=True)
    spread = jnp.mean(center * center, axis=-1, keepdims=True)
    return center * lax.rsqrt(spread + EPSILON) * gain_vec + shift_vec


def gelu_exact(values):
    return jax.nn.gelu(values, approximate=False)


def rotary_tables(segments, offset, row_count):
    length = segments.shape[-1]
    places = jnp.arange(length, dtype=jnp.int32)[None]
    change = jnp.concatenate(
        [jnp.ones((segments.shape[0], 1), dtype=bool), segments[:, 1:] != segments[:, :-1]], axis=1
    )
    starts = lax.cummax(jnp.where(change, places, 0), axis=1)
    position = lax.dynamic_slice_in_dim(places - starts, offset, row_count, 1).astype(F32)
    inverse = 10000.0 ** (-2.0 * jnp.arange(HD // 2, dtype=F32) / HD)
    angles = position[..., None] * inverse
    return jnp.cos(angles), jnp.sin(angles)


def rotate(values, cos_part, sin_part):
    paired = values.reshape(values.shape[:-1] + (HEADS, HD // 2, 2))
    even, odd = paired[..., 0], paired[..., 1]
    cos_wide, sin_wide = cos_part[..., None, :], sin_part[..., None, :]
    turned = jnp.stack(
        [even * cos_wide - odd * sin_wide, even * sin_wide + odd * cos_wide], axis=-1
    )
    return turned.reshape(values.shape)


def gather(local):
    return lax.all_gather(local, ALL, axis=0, tiled=True)


def gather_small(parts):
    joined = gather(jnp.concatenate(parts)[None])
    out, at = [], 0
    for part in parts:
        n = part.shape[0]
        out.append(joined[:, at : at + n].reshape(-1))
        at += n
    return out


def scatter_small(sums, devices):
    joined = jnp.concatenate([s.reshape(devices, -1) for s in sums], axis=1)
    own = lax.psum_scatter(joined, ALL, scatter_dimension=0, tiled=True)[0]
    out, at = [], 0
    for s in sums:
        n = s.shape[0] // devices
        out.append(own[at : at + n])
        at += n
    return out


def scatter(grad):
    return lax.psum_scatter(grad.astype(BF), ALL, scatter_dimension=0, tiled=True).astype(F32)


def heads(values):
    return values.reshape(values.shape[0], values.shape[1], HEADS, HD)


def scores_of(query, key_all, same_doc):
    raw = jnp.einsum("bqhd,bkhd->bhqk", heads(query), heads(key_all), preferred_element_type=F32)
    return jnp.where(same_doc[:, None], raw * HD ** (-0.5), -1e30)


def on_device(devices, *args):
    (tokens, segment_ids, w_qkv, b_qkv, w_out, b_out, gain_one, shift_one) = args[:8]
    (w_in, b_in, w_back, b_back, gain_two, shift_two, out_grad) = args[8:]
    b_qkv, b_out, gain_one, shift_one, b_in, b_back, gain_two, shift_two = [
        v.astype(F32)
        for v in gather_small([b_qkv, b_out, gain_one, shift_one, b_in, b_back, gain_two, shift_two])
    ]
    w_qkv, w_out, w_in, w_back = gather(w_qkv), gather(w_out), gather(w_in), gather(w_back)
    batch, rows = tokens.shape[:2]
    flat = (batch * rows, D)
    offset = lax.axis_index("seq") * rows
    cos_part, sin_part = rotary_tables(segment_ids, offset, rows)
    own_ids = lax.dynamic_slice_in_dim(segment_ids, offset, rows, 1)
    same_doc = own_ids[:, :, None] == segment_ids[:, None, :]

    tok = tokens.reshape(flat)
    joined = (mm(tok, w_qkv) + b_qkv).reshape(batch, rows, 3 * D)
    query = rotate(joined[..., :D], cos_part, sin_part).astype(BF)
    key = rotate(joined[..., D : 2 * D], cos_part, sin_part).astype(BF)
    value = joined[..., 2 * D :].astype(BF)
    key_all = lax.all_gather(key, "seq", axis=1, tiled=True)
    value_all = lax.all_gather(value, "seq", axis=1, tiled=True)
    keys = key_all.shape[1]
    scores = scores_of(query, key_all, same_doc)
    highest = jnp.max(scores, axis=-1, keepdims=True)
    exponent = jnp.exp(scores - highest)
    total = jnp.sum(exponent, axis=-1, keepdims=True)
    log_total = highest + jnp.log(total)
    mixed = jnp.einsum(
        "bhqk,bkhd->bqhd", (exponent / total).astype(BF), heads(value_all),
        preferred_element_type=F32,
    ).astype(BF).reshape(flat)
    first_sum = tok.astype(F32) + mm(mixed, w_out) + b_out
    normed = layer_norm(first_sum, gain_one, shift_one)
    normed_low = normed.astype(BF)
    inner = mm(normed_low, w_in) + b_in
    active = gelu_exact(inner).astype(BF)
    second_sum = normed + mm(active, w_back) + b_back
    result, pull_two = jax.vjp(layer_norm, second_sum, gain_two, shift_two)
    layer_out = result.astype(BF).reshape(tokens.shape)

    d_second_sum, d_gain_two, d_shift_two = pull_two(out_grad.reshape(flat).astype(F32))
    d_second = d_second_sum.astype(BF)
    d_b_back = jnp.sum(d_second.astype(F32), axis=0)
    d_w_back = scatter(jnp.einsum("qf,qd->fd", active, d_second, preferred_element_type=F32))
    d_active = jnp.einsum("qd,fd->qf", d_second, w_back, preferred_element_type=F32)
    d_inner = jax.vjp(gelu_exact, inner)[1](d_active)[0].astype(BF)
    d_b_in = jnp.sum(d_inner.astype(F32), axis=0)
    d_w_in = scatter(jnp.einsum("qd,qf->df", normed_low, d_inner, preferred_element_type=F32))
    d_normed = d_second_sum + jnp.einsum("qf,df->qd", d_inner, w_in, preferred_element_type=F32)
    d_first_sum, d_gain_one, d_shift_one = jax.vjp(layer_norm, first_sum, gain_one, shift_one)[1](
        d_normed
    )
    d_branch = d_first_sum.astype(BF)
    d_b_out = jnp.sum(d_branch.astype(F32), axis=0)
    d_w_out = scatter(jnp.einsum("qd,qe->de", mixed, d_branch, preferred_element_type=F32))
    d_mixed = jnp.einsum("qe,de->qd", d_branch, w_out, preferred_element_type=F32).astype(BF)
    d_mixed = d_mixed.reshape(batch, rows, D)

    attention = jnp.exp(scores_of(query, key_all, same_doc) - log_total)
    d_attention = jnp.einsum(
        "bqhd,bkhd->bhqk", heads(d_mixed), heads(value_all), preferred_element_type=F32
    )
    inner_sum = jnp.sum(d_attention * attention, axis=-1, keepdims=True)
    d_scores = (attention * (d_attention - inner_sum) * HD ** (-0.5)).astype(BF)
    d_query = jnp.einsum(
        "bhqk,bkhd->bqhd", d_scores, heads(key_all), preferred_element_type=F32
    ).reshape(batch, rows, D)
    d_value = jnp.einsum(
        "bhqk,bqhd->bkhd", attention.astype(BF), heads(d_mixed), preferred_element_type=F32
    ).reshape(batch, keys, D)
    d_key = jnp.einsum(
        "bhqk,bqhd->bkhd", d_scores, heads(query), preferred_element_type=F32
    ).reshape(batch, keys, D)
    d_key = lax.psum_scatter(d_key.astype(BF), "seq", scatter_dimension=1, tiled=True).astype(F32)
    d_value = lax.psum_scatter(d_value.astype(BF), "seq", scatter_dimension=1, tiled=True)
    d_joined = jnp.concatenate(
        [
            rotate(d_query, cos_part, -sin_part).astype(BF),
            rotate(d_key, cos_part, -sin_part).astype(BF),
            d_value,
        ],
        axis=-1,
    ).reshape(batch * rows, 3 * D)
    d_b_qkv = jnp.sum(d_joined.astype(F32), axis=0)
    d_w_qkv = scatter(jnp.einsum("qd,qe->de", tok, d_joined, preferred_element_type=F32))
    d_tokens = (
        jnp.einsum("qe,de->qd", d_joined, w_qkv, preferred_element_type=F32) + d_first_sum
    ).reshape(tokens.shape)
    small = scatter_small(
        [d_b_qkv, d_b_out, d_gain_one, d_shift_one, d_b_in, d_b_back, d_gain_two, d_shift_two],
        devices,
    )
    return (
        layer_out, d_tokens, d_w_qkv, small[0], d_w_out, small[1], small[2], small[3],
        d_w_in, small[4], d_w_back, small[5], small[6], small[7],
    )


def solution(mesh):
    devices = mesh.shape["dp"] * mesh.shape["seq"]
    rows3 = P("dp", "seq", None)
    mat, vec = P(ALL, None), P(ALL)
    params = (mat, vec, mat, vec, vec, vec, mat, vec, mat, vec, vec, vec)
    return jax.shard_map(
        lambda *args: on_device(devices, *args),
        mesh=mesh,
        in_specs=(rows3, P("dp", None)) + params + (rows3,),
        out_specs=(rows3, rows3) + params,
        check_vma=False,
    )
```

```python
import functools
import jax
import jax.numpy as jnp
from jax import lax
from jax.experimental import pallas as pl
from jax.experimental.pallas import tpu as pltpu
from jax.sharding import PartitionSpec as P

D = 768
HEADS = 12
HD = 64
FF = 3072
EPSILON = 1e-06
ALL = ("dp", "seq")
BF = jnp.bfloat16
F32 = jnp.float32


def mm(a, b):
    return jnp.dot(a, b, preferred_element_type=F32)


def layer_norm(values, gain_vec, shift_vec):
    center = values - jnp.mean(values, axis=-1, keepdims=True)
    spread = jnp.mean(center * center, axis=-1, keepdims=True)
    return center * lax.rsqrt(spread + EPSILON) * gain_vec + shift_vec


def gelu_exact(values):
    return jax.nn.gelu(values, approximate=False)


def rotary_tables(segments, offset, row_count):
    length = segments.shape[-1]
    places = jnp.arange(length, dtype=jnp.int32)[None]
    change = jnp.concatenate(
        [jnp.ones((segments.shape[0], 1), dtype=bool), segments[:, 1:] != segments[:, :-1]], axis=1
    )
    starts = lax.cummax(jnp.where(change, places, 0), axis=1)
    position = lax.dynamic_slice_in_dim(places - starts, offset, row_count, 1).astype(F32)
    inverse = 10000.0 ** (-2.0 * jnp.arange(HD // 2, dtype=F32) / HD)
    angles = position[..., None] * inverse
    return jnp.cos(angles), jnp.sin(angles)


def rotate(values, cos_part, sin_part):
    paired = values.reshape(values.shape[:-1] + (HEADS, HD // 2, 2))
    even, odd = paired[..., 0], paired[..., 1]
    cos_wide, sin_wide = cos_part[..., None, :], sin_part[..., None, :]
    turned = jnp.stack(
        [even * cos_wide - odd * sin_wide, even * sin_wide + odd * cos_wide], axis=-1
    )
    return turned.reshape(values.shape)


def gather(local):
    return lax.all_gather(local, ALL, axis=0, tiled=True)


def gather_small(parts):
    joined = gather(jnp.concatenate(parts)[None])
    out, at = [], 0
    for part in parts:
        n = part.shape[0]
        out.append(joined[:, at : at + n].reshape(-1))
        at += n
    return out


def scatter_small(sums, devices):
    joined = jnp.concatenate([s.reshape(devices, -1) for s in sums], axis=1)
    own = lax.psum_scatter(joined, ALL, scatter_dimension=0, tiled=True)[0]
    out, at = [], 0
    for s in sums:
        n = s.shape[0] // devices
        out.append(own[at : at + n])
        at += n
    return out


def scatter(grad):
    return lax.psum_scatter(grad.astype(BF), ALL, scatter_dimension=0, tiled=True).astype(F32)


def heads(values):
    return values.reshape(values.shape[0], values.shape[1], HEADS, HD)


def scores_of(query, key_all, same_doc):
    raw = jnp.einsum("bqhd,bkhd->bhqk", heads(query), heads(key_all), preferred_element_type=F32)
    return jnp.where(same_doc[:, None], raw * HD ** (-0.5), -1e30)


def on_device(devices, *args):
    (tokens, segment_ids, w_qkv, b_qkv, w_out, b_out, gain_one, shift_one) = args[:8]
    (w_in, b_in, w_back, b_back, gain_two, shift_two, out_grad) = args[8:]
    b_qkv, b_out, gain_one, shift_one, b_in, b_back, gain_two, shift_two = [
        v.astype(F32)
        for v in gather_small([b_qkv, b_out, gain_one, shift_one, b_in, b_back, gain_two, shift_two])
    ]
    w_qkv, w_out, w_in, w_back = gather(w_qkv), gather(w_out), gather(w_in), gather(w_back)
    batch, rows = tokens.shape[:2]
    flat = (batch * rows, D)
    offset = lax.axis_index("seq") * rows
    cos_part, sin_part = rotary_tables(segment_ids, offset, rows)
    own_ids = lax.dynamic_slice_in_dim(segment_ids, offset, rows, 1)
    same_doc = own_ids[:, :, None] == segment_ids[:, None, :]

    tok = tokens.reshape(flat)
    joined = (mm(tok, w_qkv) + b_qkv).reshape(batch, rows, 3 * D)
    query = rotate(joined[..., :D], cos_part, sin_part).astype(BF)
    key = rotate(joined[..., D : 2 * D], cos_part, sin_part).astype(BF)
    value = joined[..., 2 * D :].astype(BF)
    key_all = lax.all_gather(key, "seq", axis=1, tiled=True)
    value_all = lax.all_gather(value, "seq", axis=1, tiled=True)
    keys = key_all.shape[1]
    scores = scores_of(query, key_all, same_doc)
    highest = jnp.max(scores, axis=-1, keepdims=True)
    exponent = jnp.exp(scores - highest)
    total = jnp.sum(exponent, axis=-1, keepdims=True)
    log_total = highest + jnp.log(total)
    mixed = jnp.einsum(
        "bhqk,bkhd->bqhd", (exponent / total).astype(BF), heads(value_all),
        preferred_element_type=F32,
    ).astype(BF).reshape(flat)
    first_sum = tok.astype(F32) + mm(mixed, w_out) + b_out
    normed = layer_norm(first_sum, gain_one, shift_one)
    normed_low = normed.astype(BF)
    inner = mm(normed_low, w_in) + b_in
    active = gelu_exact(inner).astype(BF)
    second_sum = normed + mm(active, w_back) + b_back
    result, pull_two = jax.vjp(layer_norm, second_sum, gain_two, shift_two)
    layer_out = result.astype(BF).reshape(tokens.shape)

    d_second_sum, d_gain_two, d_shift_two = pull_two(out_grad.reshape(flat).astype(F32))
    d_second = d_second_sum.astype(BF)
    d_b_back = jnp.sum(d_second.astype(F32), axis=0)
    d_w_back = scatter(jnp.einsum("qf,qd->fd", active, d_second, preferred_element_type=F32))
    d_active = jnp.einsum("qd,fd->qf", d_second, w_back, preferred_element_type=F32)
    d_inner = jax.vjp(gelu_exact, inner)[1](d_active)[0].astype(BF)
    d_b_in = jnp.sum(d_inner.astype(F32), axis=0)
    d_w_in = scatter(jnp.einsum("qd,qf->df", normed_low, d_inner, preferred_element_type=F32))
    d_normed = d_second_sum + jnp.einsum("qf,df->qd", d_inner, w_in, preferred_element_type=F32)
    d_first_sum, d_gain_one, d_shift_one = jax.vjp(layer_norm, first_sum, gain_one, shift_one)[1](
        d_normed
    )
    d_branch = d_first_sum.astype(BF)
    d_b_out = jnp.sum(d_branch.astype(F32), axis=0)
    d_w_out = scatter(jnp.einsum("qd,qe->de", mixed, d_branch, preferred_element_type=F32))
    d_mixed = jnp.einsum("qe,de->qd", d_branch, w_out, preferred_element_type=F32).astype(BF)
    d_mixed = d_mixed.reshape(batch, rows, D)

    attention = jnp.exp(scores_of(query, key_all, same_doc) - log_total)
    d_attention = jnp.einsum(
        "bqhd,bkhd->bhqk", heads(d_mixed), heads(value_all), preferred_element_type=F32
    )
    inner_sum = jnp.sum(d_attention * attention, axis=-1, keepdims=True)
    d_scores = (attention * (d_attention - inner_sum) * HD ** (-0.5)).astype(BF)
    d_query = jnp.einsum(
        "bhqk,bkhd->bqhd", d_scores, heads(key_all), preferred_element_type=F32
    ).reshape(batch, rows, D)
    d_value = jnp.einsum(
        "bhqk,bqhd->bkhd", attention.astype(BF), heads(d_mixed), preferred_element_type=F32
    ).reshape(batch, keys, D)
    d_key = jnp.einsum(
        "bhqk,bqhd->bkhd", d_scores, heads(query), preferred_element_type=F32
    ).reshape(batch, keys, D)
    d_key = lax.psum_scatter(d_key.astype(BF), "seq", scatter_dimension=1, tiled=True).astype(F32)
    d_value = lax.psum_scatter(d_value.astype(BF), "seq", scatter_dimension=1, tiled=True)
    d_joined = jnp.concatenate(
        [
            rotate(d_query, cos_part, -sin_part).astype(BF),
            rotate(d_key, cos_part, -sin_part).astype(BF),
            d_value,
        ],
        axis=-1,
    ).reshape(batch * rows, 3 * D)
    d_b_qkv = jnp.sum(d_joined.astype(F32), axis=0)
    d_w_qkv = scatter(jnp.einsum("qd,qe->de", tok, d_joined, preferred_element_type=F32))
    d_tokens = (
        jnp.einsum("qe,de->qd", d_joined, w_qkv, preferred_element_type=F32) + d_first_sum
    ).reshape(tokens.shape)
    small = scatter_small(
        [d_b_qkv, d_b_out, d_gain_one, d_shift_one, d_b_in, d_b_back, d_gain_two, d_shift_two],
        devices,
    )
    return (
        layer_out, d_tokens, d_w_qkv, small[0], d_w_out, small[1], small[2], small[3],
        d_w_in, small[4], d_w_back, small[5], small[6], small[7],
    )


NZ = 4
HBM = pl.BlockSpec(memory_space=pl.ANY)


def place():
    dp, seq = lax.axis_index("dp"), lax.axis_index("seq")
    return dp // 2, dp % 2, seq // 2, seq % 2


def device(z, y, x, c):
    return (z * 2 + y, x * 2 + c)


def z_order(k, z):
    low = z < 2
    near = jnp.where(low, z, 3 - z)
    second = {0: 1, 1: 0, 2: 2, 3: 3}[k]
    found = jnp.where(near == 0, k, second)
    return jnp.where(low, found, 3 - found)


def greet():
    z, y, x, c = place()
    barrier = pltpu.get_barrier_semaphore()

    def signal(target):
        pl.semaphore_signal(
            barrier, inc=1, device_id=target, device_id_type=pl.DeviceIdType.MESH
        )

    signal(device(z, y, x, 1 - c))
    signal(device(z, y, 1 - x, c))
    signal(device(z, 1 - y, x, c))
    pl.when(z < NZ - 1)(lambda: signal(device(z + 1, y, x, c)))
    pl.when(z > 0)(lambda: signal(device(z - 1, y, x, c)))
    pl.semaphore_wait(barrier, 3 + (z < NZ - 1).astype(jnp.int32) + (z > 0).astype(jnp.int32))


class Mail:
    def __init__(self, send_sems, recv_sems):
        self.send_sems, self.recv_sems = send_sems, recv_sems
        self.sent, self.slots = [], 0

    def slot(self, count):
        at = self.slots
        self.slots += count
        return at

    def send(self, src, dst, slot, target, cond=None):
        copy = pltpu.make_async_remote_copy(
            src_ref=src, dst_ref=dst, send_sem=self.send_sems.at[len(self.sent)],
            recv_sem=self.recv_sems.at[slot], device_id=target,
            device_id_type=pl.DeviceIdType.MESH,
        )
        self.sent.append((copy, cond))
        if cond is None:
            copy.start()
        else:
            pl.when(cond)(copy.start)

    def arrived(self, dst, slot, cond=None):
        z, y, x, c = place()
        copy = pltpu.make_async_remote_copy(
            src_ref=dst, dst_ref=dst, send_sem=self.send_sems.at[0],
            recv_sem=self.recv_sems.at[slot], device_id=device(z, y, x, 1 - c),
            device_id_type=pl.DeviceIdType.MESH,
        )
        if cond is None:
            copy.wait_recv()
        else:
            pl.when(cond)(copy.wait_recv)

    def finish(self):
        for copy, cond in self.sent:
            if cond is None:
                copy.wait_send()
            else:
                pl.when(cond)(copy.wait_send)


def along_z(mail, block, slot, zz, k):
    z, y, x, c = place()
    if k == 0:
        mail.send(block, block, slot + z, device(z + 1, y, x, c), z < NZ - 1)
        mail.send(block, block, slot + z, device(z - 1, y, x, c), z > 0)
    else:
        up = zz < z
        cond = jnp.where(up, (z < NZ - 1).astype(jnp.int32), (z > 0).astype(jnp.int32)) == 1
        mail.send(block, block, slot + zz, device(jnp.where(up, z + 1, z - 1), y, x, c), cond)


def gather_unit(mail, order, out, own_copy):
    z, y, x, c = place()
    both = pl.ds(0, 2)
    to_x, to_y = device(z, y, 1 - x, c), device(z, 1 - y, x, c)
    to_core = device(z, y, x, 1 - c)
    core = []

    def pair(src, slot):
        core.append(slot)
        mail.send(src, src, slot, to_core)

    own_copy.wait()
    if order in ("zyx", "zxy"):
        first, second = (to_y, to_x) if order == "zyx" else (to_x, to_y)

        def at(zz, one, two):
            if order == "zyx":
                yy = both if one is None else (1 - y if one else y)
                return out.at[zz, yy, 1 - x if two else x, c]
            xx = both if one is None else (1 - x if one else x)
            return out.at[zz, 1 - y if two else y, xx, c]

        s_z, s_one, s_two, s_c = mail.slot(4), mail.slot(4), mail.slot(4), mail.slot(8)
        along_z(mail, at(z, 0, 0), s_z, z, 0)
        mail.send(at(z, 0, 0), at(z, 0, 0), s_one + z, first)
        for k in (1, 2, 3):
            yield
            zz = z_order(k, z)
            mail.arrived(at(zz, 0, 0), s_z + zz)
            along_z(mail, at(zz, 0, 0), s_z, zz, k)
            mail.send(at(zz, 0, 0), at(zz, 0, 0), s_one + zz, first)
        for k in range(4):
            yield
            zz = z_order(k, z)
            mail.arrived(at(zz, 1, 0), s_one + zz)
            mail.send(at(zz, None, 0), at(zz, None, 0), s_two + zz, second)
            mail.send(at(zz, None, 0), at(zz, None, 0), s_c + zz, to_core)
        for k in range(4):
            yield
            zz = z_order(k, z)
            mail.arrived(at(zz, None, 1), s_two + zz)
            mail.send(at(zz, None, 1), at(zz, None, 1), s_c + 4 + zz, to_core)
        for k in range(8):
            yield
            if order == "zyx":
                landed = out.at[z_order(k % 4, z), both, x if k < 4 else 1 - x, 1 - c]
            else:
                landed = out.at[z_order(k % 4, z), y if k < 4 else 1 - y, both, 1 - c]
            mail.arrived(landed, s_c + (k // 4) * 4 + z_order(k % 4, z))
    elif order == "xyz":
        s_x, s_y, s_z, s_c = mail.slot(1), mail.slot(1), mail.slot(4), mail.slot(4)
        mail.send(out.at[z, y, x, c], out.at[z, y, x, c], s_x, to_x)
        yield
        mail.arrived(out.at[z, y, 1 - x, c], s_x)
        mail.send(out.at[z, y, both, c], out.at[z, y, both, c], s_y, to_y)
        yield
        mail.arrived(out.at[z, 1 - y, both, c], s_y)
        for k in range(4):
            zz = z_order(k, z)
            block = out.at[zz, both, both, c]
            if k:
                yield
                mail.arrived(block, s_z + zz)
            along_z(mail, block, s_z, zz, k)
            mail.send(block, block, s_c + zz, to_core)
        for k in range(4):
            yield
            zz = z_order(k, z)
            mail.arrived(out.at[zz, both, both, 1 - c], s_c + zz)
    else:
        s_x, s_y, s_z, s_c = mail.slot(1), mail.slot(4), mail.slot(4), mail.slot(4)
        mail.send(out.at[z, y, x, c], out.at[z, y, x, c], s_x, to_x)
        yield
        mail.arrived(out.at[z, y, 1 - x, c], s_x)
        for k in range(4):
            zz = z_order(k, z)
            block = out.at[zz, y, both, c]
            if k:
                yield
                mail.arrived(block, s_z + zz)
            along_z(mail, block, s_z, zz, k)
            mail.send(block, block, s_y + zz, to_y)
        for k in range(4):
            yield
            zz = z_order(k, z)
            mail.arrived(out.at[zz, 1 - y, both, c], s_y + zz)
            block = out.at[zz, both, both, c]
            mail.send(block, block, s_c + zz, to_core)
        for k in range(4):
            yield
            zz = z_order(k, z)
            mail.arrived(out.at[zz, both, both, 1 - c], s_c + zz)


def run_together(routines):
    live = list(routines)
    while live:
        live = [r for r in live if next(r, "end") != "end"]


SENDS, RECVS = 160, 160


def gather_kernel(orders, *refs):
    n = len(orders)
    srcs, outs = refs[:n], refs[n : 2 * n]
    send_sems, recv_sems, own_sems = refs[2 * n :]
    z, y, x, c = place()
    copies = [
        pltpu.make_async_copy(s, o.at[z, y, x, c], own_sems.at[i])
        for i, (s, o) in enumerate(zip(srcs, outs))
    ]
    for copy in copies:
        copy.start()
    greet()
    mail = Mail(send_sems, recv_sems)
    run_together([gather_unit(mail, o, out, cp) for o, out, cp in zip(orders, outs, copies)])
    mail.finish()


def gather_all(parts, orders, collective_id):
    shapes = [jax.ShapeDtypeStruct((4, 2, 2, 2) + p.shape, p.dtype) for p in parts]
    outs = pl.pallas_call(
        functools.partial(gather_kernel, orders),
        out_shape=shapes,
        in_specs=[HBM] * len(parts),
        out_specs=[HBM] * len(parts),
        scratch_shapes=[
            pltpu.SemaphoreType.DMA((SENDS,)),
            pltpu.SemaphoreType.DMA((RECVS,)),
            pltpu.SemaphoreType.DMA((len(parts),)),
        ],
        compiler_params=pltpu.CompilerParams(collective_id=collective_id, has_side_effects=True),
    )(*parts)
    return [o.reshape((32,) + p.shape) for o, p in zip(outs, parts)]


def add_into(acc, others, cols):
    step = 384 if cols % 384 == 0 else 128

    def chunk(i, _):
        at = pl.ds(pl.multiple_of(i * step, step), step)
        where = tuple(slice(None) for _ in range(len(acc.shape) - 1)) + (at,)
        total = acc[where].astype(F32)
        for other in others:
            total = total + other[where].astype(F32)
        acc[where] = total.astype(acc.dtype)
        return 0

    lax.fori_loop(0, cols // step, chunk, 0)


def reduce_unit(mail, order, grad, refs, local_sem, out):
    acc, from_core, from_x, from_y, from_z = refs
    cols = grad.shape[-1]
    z, y, x, c = place()
    both = pl.ds(0, 2)
    to_x, to_y = device(z, y, 1 - x, c), device(z, 1 - y, x, c)
    to_core = device(z, y, x, 1 - c)
    own = pltpu.make_async_copy(grad.at[:, :, :, c], acc, local_sem)
    own.start()
    s_c, s_z = mail.slot(4), mail.slot(8)
    for k in range(4):
        zz = z_order(3 - k, z)
        mail.send(grad.at[zz, :, :, 1 - c], from_core.at[zz], s_c + zz, to_core)

    def line(pick, k, zz):
        block = acc.at[(zz,) + pick]
        if k < 3:
            up = zz > z
            more = jnp.where(up, (z > 0).astype(jnp.int32), (z < NZ - 1).astype(jnp.int32)) == 1
            side = jnp.where(up, 0, 1)
            landed = from_z.at[side, zz]

            def take():
                mail.arrived(landed, s_z + side * 4 + zz)
                add_into(block, [landed], cols)

            pl.when(more)(take)
            mail.send(block, landed, s_z + side * 4 + zz, device(jnp.where(up, z + 1, z - 1), y, x, c))
        else:
            for side, there in ((0, z > 0), (1, z < NZ - 1)):
                landed = from_z.at[side, zz]

                def take(landed=landed, side=side):
                    mail.arrived(landed, s_z + side * 4 + zz)
                    add_into(block, [landed], cols)

                pl.when(there)(take)

    if order in ("zyx", "zxy"):
        flip = order == "zxy"
        if flip:
            part = lambda zz, one, two: (zz, 1 - y if two else y, both if one is None else (1 - x if one else x))
            far, near, to_far, to_near = from_y, from_x, to_y, to_x
        else:
            part = lambda zz, one, two: (zz, both if one is None else (1 - y if one else y), 1 - x if two else x)
            far, near, to_far, to_near = from_x, from_y, to_x, to_y
        s_far, s_near = mail.slot(4), mail.slot(4)
        for k in range(4):
            yield
            zz = z_order(3 - k, z)
            if k == 0:
                own.wait()
            mail.arrived(from_core.at[zz], s_c + zz)
            add_into(acc.at[zz], [from_core.at[zz]], cols)
            mail.send(acc.at[part(zz, None, 1)], far.at[zz], s_far + zz, to_far)
        for k in range(4):
            yield
            zz = z_order(3 - k, z)
            mail.arrived(far.at[zz], s_far + zz)
            add_into(acc.at[part(zz, None, 0)], [far.at[zz]], cols)
            mail.send(acc.at[part(zz, 1, 0)], near.at[zz], s_near + zz, to_near)
        for k in range(4):
            yield
            zz = z_order(3 - k, z)
            mail.arrived(near.at[zz], s_near + zz)
            add_into(acc.at[part(zz, 0, 0)], [near.at[zz]], cols)
            line((y, x), k, zz)
    elif order == "xyz":
        s_y, s_x = mail.slot(1), mail.slot(1)
        for k in range(4):
            yield
            zz = z_order(3 - k, z)
            if k == 0:
                own.wait()
            mail.arrived(from_core.at[zz], s_c + zz)
            add_into(acc.at[zz], [from_core.at[zz]], cols)
            line((both, both), k, zz)
        mail.send(acc.at[z, 1 - y], from_y, s_y, to_y)
        yield
        mail.arrived(from_y, s_y)
        add_into(acc.at[z, y], [from_y], cols)
        mail.send(acc.at[z, y, 1 - x], from_x, s_x, to_x)
        yield
        mail.arrived(from_x, s_x)
        add_into(acc.at[z, y, x], [from_x], cols)
    else:
        s_y, s_x = mail.slot(4), mail.slot(1)
        for k in range(4):
            yield
            zz = z_order(3 - k, z)
            if k == 0:
                own.wait()
            mail.arrived(from_core.at[zz], s_c + zz)
            add_into(acc.at[zz], [from_core.at[zz]], cols)
            mail.send(acc.at[zz, 1 - y], from_y.at[zz], s_y + zz, to_y)
        for k in range(4):
            yield
            zz = z_order(3 - k, z)
            mail.arrived(from_y.at[zz], s_y + zz)
            add_into(acc.at[zz, y], [from_y.at[zz]], cols)
            line((y, both), k, zz)
        mail.send(acc.at[z, y, 1 - x], from_x, s_x, to_x)
        yield
        mail.arrived(from_x, s_x)
        add_into(acc.at[z, y, x], [from_x], cols)
    out[...] = acc[z, y, x].astype(F32)


def reduce_scratch(order, shape, dtype):
    per_x = {"zyx": (4, 2), "zxy": (4,), "xyz": (), "xzy": ()}[order]
    per_y = {"zyx": (4,), "zxy": (4, 2), "xyz": (2,), "xzy": (4, 2)}[order]
    per_z = {"zyx": (2, 4), "zxy": (2, 4), "xyz": (2, 4, 2, 2), "xzy": (2, 4, 2)}[order]
    return [
        pltpu.VMEM(lead + shape, dtype)
        for lead in ((4, 2, 2), (4, 2, 2), per_x, per_y, per_z)
    ]


def reduce_kernel(orders, *refs):
    n = len(orders)
    grads, outs = refs[:n], refs[n : 2 * n]
    scratch = refs[2 * n : 7 * n]
    send_sems, recv_sems, own_sems = refs[7 * n :]
    greet()
    mail = Mail(send_sems, recv_sems)
    run_together(
        [
            reduce_unit(mail, o, grads[i], scratch[5 * i : 5 * i + 5], own_sems.at[i], outs[i])
            for i, o in enumerate(orders)
        ]
    )
    mail.finish()


def reduce_all(grads, orders, collective_id):
    shapes = [jax.ShapeDtypeStruct(g.shape[1:], F32) for g in grads]
    scratch = []
    for g, o in zip(grads, orders):
        scratch += reduce_scratch(o, g.shape[1:], g.dtype)
    return pl.pallas_call(
        functools.partial(reduce_kernel, orders),
        out_shape=shapes,
        in_specs=[HBM] * len(grads),
        out_specs=[pl.BlockSpec(memory_space=pltpu.VMEM)] * len(grads),
        scratch_shapes=scratch
        + [
            pltpu.SemaphoreType.DMA((SENDS,)),
            pltpu.SemaphoreType.DMA((RECVS,)),
            pltpu.SemaphoreType.DMA((len(grads),)),
        ],
        compiler_params=pltpu.CompilerParams(
            collective_id=collective_id, has_side_effects=True, vmem_limit_bytes=60 << 20
        ),
    )(*[g.reshape((4, 2, 2, 2) + g.shape[1:]) for g in grads])


def swap(values, distance):
    return lax.ppermute(values, "seq", [(s, s ^ distance) for s in range(4)])


def to_one_sequence(values):
    _, _, x, _ = place()
    mine = lax.dynamic_index_in_dim(values, x, 0, keepdims=False)
    theirs = swap(lax.dynamic_index_in_dim(values, 1 - x, 0, keepdims=False), 2)
    low = x == 0
    return jnp.stack([jnp.where(low, mine, theirs), jnp.where(low, theirs, mine)])


VECTORS = (72, 24, 24, 24, 96, 24, 24, 24)


def pack_vectors(parts):
    joined = jnp.concatenate(parts, axis=-1)
    lead = joined.shape[:-1]
    joined = jnp.pad(joined, [(0, 0)] * len(lead) + [(0, 2048 - joined.shape[-1])])
    return joined.reshape(lead + (16, 128))


def unpack_vectors(packed):
    joined = packed.reshape(packed.shape[:-2] + (2048,))
    out, at = [], 0
    for n in VECTORS:
        out.append(joined[..., at : at + n])
        at += n
    return out


ORDERS = ("xyz", "xzy", "zyx", "zyx", "xyz", "zyx", "zxy")


def fast_device(*args):
    (tokens, segment_ids, w_qkv, b_qkv, w_out, b_out, gain_one, shift_one) = args[:8]
    (w_in, b_in, w_back, b_back, gain_two, shift_two, out_grad) = args[8:]
    z, y, x, c = place()
    rows = tokens.shape[1]
    count = 2 * rows
    vectors = pack_vectors([b_qkv, b_out, gain_one, shift_one, b_in, b_back, gain_two, shift_two])
    w_q, w_k, w_v, vectors, w_out, w_in, w_back = gather_all(
        [w_qkv[:, :D], w_qkv[:, D : 2 * D], w_qkv[:, 2 * D :], vectors, w_out, w_in, w_back],
        ORDERS, 0,
    )
    w_q, w_k, w_v, w_out, w_in, w_back = [
        w.reshape(-1, w.shape[-1]) for w in (w_q, w_k, w_v, w_out, w_in, w_back)
    ]
    b_qkv, b_out, gain_one, shift_one, b_in, b_back, gain_two, shift_two = [
        v.reshape(-1).astype(F32) for v in unpack_vectors(vectors)
    ]
    ids = lax.dynamic_index_in_dim(segment_ids, x, 0)
    length = ids.shape[1]
    cos_all, sin_all = rotary_tables(ids, 0, length)

    def own_rows(values):
        halves = values.reshape((2, 2, rows) + values.shape[2:])
        return lax.dynamic_index_in_dim(halves, c, 1, keepdims=False).reshape(
            (1, count) + values.shape[2:]
        )

    def both_cores(own):
        other = swap(own, 1)
        low = c == 0
        one = jnp.where(low, own, other).reshape(2, 1, rows, own.shape[-1])
        two = jnp.where(low, other, own).reshape(2, 1, rows, own.shape[-1])
        return jnp.concatenate([one, two], axis=1).reshape(1, 2 * count, own.shape[-1])

    own_ids, cos_part, sin_part = own_rows(ids), own_rows(cos_all), own_rows(sin_all)
    same_doc = own_ids[:, :, None] == ids[:, None, :]

    tok = to_one_sequence(tokens).reshape(count, D)
    grad_rows = to_one_sequence(out_grad).reshape(count, D)
    query = rotate((mm(tok, w_q) + b_qkv[:D])[None], cos_part, sin_part).astype(BF)
    key = rotate((mm(tok, w_k) + b_qkv[D : 2 * D])[None], cos_part, sin_part).astype(BF)
    value = (mm(tok, w_v) + b_qkv[2 * D :]).astype(BF)[None]
    key_all, value_all = both_cores(key), both_cores(value)
    scores = scores_of(query, key_all, same_doc)
    highest = jnp.max(scores, axis=-1, keepdims=True)
    exponent = jnp.exp(scores - highest)
    total = jnp.sum(exponent, axis=-1, keepdims=True)
    log_total = highest + jnp.log(total)
    mixed = jnp.einsum(
        "bhqk,bkhd->bqhd", (exponent / total).astype(BF), heads(value_all),
        preferred_element_type=F32,
    ).astype(BF).reshape(count, D)
    first_sum = tok.astype(F32) + mm(mixed, w_out) + b_out
    normed = layer_norm(first_sum, gain_one, shift_one)
    normed_low = normed.astype(BF)
    inner = mm(normed_low, w_in) + b_in
    active = gelu_exact(inner).astype(BF)
    second_sum = normed + mm(active, w_back) + b_back
    result, pull_two = jax.vjp(layer_norm, second_sum, gain_two, shift_two)
    layer_out = to_one_sequence(result.astype(BF).reshape(2, rows, D))

    d_second_sum, d_gain_two, d_shift_two = pull_two(grad_rows.astype(F32))
    d_second = d_second_sum.astype(BF)
    d_b_back = jnp.sum(d_second.astype(F32), axis=0)
    d_w_back = jnp.einsum("qf,qd->fd", active, d_second, preferred_element_type=F32).astype(BF)
    d_active = jnp.einsum("qd,fd->qf", d_second, w_back, preferred_element_type=F32)
    d_inner = jax.vjp(gelu_exact, inner)[1](d_active)[0].astype(BF)
    d_b_in = jnp.sum(d_inner.astype(F32), axis=0)
    d_w_in = jnp.einsum("qd,qf->df", normed_low, d_inner, preferred_element_type=F32).astype(BF)
    d_normed = d_second_sum + jnp.einsum("qf,df->qd", d_inner, w_in, preferred_element_type=F32)
    d_first_sum, d_gain_one, d_shift_one = jax.vjp(layer_norm, first_sum, gain_one, shift_one)[1](
        d_normed
    )
    d_branch = d_first_sum.astype(BF)
    d_b_out = jnp.sum(d_branch.astype(F32), axis=0)
    d_w_out = jnp.einsum("qd,qe->de", mixed, d_branch, preferred_element_type=F32).astype(BF)
    d_mixed = jnp.einsum("qe,de->qd", d_branch, w_out, preferred_element_type=F32).astype(BF)[None]

    attention = jnp.exp(scores_of(query, key_all, same_doc) - log_total)
    d_attention = jnp.einsum(
        "bqhd,bkhd->bhqk", heads(d_mixed), heads(value_all), preferred_element_type=F32
    )
    inner_sum = jnp.sum(d_attention * attention, axis=-1, keepdims=True)
    d_scores = (attention * (d_attention - inner_sum) * HD ** (-0.5)).astype(BF)
    d_query = jnp.einsum(
        "bhqk,bkhd->bqhd", d_scores, heads(key_all), preferred_element_type=F32
    ).reshape(1, count, D)

    def sum_cores(partial):
        quarters = partial.reshape(2, 2, rows, D)
        mine = lax.dynamic_index_in_dim(quarters, c, 1, keepdims=False)
        theirs = lax.dynamic_index_in_dim(quarters, 1 - c, 1, keepdims=False).astype(BF)
        return (mine + swap(theirs, 1).astype(F32)).reshape(1, count, D)

    d_value = sum_cores(jnp.einsum(
        "bhqk,bqhd->bkhd", attention.astype(BF), heads(d_mixed), preferred_element_type=F32
    ).reshape(1, 2 * count, D)).astype(BF)[0]
    d_key = sum_cores(jnp.einsum(
        "bhqk,bqhd->bkhd", d_scores, heads(query), preferred_element_type=F32
    ).reshape(1, 2 * count, D))
    d_query = rotate(d_query, cos_part, -sin_part).astype(BF)[0]
    d_key = rotate(d_key, cos_part, -sin_part).astype(BF)[0]
    d_b_qkv = jnp.concatenate([jnp.sum(d.astype(F32), axis=0) for d in (d_query, d_key, d_value)])
    d_w_q, d_w_k, d_w_v = [
        jnp.einsum("qd,qe->de", tok, d, preferred_element_type=F32).astype(BF)
        for d in (d_query, d_key, d_value)
    ]
    d_tokens = d_first_sum
    for d, w in ((d_query, w_q), (d_key, w_k), (d_value, w_v)):
        d_tokens = d_tokens + jnp.einsum("qe,de->qd", d, w, preferred_element_type=F32)
    d_tokens = to_one_sequence(d_tokens.astype(BF).reshape(2, rows, D)).astype(F32)
    small = pack_vectors([
        v.reshape(32, -1)
        for v in (d_b_qkv, d_b_out, d_gain_one, d_shift_one, d_b_in, d_b_back, d_gain_two, d_shift_two)
    ]).astype(BF)
    d_w_q, d_w_k, d_w_v, d_w_out, d_w_in, d_w_back = [
        g.reshape(32, -1, g.shape[-1]) for g in (d_w_q, d_w_k, d_w_v, d_w_out, d_w_in, d_w_back)
    ]
    d_w_q, d_w_k, d_w_v, small, d_w_out, d_w_in, d_w_back = reduce_all(
        [d_w_q, d_w_k, d_w_v, small, d_w_out, d_w_in, d_w_back], ORDERS, 1
    )
    small = unpack_vectors(small)
    return (
        layer_out, d_tokens, jnp.concatenate([d_w_q, d_w_k, d_w_v], axis=1), small[0], d_w_out,
        small[1], small[2], small[3], d_w_in, small[4], d_w_back, small[5], small[6], small[7],
    )


def solution(mesh):
    devices = mesh.shape["dp"] * mesh.shape["seq"]
    fast = mesh.shape["dp"] == 8 and mesh.shape["seq"] == 4
    rows3 = P("dp", "seq", None)
    mat, vec = P(ALL, None), P(ALL)
    params = (mat, vec, mat, vec, vec, vec, mat, vec, mat, vec, vec, vec)
    return jax.shard_map(
        fast_device if fast else (lambda *args: on_device(devices, *args)),
        mesh=mesh,
        in_specs=(rows3, P("dp", None)) + params + (rows3,),
        out_specs=(rows3, rows3) + params,
        check_vma=False,
    )
```

```python
import functools
import jax
import jax.numpy as jnp
from jax import lax
from jax.experimental import pallas as pl
from jax.experimental.pallas import tpu as pltpu
from jax.sharding import PartitionSpec as P

D = 768
HEADS = 12
HD = 64
FF = 3072
EPSILON = 1e-06
ALL = ("dp", "seq")
BF = jnp.bfloat16
F32 = jnp.float32


def mm(a, b):
    return jnp.dot(a, b, preferred_element_type=F32)


def layer_norm(values, gain_vec, shift_vec):
    center = values - jnp.mean(values, axis=-1, keepdims=True)
    spread = jnp.mean(center * center, axis=-1, keepdims=True)
    return center * lax.rsqrt(spread + EPSILON) * gain_vec + shift_vec


def gelu_exact(values):
    return jax.nn.gelu(values, approximate=False)


def rotary_tables(segments, offset, row_count):
    length = segments.shape[-1]
    places = jnp.arange(length, dtype=jnp.int32)[None]
    change = jnp.concatenate(
        [jnp.ones((segments.shape[0], 1), dtype=bool), segments[:, 1:] != segments[:, :-1]], axis=1
    )
    starts = lax.cummax(jnp.where(change, places, 0), axis=1)
    position = lax.dynamic_slice_in_dim(places - starts, offset, row_count, 1).astype(F32)
    inverse = 10000.0 ** (-2.0 * jnp.arange(HD // 2, dtype=F32) / HD)
    angles = position[..., None] * inverse
    return jnp.cos(angles), jnp.sin(angles)


def rotate(values, cos_part, sin_part):
    paired = values.reshape(values.shape[:-1] + (HEADS, HD // 2, 2))
    even, odd = paired[..., 0], paired[..., 1]
    cos_wide, sin_wide = cos_part[..., None, :], sin_part[..., None, :]
    turned = jnp.stack(
        [even * cos_wide - odd * sin_wide, even * sin_wide + odd * cos_wide], axis=-1
    )
    return turned.reshape(values.shape)


def gather(local):
    return lax.all_gather(local, ALL, axis=0, tiled=True)


def gather_small(parts):
    joined = gather(jnp.concatenate(parts)[None])
    out, at = [], 0
    for part in parts:
        n = part.shape[0]
        out.append(joined[:, at : at + n].reshape(-1))
        at += n
    return out


def scatter_small(sums, devices):
    joined = jnp.concatenate([s.reshape(devices, -1) for s in sums], axis=1)
    own = lax.psum_scatter(joined, ALL, scatter_dimension=0, tiled=True)[0]
    out, at = [], 0
    for s in sums:
        n = s.shape[0] // devices
        out.append(own[at : at + n])
        at += n
    return out


def scatter(grad):
    return lax.psum_scatter(grad.astype(BF), ALL, scatter_dimension=0, tiled=True).astype(F32)


def heads(values):
    return values.reshape(values.shape[0], values.shape[1], HEADS, HD)


def scores_of(query, key_all, same_doc):
    raw = jnp.einsum("bqhd,bkhd->bhqk", heads(query), heads(key_all), preferred_element_type=F32)
    return jnp.where(same_doc[:, None], raw * HD ** (-0.5), -1e30)


def on_device(devices, *args):
    (tokens, segment_ids, w_qkv, b_qkv, w_out, b_out, gain_one, shift_one) = args[:8]
    (w_in, b_in, w_back, b_back, gain_two, shift_two, out_grad) = args[8:]
    b_qkv, b_out, gain_one, shift_one, b_in, b_back, gain_two, shift_two = [
        v.astype(F32)
        for v in gather_small([b_qkv, b_out, gain_one, shift_one, b_in, b_back, gain_two, shift_two])
    ]
    w_qkv, w_out, w_in, w_back = gather(w_qkv), gather(w_out), gather(w_in), gather(w_back)
    batch, rows = tokens.shape[:2]
    flat = (batch * rows, D)
    offset = lax.axis_index("seq") * rows
    cos_part, sin_part = rotary_tables(segment_ids, offset, rows)
    own_ids = lax.dynamic_slice_in_dim(segment_ids, offset, rows, 1)
    same_doc = own_ids[:, :, None] == segment_ids[:, None, :]

    tok = tokens.reshape(flat)
    joined = (mm(tok, w_qkv) + b_qkv).reshape(batch, rows, 3 * D)
    query = rotate(joined[..., :D], cos_part, sin_part).astype(BF)
    key = rotate(joined[..., D : 2 * D], cos_part, sin_part).astype(BF)
    value = joined[..., 2 * D :].astype(BF)
    key_all = lax.all_gather(key, "seq", axis=1, tiled=True)
    value_all = lax.all_gather(value, "seq", axis=1, tiled=True)
    keys = key_all.shape[1]
    scores = scores_of(query, key_all, same_doc)
    highest = jnp.max(scores, axis=-1, keepdims=True)
    exponent = jnp.exp(scores - highest)
    total = jnp.sum(exponent, axis=-1, keepdims=True)
    log_total = highest + jnp.log(total)
    mixed = jnp.einsum(
        "bhqk,bkhd->bqhd", (exponent / total).astype(BF), heads(value_all),
        preferred_element_type=F32,
    ).astype(BF).reshape(flat)
    first_sum = tok.astype(F32) + mm(mixed, w_out) + b_out
    normed = layer_norm(first_sum, gain_one, shift_one)
    normed_low = normed.astype(BF)
    inner = mm(normed_low, w_in) + b_in
    active = gelu_exact(inner).astype(BF)
    second_sum = normed + mm(active, w_back) + b_back
    result, pull_two = jax.vjp(layer_norm, second_sum, gain_two, shift_two)
    layer_out = result.astype(BF).reshape(tokens.shape)

    d_second_sum, d_gain_two, d_shift_two = pull_two(out_grad.reshape(flat).astype(F32))
    d_second = d_second_sum.astype(BF)
    d_b_back = jnp.sum(d_second.astype(F32), axis=0)
    d_w_back = scatter(jnp.einsum("qf,qd->fd", active, d_second, preferred_element_type=F32))
    d_active = jnp.einsum("qd,fd->qf", d_second, w_back, preferred_element_type=F32)
    d_inner = jax.vjp(gelu_exact, inner)[1](d_active)[0].astype(BF)
    d_b_in = jnp.sum(d_inner.astype(F32), axis=0)
    d_w_in = scatter(jnp.einsum("qd,qf->df", normed_low, d_inner, preferred_element_type=F32))
    d_normed = d_second_sum + jnp.einsum("qf,df->qd", d_inner, w_in, preferred_element_type=F32)
    d_first_sum, d_gain_one, d_shift_one = jax.vjp(layer_norm, first_sum, gain_one, shift_one)[1](
        d_normed
    )
    d_branch = d_first_sum.astype(BF)
    d_b_out = jnp.sum(d_branch.astype(F32), axis=0)
    d_w_out = scatter(jnp.einsum("qd,qe->de", mixed, d_branch, preferred_element_type=F32))
    d_mixed = jnp.einsum("qe,de->qd", d_branch, w_out, preferred_element_type=F32).astype(BF)
    d_mixed = d_mixed.reshape(batch, rows, D)

    attention = jnp.exp(scores_of(query, key_all, same_doc) - log_total)
    d_attention = jnp.einsum(
        "bqhd,bkhd->bhqk", heads(d_mixed), heads(value_all), preferred_element_type=F32
    )
    inner_sum = jnp.sum(d_attention * attention, axis=-1, keepdims=True)
    d_scores = (attention * (d_attention - inner_sum) * HD ** (-0.5)).astype(BF)
    d_query = jnp.einsum(
        "bhqk,bkhd->bqhd", d_scores, heads(key_all), preferred_element_type=F32
    ).reshape(batch, rows, D)
    d_value = jnp.einsum(
        "bhqk,bqhd->bkhd", attention.astype(BF), heads(d_mixed), preferred_element_type=F32
    ).reshape(batch, keys, D)
    d_key = jnp.einsum(
        "bhqk,bqhd->bkhd", d_scores, heads(query), preferred_element_type=F32
    ).reshape(batch, keys, D)
    d_key = lax.psum_scatter(d_key.astype(BF), "seq", scatter_dimension=1, tiled=True).astype(F32)
    d_value = lax.psum_scatter(d_value.astype(BF), "seq", scatter_dimension=1, tiled=True)
    d_joined = jnp.concatenate(
        [
            rotate(d_query, cos_part, -sin_part).astype(BF),
            rotate(d_key, cos_part, -sin_part).astype(BF),
            d_value,
        ],
        axis=-1,
    ).reshape(batch * rows, 3 * D)
    d_b_qkv = jnp.sum(d_joined.astype(F32), axis=0)
    d_w_qkv = scatter(jnp.einsum("qd,qe->de", tok, d_joined, preferred_element_type=F32))
    d_tokens = (
        jnp.einsum("qe,de->qd", d_joined, w_qkv, preferred_element_type=F32) + d_first_sum
    ).reshape(tokens.shape)
    small = scatter_small(
        [d_b_qkv, d_b_out, d_gain_one, d_shift_one, d_b_in, d_b_back, d_gain_two, d_shift_two],
        devices,
    )
    return (
        layer_out, d_tokens, d_w_qkv, small[0], d_w_out, small[1], small[2], small[3],
        d_w_in, small[4], d_w_back, small[5], small[6], small[7],
    )


HBM = pl.BlockSpec(memory_space=pl.ANY)
VMEM = pl.BlockSpec(memory_space=pltpu.VMEM)
MESH = pl.DeviceIdType.MESH
NEVER = -1e30
BOTH, LINE = pl.ds(0, 2), pl.ds(0, 4)
PAIRS = HEADS // 2


def place():
    dp, seq = lax.axis_index("dp"), lax.axis_index("seq")
    return dp // 2, dp % 2, seq // 2, seq % 2


def device(z, y, x, c):
    return (z * 2 + y, x * 2 + c)


def other_z(k, z):
    return lax.rem(z + k, 4)


def greet():
    z, y, x, c = place()
    barrier = pltpu.get_barrier_semaphore()
    partners = [device(z, y, x, 1 - c), device(z, y, 1 - x, c), device(z, 1 - y, x, c)]
    partners += [device(other_z(k, z), y, x, c) for k in (1, 2, 3)]
    for partner in partners:
        pl.semaphore_signal(barrier, inc=1, device_id=partner, device_id_type=MESH)
    pl.semaphore_wait(barrier, len(partners))


class Mail:
    def __init__(self, send_sems, recv_sems):
        self.send_sems, self.recv_sems = send_sems, recv_sems
        self.sent, self.sends, self.slots = [], 0, 0

    def slot(self, count=1):
        at = self.slots
        self.slots += count
        return at

    def send(self, src, dst, slot, target):
        copy = pltpu.make_async_remote_copy(
            src_ref=src, dst_ref=dst, send_sem=self.send_sems.at[self.sends],
            recv_sem=self.recv_sems.at[slot], device_id=target, device_id_type=MESH,
        )
        self.sent.append(copy)
        self.sends += 1
        copy.start()

    def arrived(self, dst, slot):
        z, y, x, c = place()
        pltpu.make_async_remote_copy(
            src_ref=dst, dst_ref=dst, send_sem=self.send_sems.at[0],
            recv_sem=self.recv_sems.at[slot], device_id=device(z, y, x, 1 - c),
            device_id_type=MESH,
        ).wait_recv()

    def finish(self):
        for copy in self.sent:
            copy.wait_send()
        self.sent = []


def gather_unit(mail, order, at):
    z, y, x, c = place()
    to_x, to_y, to_core = device(z, y, 1 - x, c), device(z, 1 - y, x, c), device(z, y, x, 1 - c)

    def copy(ref, slot, target):
        mail.send(ref, ref, slot, target)

    if order == "xyz":
        s_x, s_y, s_z, s_c = mail.slot(), mail.slot(), mail.slot(4), mail.slot()
        copy(at(z, y, x, c), s_x, to_x)
        yield
        mail.arrived(at(z, y, 1 - x, c), s_x)
        copy(at(z, y, BOTH, c), s_y, to_y)
        yield
        mail.arrived(at(z, 1 - y, BOTH, c), s_y)
        for k in (1, 2, 3):
            copy(at(z, BOTH, BOTH, c), s_z + z, device(other_z(k, z), y, x, c))
        yield
        for k in (1, 2, 3):
            zz = other_z(4 - k, z)
            mail.arrived(at(zz, BOTH, BOTH, c), s_z + zz)
        copy(at(LINE, BOTH, BOTH, c), s_c, to_core)
        yield
        mail.arrived(at(LINE, BOTH, BOTH, 1 - c), s_c)
        return
    s_z, s_one, s_two, s_c = mail.slot(4), mail.slot(), mail.slot(2), mail.slot(2)
    for k in (1, 2, 3):
        copy(at(z, y, x, c), s_z + z, device(other_z(k, z), y, x, c))
    yield
    for k in (1, 2, 3):
        zz = other_z(4 - k, z)
        mail.arrived(at(zz, y, x, c), s_z + zz)
    flip = order == "zxy"
    first, last = (to_x, to_y) if flip else (to_y, to_x)

    def pick(one, two, part):
        here = (x, y) if flip else (y, x)
        one, two = [BOTH if s is None else (1 - h if s else h) for s, h in zip((one, two), here)]
        return at(LINE, two, one, part) if flip else at(LINE, one, two, part)

    copy(pick(0, 0, c), s_one, first)
    copy(pick(0, 0, c), s_two, last)
    yield
    mail.arrived(pick(1, 0, c), s_one)
    copy(pick(1, 0, c), s_two + 1, last)
    copy(pick(None, 0, c), s_c, to_core)
    yield
    mail.arrived(pick(0, 1, c), s_two)
    mail.arrived(pick(1, 1, c), s_two + 1)
    copy(pick(None, 1, c), s_c + 1, to_core)
    yield
    mail.arrived(pick(None, 0, 1 - c), s_c)
    mail.arrived(pick(None, 1, 1 - c), s_c + 1)


def add_into(acc, landed):
    def one(i, _):
        acc[i] = (acc[i].astype(F32) + landed[i].astype(F32)).astype(acc.dtype)
        return 0

    lax.fori_loop(0, acc.shape[0], one, 0)


def reduce_unit(mail, order, at, landing, done):
    from_core, from_far, from_near, from_z = landing
    z, y, x, c = place()
    to_x, to_y, to_core = device(z, y, 1 - x, c), device(z, 1 - y, x, c), device(z, y, x, 1 - c)
    flip = order == "zxy"
    near_link, far_link = (to_x, to_y) if flip else (to_y, to_x)

    def pick(one, two):
        here = (x, y) if flip else (y, x)
        one, two = [BOTH if s is None else (1 - h if s else h) for s, h in zip((one, two), here)]
        return at(LINE, two, one, c) if flip else at(LINE, one, two, c)

    s_c, s_far, s_near, s_z = mail.slot(), mail.slot(), mail.slot(), mail.slot(3)
    mail.send(at(LINE, BOTH, BOTH, 1 - c), from_core, s_c, to_core)
    yield
    mail.arrived(from_core, s_c)
    add_into(at(LINE, BOTH, BOTH, c), from_core)
    mail.send(pick(None, 1), from_far, s_far, far_link)
    yield
    mail.arrived(from_far, s_far)
    add_into(pick(None, 0), from_far)
    mail.send(pick(1, 0), from_near, s_near, near_link)
    yield
    mail.arrived(from_near, s_near)
    add_into(pick(0, 0), from_near)
    for k in (1, 2, 3):
        zz = other_z(k, z)
        mail.send(at(zz, y, x, c), from_z.at[k - 1], s_z + k - 1, device(zz, y, x, c))
    yield
    total = at(z, y, x, c)[...].astype(F32)
    for k in (1, 2, 3):
        mail.arrived(from_z.at[k - 1], s_z + k - 1)
        total = total + from_z[k - 1].astype(F32)
    done(total)


class Pump:
    def __init__(self, routines, order):
        self.routines, self.order, self.at = routines, order, 0

    def steps(self, count):
        for _ in range(count):
            if self.at < len(self.order):
                next(self.routines[self.order[self.at]], None)
                self.at += 1

    def until(self, unit):
        last = max(i for i, u in enumerate(self.order) if u == unit)
        self.steps(last + 1 - self.at)

    def rest(self):
        self.steps(len(self.order))


def lanes(shape):
    return lax.broadcasted_iota(jnp.int32, shape, len(shape) - 1)


def nt(a, b):
    return lax.dot_general(a, b, (((1,), (1,)), ((), ())), preferred_element_type=F32)


def tn(a, b):
    return lax.dot_general(a, b, (((0,), (0,)), ((), ())), preferred_element_type=F32)


def turn(values, cos_wide, sin_wide):
    count = values.shape[-1]
    even = lanes(values.shape) % 2 == 0
    partner = jnp.where(
        even, pltpu.roll(values, count - 1, axis=1), pltpu.roll(values, 1, axis=1)
    )
    return values * cos_wide + partner * sin_wide


def selection(devices, per_device, row, step, col):
    return (lax.rem(col, step) == row).astype(F32)


WIDE = ((0, 72, 0), (1, 96, 0))
NARROW = (2, 24)


def spread_vector(packed, row, step, lane):
    total = 32 * step
    device_row = lax.broadcasted_iota(jnp.int32, (32, 512), 0) * 16 + row
    pick = (lanes((32, 512)) == device_row).astype(BF)
    slices = mm(pick, packed).astype(BF)
    within = lax.rem(lanes((128, total)), step) + lane
    place_at = (lax.broadcasted_iota(jnp.int32, (128, total), 0) == within).astype(BF)
    placed = mm(slices, place_at)
    owner = lanes((32, total)) // step == lax.broadcasted_iota(jnp.int32, (32, total), 0)
    return jnp.sum(jnp.where(owner, placed, 0.0), axis=0, keepdims=True)


def collect_vector(vector, row, step, lane):
    total = 32 * step
    owner = lanes((32, total)) // step == lax.broadcasted_iota(jnp.int32, (32, total), 0)
    owned = jnp.where(owner, jnp.broadcast_to(vector, (32, total)), 0.0).astype(BF)
    within = lax.rem(lanes((128, total)), step) + lane
    place_at = (lax.broadcasted_iota(jnp.int32, (128, total), 0) == within).astype(BF)
    slices = nt(owned, place_at).astype(BF)
    at = lax.broadcasted_iota(jnp.int32, (512, 32), 0)
    pick = (at == lanes((512, 32)) * 16 + row).astype(BF)
    return mm(pick, slices)


PLACES = (
    ("b_qkv", 0, 72, 0), ("b_in", 1, 96, 0), ("b_out", 2, 24, 0), ("gain_one", 2, 24, 24),
    ("shift_one", 2, 24, 48), ("gain_two", 2, 24, 72), ("shift_two", 2, 24, 96),
    ("b_back", 3, 24, 0),
)
ROW_OF = {name: i for i, (name, _, _, _) in enumerate(PLACES)}


def norm_parts(values):
    center = values - jnp.mean(values, axis=-1, keepdims=True)
    inverse = lax.rsqrt(jnp.mean(center * center, axis=-1, keepdims=True) + EPSILON)
    return center * inverse, inverse


def norm_back(normal, inverse, scaled):
    mean_one = jnp.mean(scaled, axis=-1, keepdims=True)
    mean_two = jnp.mean(scaled * normal, axis=-1, keepdims=True)
    return (scaled - mean_one - normal * mean_two) * inverse


GATHER = (
    ("vec", 0, "zyx"), ("qkv", 0, "zxy"), ("qkv", 1, "zyx"), ("qkv", 2, "zxy"), ("out", 0, "xyz"),
    ("in", 0, "zyx"), ("in", 1, "zxy"), ("in", 2, "zyx"), ("in", 3, "zxy"),
    ("back", 0, "zyx"), ("back", 1, "zxy"), ("back", 2, "zyx"), ("back", 3, "zxy"),
)
REDUCE = (
    ("back", 0, "zyx"), ("back", 1, "zxy"), ("back", 2, "zyx"), ("back", 3, "zxy"),
    ("in", 0, "zyx"), ("in", 1, "zxy"), ("in", 2, "zyx"), ("in", 3, "zxy"),
    ("out", 0, "zyx"), ("qkv", 0, "zxy"), ("qkv", 1, "zyx"), ("qkv", 2, "zxy"), ("vec", 0, "zyx"),
)


def unit_at(buffers, which, cut):
    buf = buffers[which]
    if which == "vec":
        return lambda z, y, x, part: buf.at[z, y, x, part]
    rows, half = buf.shape[3], buf.shape[4] // 2
    if which == "back":
        return lambda z, y, x, part: buf.at[
            z, y, x, pl.ds(cut * 48, 48), pl.ds(pl.multiple_of(part * half, 128), half)
        ]
    return lambda z, y, x, part: buf.at[
        z, y, x, pl.ds(0, 48), pl.ds(pl.multiple_of(part * half + cut * 384, 128), 384)
    ]


def layer_kernel(rows, gather_order, *refs):
    refs = iter(refs)
    take = lambda n: [next(refs) for _ in range(n)]
    tokens, out_grad, s_qkv, s_out, s_in, s_back, s_vec, cos_ref, sin_ref, key_ids, own_ids = take(11)
    o_layer, o_grad, o_qkv, o_out, o_in, o_back, o_vec = take(7)
    w_qkv, w_out, w_in, w_back, vec = take(5)
    sw_qkv, sw_out, sw_in = take(3)
    f_core, f_far, f_near, f_z, v_core, v_far, v_near, v_z = take(8)
    tok_ref, og_ref, query, keys, values, mixed, normal, inverse, total, normed_low = take(10)
    active, slope, low, lse, layer, sums, dkv, ig_own, ig_send, ig_got, vectors, d_vectors = take(12)
    n_qkv, n_out, n_in, n_back = take(4)
    send_sems, recv_sems, own_sems = take(3)
    z, y, x, c = place()
    count = 2 * rows
    sibling, partner = device(z, y, x, 1 - c), device(z, y, 1 - x, c)
    wide = lambda start, size: pl.ds(pl.multiple_of(start, 128), size)
    vector = lambda name, cols: vectors[pl.ds(ROW_OF[name], 1), cols]
    all_d = pl.ds(0, D)

    own_copies = [
        pltpu.make_async_copy(tokens.at[x], tok_ref.at[x], own_sems.at[0]),
        pltpu.make_async_copy(out_grad.at[x], og_ref.at[x], own_sems.at[1]),
        pltpu.make_async_copy(s_vec, vec.at[z, y, x, c], own_sems.at[2]),
    ]
    for copy in own_copies:
        copy.start()
    greet()
    mail = Mail(send_sems, recv_sems)

    first_slots = []
    for shard, landing in ((s_qkv, sw_qkv), (s_in, sw_in), (s_out, sw_out)):
        half = landing.shape[1]
        first_slots.append(mail.slot())
        mail.send(shard.at[:, wide((1 - c) * half, half)], landing, first_slots[-1], sibling)
    back_slot = mail.slot()
    back_part = lambda core, part: w_back.at[
        z, y, x, pl.ds(pl.multiple_of(core * 96, 32), 96), wide(part * 384, 384)
    ]
    mail.send(s_back.at[:, wide((1 - c) * 384, 384)], back_part(c, 1 - c), back_slot, sibling)
    tok_slot, og_slot = mail.slot(), mail.slot()
    mail.send(tokens.at[1 - x], tok_ref.at[x], tok_slot, partner)

    def merge(shard, landing, target, slot):
        half = landing.shape[1]
        mail.arrived(landing, slot)
        own = shard[:, wide(c * half, half)].astype(F32)
        other = landing[...].astype(F32)
        first = jnp.where(c == 0, own, other)
        second = jnp.where(c == 0, other, own)
        target[z, y, x, :, wide(c * half, half)] = jnp.concatenate([first, second], 0).astype(BF)

    own_copies[2].wait()
    merge(s_qkv, sw_qkv, w_qkv, first_slots[0])
    buffers = {"qkv": w_qkv, "out": w_out, "in": w_in, "back": w_back, "vec": vec}
    gathers = [
        gather_unit(mail, order, unit_at(buffers, which, cut)) for which, cut, order in GATHER
    ]
    pump = Pump(gathers, gather_order)
    pump.steps(3)
    merge(s_out, sw_out, w_out, first_slots[2])
    merge(s_in, sw_in, w_in, first_slots[1])
    mail.arrived(back_part(1 - c, c), back_slot)
    back_part(c, c)[...] = s_back[:, wide(c * 384, 384)]

    pump.until(0)
    packed = vec[...].reshape(512, 128)
    for name, row, step, lane in PLACES:
        vectors[pl.ds(ROW_OF[name], 1), pl.ds(0, 32 * step)] = spread_vector(packed, row, step, lane)
    own_copies[0].wait()
    mail.arrived(tok_ref.at[1 - x], tok_slot)
    mail.send(out_grad.at[1 - x], og_ref.at[x], og_slot, partner)
    pump.until(3)

    def project(tile):
        cols = wide(tile * 256, 256)
        weight = w_qkv[:, :, :, :, cols].reshape(D, 256)
        return mm(tok_ref[...].reshape(count, D), weight) + vector("b_qkv", cols)

    cos_two = lambda at=slice(None): jnp.concatenate([cos_ref[at], cos_ref[at]], axis=1)
    sin_two = lambda at=slice(None): jnp.concatenate([sin_ref[at], sin_ref[at]], axis=1)

    def key_tile(i, _):
        keys[c, :, wide(i * 256, 256)] = turn(project(3 + i), cos_two(), sin_two()).astype(BF)
        return 0

    def value_tile(i, _):
        values[c, :, wide(i * 256, 256)] = project(6 + i).astype(BF)
        return 0

    def query_tile(i, _):
        turned = turn(project(i), cos_two(), sin_two()).astype(BF)
        query[:, wide(i * 256, 256)] = turned * jnp.asarray(HD ** (-0.5), BF)
        return 0

    key_slot, value_slot = mail.slot(), mail.slot()
    lax.fori_loop(0, 3, key_tile, 0)
    mail.send(keys.at[c], keys.at[c], key_slot, sibling)
    pump.steps(1)
    lax.fori_loop(0, 3, value_tile, 0)
    mail.send(values.at[c], values.at[c], value_slot, sibling)
    pump.steps(1)
    lax.fori_loop(0, 3, query_tile, 0)
    mail.arrived(keys.at[1 - c], key_slot)
    mail.arrived(values.at[1 - c], value_slot)

    block = min(256, rows)
    all_keys = 2 * count

    def head_of(values_, s):
        return jnp.where(lanes(values_.shape) // HD == s, values_, jnp.zeros_like(values_))

    def same_doc(at):
        per_key = jnp.concatenate([key_ids[...]] * (block // 128), axis=1)
        return per_key == own_ids[:, at]

    for pair in range(PAIRS):
        cols = pl.ds(pair * 128, 128)
        key = keys[:, :, cols].reshape(all_keys, 128)
        value_t = values[:, :, cols].reshape(all_keys, 128).T

        def attend(i, _, key=key, value_t=value_t, cols=cols, pair=pair):
            at = wide(i * block, block)
            q = query[at, cols]
            same = same_doc(at)
            outs = []
            for s in (0, 1):
                scores = jnp.where(same, nt(key, head_of(q, s)), NEVER)
                highest = jnp.max(scores, axis=0, keepdims=True)
                exponent = jnp.exp(scores - highest)
                row_total = jnp.sum(exponent, axis=0, keepdims=True)
                out = mm(value_t[s * HD : (s + 1) * HD], exponent.astype(BF))
                outs.append(out / row_total)
                lse[pl.ds(2 * pair + s, 1), at] = highest + jnp.log(row_total)
            mixed[at, cols] = jnp.concatenate(outs, axis=0).T.astype(BF)
            return 0

        lax.fori_loop(0, count // block, attend, 0)
        pump.steps(3)

    pump.until(4)
    chunk = 128
    chunks = count // chunk
    per_slot = rows // chunk

    def rows_of(ref, i):
        return ref.at[i // per_slot, pl.ds(pl.multiple_of(lax.rem(i, per_slot) * chunk, chunk), chunk)]

    def span(i):
        return pl.ds(pl.multiple_of(i * chunk, chunk), chunk)

    def first_norm(i, _):
        at = span(i)
        branch = mm(mixed[at], w_out[...].reshape(D, D)) + vector("b_out", all_d)
        normal_part, inverse_part = norm_parts(rows_of(tok_ref, i)[...].astype(F32) + branch)
        normal[at] = normal_part
        inverse[at] = inverse_part
        normed = normal_part * vector("gain_one", all_d) + vector("shift_one", all_d)
        normed_low[at] = normed.astype(BF)
        return 0

    lax.fori_loop(0, chunks, first_norm, 0)
    pump.steps(2)
    for cut in range(4):
        pump.until(5 + cut)

        def feed(i, _, cut=cut):
            at = pl.ds(pl.multiple_of((i % 2) * rows, rows), rows)
            cols = wide((i // 2) * (FF // 2) + cut * 384, 384)
            weight = w_in[:, :, :, :, cols].reshape(D, 384)
            inner = mm(normed_low[at], weight) + vector("b_in", cols)
            phi = 0.5 + 0.5 * lax.erf(inner * (0.5**0.5))
            density = jnp.exp(-0.5 * inner * inner) * 0.3989422804014327
            active[at, cols] = (inner * phi).astype(BF)
            slope[at, cols] = (phi + inner * density).astype(BF)
            return 0

        lax.fori_loop(0, 4, feed, 0)
    pump.rest()

    def second(i, _):
        cols = wide(i * 256, 256)
        total[:, cols] = mm(active[...], w_back[:, :, :, :, cols].reshape(FF, 256))
        return 0

    lax.fori_loop(0, D // 256, second, 0)
    own_copies[1].wait()
    mail.arrived(og_ref.at[1 - x], og_slot)

    def second_norm(i, carry):
        at = span(i)
        normed = normal[at] * vector("gain_one", all_d) + vector("shift_one", all_d)
        part, root = norm_parts(normed + total[at] + vector("b_back", all_d))
        gain = vector("gain_two", all_d)
        rows_of(layer, i)[...] = (part * gain + vector("shift_two", all_d)).astype(BF)
        grad = rows_of(og_ref, i)[...].astype(F32)
        d_sum = norm_back(part, root, grad * gain)
        total[at] = d_sum
        d_low = d_sum.astype(BF)
        low[at] = d_low
        terms = (grad * part, grad, d_low.astype(F32))
        return tuple(k + jnp.sum(t, axis=0, keepdims=True) for k, t in zip(carry, terms))

    zero = jnp.zeros((1, D), F32)
    grads = lax.fori_loop(0, chunks, second_norm, (zero, zero, zero))
    for name, grad in zip(("gain_two", "shift_two", "b_back"), grads):
        d_vectors[pl.ds(ROW_OF[name], 1), all_d] = grad
    layer_slot = mail.slot()
    mail.send(layer.at[1 - x], o_layer.at[x], layer_slot, partner)
    layer_own = pltpu.make_async_copy(layer.at[x], o_layer.at[x], own_sems.at[3])
    layer_own.start()

    mail.finish()

    def inner_grad(i, _):
        cols = wide(i * 384, 384)
        weight = w_back[i // 2, i % 2].reshape(384, D)
        d_inner = (nt(low[...], weight) * slope[:, cols].astype(F32)).astype(BF)
        slope[:, cols] = d_inner
        d_vectors[pl.ds(ROW_OF["b_in"], 1), cols] = jnp.sum(
            d_inner.astype(F32), axis=0, keepdims=True
        )
        return 0

    lax.fori_loop(0, FF // 384, inner_grad, 0)

    def back_grad(i, _):
        grad = tn(active[:, wide(i * 384, 384)], low[...])
        w_back[i // 2, i % 2] = grad.astype(BF).reshape(2, 192, D)
        return 0

    lax.fori_loop(0, FF // 384, back_grad, 0)

    reducers = []
    news = {"qkv": n_qkv, "out": n_out, "in": n_in, "back": n_back}
    for number, (which, cut, order) in enumerate(REDUCE):
        if which == "vec":
            landing = (v_core, v_far, v_near, v_z)

            def done(sum_):
                o_vec[...] = sum_
        else:
            landing = tuple(r.at[number] for r in (f_core, f_far, f_near, f_z))

            def done(sum_, which=which, cut=cut):
                if which == "back":
                    n_back[pl.ds(cut * 48, 48), :] = sum_
                else:
                    news[which][:, pl.ds(cut * 384, 384)] = sum_

        reducers.append(reduce_unit(mail, order, unit_at(buffers, which, cut), landing, done))
    live = []

    def start(*numbers):
        for number in numbers:
            next(reducers[number])
            live.append(number)

    finals = []

    def finish_weight(which, out):
        part = news[which]
        half, own_rows = part.shape[1], part.shape[0] // 2
        mine = pl.ds(pl.multiple_of(c * own_rows, 8), own_rows)
        theirs = pl.ds(pl.multiple_of((1 - c) * own_rows, 8), own_rows)
        slot = mail.slot()
        mail.send(part.at[theirs], out.at[:, wide(c * half, half)], slot, sibling)
        own = pltpu.make_async_copy(
            part.at[mine], out.at[:, wide(c * half, half)], own_sems.at[4 + len(finals)]
        )
        own.start()
        finals.append((own, out.at[:, wide((1 - c) * half, half)], slot))

    left = {"back": 4, "in": 4, "out": 1, "qkv": 3, "vec": 1}
    outs = {"qkv": o_qkv, "out": o_out, "in": o_in, "back": o_back}

    def advance(most=None):
        for number in list(live)[:most]:
            if next(reducers[number], "end") == "end":
                live.remove(number)
                which = REDUCE[number][0]
                left[which] -= 1
                if which != "vec" and not left[which]:
                    finish_weight(which, outs[which])

    start(0, 1, 2, 3)

    def normed_grad(i, _):
        cols = wide(i * 512, 512)
        weight = w_in[:, :, :, :, cols].reshape(D, 512)
        total[...] = total[...] + nt(slope[:, cols], weight)
        return 0

    lax.fori_loop(0, FF // 512, normed_grad, 0)
    advance(2)

    def first_back(i, carry):
        at = span(i)
        part = normal[at]
        grad = total[at]
        d_sum = norm_back(part, inverse[at], grad * vector("gain_one", all_d))
        total[at] = d_sum
        d_low = d_sum.astype(BF)
        low[at] = d_low
        terms = (grad * part, grad, d_low.astype(F32))
        return tuple(k + jnp.sum(t, axis=0, keepdims=True) for k, t in zip(carry, terms))

    grads = lax.fori_loop(0, chunks, first_back, (zero, zero, zero))
    for name, grad in zip(("gain_one", "shift_one", "b_out"), grads):
        d_vectors[pl.ds(ROW_OF[name], 1), all_d] = grad

    for cut in range(4):

        def in_grad(h, _, cut=cut):
            cols = wide(h * (FF // 2) + cut * 384, 384)
            grad = tn(normed_low[...], slope[:, cols])
            w_in[:, :, :, :, cols] = grad.astype(BF).reshape(4, 2, 2, 48, 384)
            return 0

        lax.fori_loop(0, 2, in_grad, 0)
        if cut < 2:
            start(4 + cut)
        advance(2)

    def mixed_grad(i, _):
        at = span(i)
        active[at, pl.ds(3 * D, D)] = nt(low[at], w_out[...].reshape(D, D)).astype(BF)
        return 0

    lax.fori_loop(0, chunks, mixed_grad, 0)

    def out_grad_tile(h, _):
        cols = wide(h * 384, 384)
        grad = tn(mixed[...], low[:, cols])
        w_out[:, :, :, :, cols] = grad.astype(BF).reshape(4, 2, 2, 48, 384)
        return 0

    lax.fori_loop(0, 2, out_grad_tile, 0)
    advance(2)

    d_slots = []
    for pair in range(PAIRS):
        cols = pl.ds(pair * 128, 128)
        key = keys[:, :, cols].reshape(all_keys, 128)
        key_t = key.T
        value = values[:, :, cols].reshape(all_keys, 128)

        def attend_back(i, _, key=key, key_t=key_t, value=value, cols=cols, pair=pair):
            at = wide(i * block, block)
            q = query[at, cols]
            d_out = active[at, pl.ds(3 * D + pair * 128, 128)]
            product = (d_out.astype(F32) * mixed[at, cols].astype(F32)).T
            same = same_doc(at)
            d_queries = []
            d_key, d_value = sums[0], sums[1]
            for s in (0, 1):
                q_s, d_s = head_of(q, s), head_of(d_out, s)
                delta = jnp.sum(product[s * HD : (s + 1) * HD], axis=0, keepdims=True)
                scores = jnp.where(same, nt(key, q_s), NEVER)
                attention = jnp.exp(scores - lse[pl.ds(2 * pair + s, 1), at])
                d_value = d_value + mm(attention.astype(BF), d_s)
                d_scores = (attention * (nt(value, d_s) - delta)).astype(BF)
                d_key = d_key + mm(d_scores, q_s)
                d_queries.append(mm(key_t[s * HD : (s + 1) * HD], d_scores))
            sums[0], sums[1] = d_key, d_value
            d_query = jnp.concatenate(d_queries, axis=0).T * HD ** (-0.5)
            active[at, cols] = turn(d_query, cos_ref[at], -sin_ref[at]).astype(BF)
            return 0

        sums[...] = jnp.zeros_like(sums)
        lax.fori_loop(0, count // block, attend_back, 0)
        for which in (0, 1):
            for core in (0, 1):
                slope[:, pl.ds(which * 2 * D + core * D + pair * 128, 128)] = sums[
                    which, pl.ds(core * count, count)
                ].astype(BF)
            d_slots.append(mail.slot())
            mail.send(
                slope.at[:, wide(which * 2 * D + (1 - c) * D + pair * 128, 128)],
                dkv.at[which, :, cols], d_slots[-1], sibling,
            )
        if pair == 0:
            start(6)
        elif pair == 1:
            start(7)
        elif pair == 2:
            start(8)
        advance(3)

    for pair in range(PAIRS):
        for which in (0, 1):
            mail.arrived(dkv.at[which, :, pl.ds(pair * 128, 128)], d_slots[2 * pair + which])

    def own_key_grads(i, _):
        cols = wide(i * 128, 128)
        d_key = slope[:, wide(c * D + i * 128, 128)].astype(F32) + dkv[0, :, cols].astype(F32)
        d_key = turn(d_key, cos_ref[...], -sin_ref[...])
        d_value = slope[:, wide(2 * D + c * D + i * 128, 128)].astype(F32)
        d_value = d_value + dkv[1, :, cols].astype(F32)
        active[:, wide(D + i * 128, 128)] = d_key.astype(BF)
        active[:, wide(2 * D + i * 128, 128)] = d_value.astype(BF)
        return 0

    lax.fori_loop(0, PAIRS, own_key_grads, 0)
    advance(3)

    def token_grad(i):
        at = span(i)
        return nt(active[at, pl.ds(0, 3 * D)], w_qkv[...].reshape(D, 3 * D)) + total[at]

    def token_there(i, _):
        ig_send[span(i)] = token_grad((1 - x) * per_slot + i).astype(BF)
        return 0

    lax.fori_loop(0, per_slot, token_there, 0)
    ig_slot = mail.slot()
    mail.send(ig_send, ig_got, ig_slot, partner)

    def token_here(i, _):
        ig_own[0, span(i)] = token_grad(x * per_slot + i)
        return 0

    lax.fori_loop(0, per_slot, token_here, 0)
    ig_here = pltpu.make_async_copy(ig_own.at[0], o_grad.at[x], own_sems.at[8])
    ig_here.start()
    for cut in range(3):

        def qkv_grad(h, _, cut=cut):
            cols = wide(h * (3 * D // 2) + cut * 384, 384)
            grad = tn(tok_ref[...].reshape(count, D), active[:, cols])
            w_qkv[:, :, :, :, cols] = grad.astype(BF).reshape(4, 2, 2, 48, 384)
            return 0

        lax.fori_loop(0, 2, qkv_grad, 0)
        start(9 + cut)
    for i in range(3 * D // 256):
        cols = pl.ds(i * 256, 256)
        d_vectors[pl.ds(ROW_OF["b_qkv"], 1), cols] = jnp.sum(
            active[:, cols].astype(F32), axis=0, keepdims=True
        )
    packed = jnp.zeros((512, 128), F32)
    for name, row, step, lane in PLACES:
        packed = packed + collect_vector(
            d_vectors[pl.ds(ROW_OF[name], 1), pl.ds(0, 32 * step)], row, step, lane
        )
    vec[...] = packed.astype(BF).reshape(4, 2, 2, 2, 16, 128)
    start(12)
    advance(4)
    mail.arrived(ig_got, ig_slot)
    ig_own[1] = ig_got[...].astype(F32)
    ig_there = pltpu.make_async_copy(ig_own.at[1], o_grad.at[1 - x], own_sems.at[9])
    ig_there.start()
    while live:
        advance()
    for own, landed, slot in finals:
        own.wait()
        mail.arrived(landed, slot)
    mail.arrived(o_layer.at[1 - x], layer_slot)
    layer_own.wait()
    ig_here.wait()
    ig_there.wait()
    mail.finish()


GATHER_ORDER = (
    0, 1, 0, 2, 0, 1, 3, 0, 2, 4, 0, 3, 5, 4, 6, 2, 7, 5, 8, 1, 4, 6, 9, 3,
    5, 1, 2, 7, 10, 1, 8, 11, 2, 3, 6, 9, 12, 5, 3, 7, 5, 8, 10, 11, 6, 9, 12, 6,
    7, 7, 4, 8, 10, 4, 11, 8, 9, 12, 10, 11, 9, 10, 12, 11, 12,
)


def pack_vectors(parts):
    by_name = dict(zip(("b_qkv", "b_out", "gain_one", "shift_one", "b_in", "b_back", "gain_two", "shift_two"), parts))
    out = []
    for row in range(4):
        line = jnp.concatenate([by_name[name] for name, r, _, _ in PLACES if r == row])
        out.append(jnp.pad(line, (0, 128 - line.shape[0])))
    return jnp.pad(jnp.stack(out), ((0, 12), (0, 0)))


def fast_device(*args):
    (tokens, segment_ids, w_qkv, b_qkv, w_out, b_out, gain_one, shift_one) = args[:8]
    (w_in, b_in, w_back, b_back, gain_two, shift_two, out_grad) = args[8:]
    z, y, x, c = place()
    rows = tokens.shape[1]
    count = 2 * rows
    packed = pack_vectors([b_qkv, b_out, gain_one, shift_one, b_in, b_back, gain_two, shift_two])
    ids = lax.dynamic_index_in_dim(segment_ids, x, 0, keepdims=False)
    by_core = ids.reshape(2, 2, rows).transpose(1, 0, 2).reshape(2, count)
    own = lax.dynamic_index_in_dim(by_core, c, 0, keepdims=False)
    places = (jnp.arange(2)[:, None] * count + c * rows + jnp.arange(rows)[None]).reshape(count)
    starts = jnp.sum((ids[None, :] < own[:, None]).astype(jnp.int32), axis=1)
    position = (places - starts).astype(F32)
    lane = jnp.arange(128)
    power = 10000.0 ** (-2.0 * ((lane % HD) // 2).astype(F32) / HD)
    angles = position[:, None] * power[None, :]
    cos_wide = jnp.cos(angles)
    sin_wide = jnp.where(lane % 2 == 0, -1.0, 1.0) * jnp.sin(angles)
    key_ids = jnp.broadcast_to(by_core.reshape(2 * count, 1).astype(F32), (2 * count, 128))
    own_ids = own.reshape(1, count).astype(F32)

    shape = jax.ShapeDtypeStruct
    part = (48, 384)
    units = 12
    vm = pltpu.VMEM
    outs = pl.pallas_call(
        functools.partial(layer_kernel, rows, GATHER_ORDER),
        out_shape=[
            shape((2, rows, D), BF), shape((2, rows, D), F32), shape((24, 3 * D), F32),
            shape((24, D), F32), shape((24, FF), F32), shape((96, D), F32), shape((16, 128), F32),
        ],
        in_specs=[HBM, HBM] + [VMEM] * 9,
        out_specs=[HBM] * 6 + [VMEM],
        scratch_shapes=[
            vm((4, 2, 2, 48, 3 * D), BF), vm((4, 2, 2, 48, D), BF), vm((4, 2, 2, 48, FF), BF),
            vm((4, 2, 2, 192, D), BF), vm((4, 2, 2, 2, 16, 128), BF),
            vm((24, 3 * D // 2), BF), vm((24, D // 2), BF), vm((24, FF // 2), BF),
            vm((units, 4, 2, 2) + part, BF), vm((units, 4, 2) + part, BF),
            vm((units, 4) + part, BF), vm((units, 3) + part, BF),
            vm((4, 2, 2, 16, 128), BF), vm((4, 2, 16, 128), BF), vm((4, 16, 128), BF),
            vm((3, 16, 128), BF),
            vm((2, rows, D), BF), vm((2, rows, D), BF), vm((count, D), BF), vm((2, count, D), BF),
            vm((2, count, D), BF), vm((count, D), BF), vm((count, D), F32), vm((count, 1), F32),
            vm((count, D), F32), vm((count, D), BF),
            vm((count, FF), BF), vm((count, FF), BF), vm((count, D), BF), vm((16, count), F32),
            vm((2, rows, D), BF), vm((2, 2 * count, 128), F32), vm((2, count, D), BF),
            vm((2, rows, D), F32), vm((rows, D), BF), vm((rows, D), BF), vm((8, FF), F32),
            vm((8, FF), F32),
            vm((48, 3 * D // 2), F32), vm((48, D // 2), F32), vm((48, FF // 2), F32),
            vm((192, D // 2), F32),
            pltpu.SemaphoreType.DMA((240,)), pltpu.SemaphoreType.DMA((240,)),
            pltpu.SemaphoreType.DMA((10,)),
        ],
        compiler_params=pltpu.CompilerParams(
            collective_id=0, has_side_effects=True, vmem_limit_bytes=63 << 20
        ),
        cost_estimate=pl.CostEstimate(
            flops=28_000_000_000, bytes_accessed=8_000_000, transcendentals=16_000_000
        ),
    )(tokens, out_grad, w_qkv, w_out, w_in, w_back, packed, cos_wide, sin_wide, key_ids, own_ids)
    layer_out, input_grad, d_qkv, d_out, d_in, d_back, small = outs
    small = {name: small[row, lane : lane + step] for name, row, step, lane in PLACES}
    return (
        layer_out, input_grad, d_qkv, small["b_qkv"], d_out, small["b_out"], small["gain_one"],
        small["shift_one"], d_in, small["b_in"], d_back, small["b_back"], small["gain_two"],
        small["shift_two"],
    )


def solution(mesh):
    devices = mesh.shape["dp"] * mesh.shape["seq"]
    fast = mesh.shape["dp"] == 8 and mesh.shape["seq"] == 4
    rows3 = P("dp", "seq", None)
    mat, vec = P(ALL, None), P(ALL)
    params = (mat, vec, mat, vec, vec, vec, mat, vec, mat, vec, vec, vec)
    return jax.shard_map(
        fast_device if fast else (lambda *args: on_device(devices, *args)),
        mesh=mesh,
        in_specs=(rows3, P("dp", None)) + params + (rows3,),
        out_specs=(rows3, rows3) + params,
        check_vma=False,
    )
```

```python
import functools
import jax
import jax.numpy as jnp
import numpy as np
from jax import lax
from jax.experimental import pallas as pl
from jax.experimental.pallas import tpu as pltpu
from jax.sharding import PartitionSpec as P

D = 768
HEADS = 12
HD = 64
FF = 3072
EPSILON = 1e-06
ALL = ("dp", "seq")
BF = jnp.bfloat16
F32 = jnp.float32


def mm(a, b):
    return jnp.dot(a, b, preferred_element_type=F32)


def layer_norm(values, gain_vec, shift_vec):
    center = values - jnp.mean(values, axis=-1, keepdims=True)
    spread = jnp.mean(center * center, axis=-1, keepdims=True)
    return center * lax.rsqrt(spread + EPSILON) * gain_vec + shift_vec


def gelu_exact(values):
    return jax.nn.gelu(values, approximate=False)


def rotary_tables(segments, offset, row_count):
    length = segments.shape[-1]
    places = jnp.arange(length, dtype=jnp.int32)[None]
    change = jnp.concatenate(
        [jnp.ones((segments.shape[0], 1), dtype=bool), segments[:, 1:] != segments[:, :-1]], axis=1
    )
    starts = lax.cummax(jnp.where(change, places, 0), axis=1)
    position = lax.dynamic_slice_in_dim(places - starts, offset, row_count, 1).astype(F32)
    inverse = 10000.0 ** (-2.0 * jnp.arange(HD // 2, dtype=F32) / HD)
    angles = position[..., None] * inverse
    return jnp.cos(angles), jnp.sin(angles)


def rotate(values, cos_part, sin_part):
    paired = values.reshape(values.shape[:-1] + (HEADS, HD // 2, 2))
    even, odd = paired[..., 0], paired[..., 1]
    cos_wide, sin_wide = cos_part[..., None, :], sin_part[..., None, :]
    turned = jnp.stack(
        [even * cos_wide - odd * sin_wide, even * sin_wide + odd * cos_wide], axis=-1
    )
    return turned.reshape(values.shape)


def gather(local):
    return lax.all_gather(local, ALL, axis=0, tiled=True)


def gather_small(parts):
    joined = gather(jnp.concatenate(parts)[None])
    out, at = [], 0
    for part in parts:
        n = part.shape[0]
        out.append(joined[:, at : at + n].reshape(-1))
        at += n
    return out


def scatter_small(sums, devices):
    joined = jnp.concatenate([s.reshape(devices, -1) for s in sums], axis=1)
    own = lax.psum_scatter(joined, ALL, scatter_dimension=0, tiled=True)[0]
    out, at = [], 0
    for s in sums:
        n = s.shape[0] // devices
        out.append(own[at : at + n])
        at += n
    return out


def scatter(grad):
    return lax.psum_scatter(grad.astype(BF), ALL, scatter_dimension=0, tiled=True).astype(F32)


def heads(values):
    return values.reshape(values.shape[0], values.shape[1], HEADS, HD)


def scores_of(query, key_all, same_doc):
    raw = jnp.einsum("bqhd,bkhd->bhqk", heads(query), heads(key_all), preferred_element_type=F32)
    return jnp.where(same_doc[:, None], raw * HD ** (-0.5), -1e30)


def on_device(devices, *args):
    (tokens, segment_ids, w_qkv, b_qkv, w_out, b_out, gain_one, shift_one) = args[:8]
    (w_in, b_in, w_back, b_back, gain_two, shift_two, out_grad) = args[8:]
    b_qkv, b_out, gain_one, shift_one, b_in, b_back, gain_two, shift_two = [
        v.astype(F32)
        for v in gather_small([b_qkv, b_out, gain_one, shift_one, b_in, b_back, gain_two, shift_two])
    ]
    w_qkv, w_out, w_in, w_back = gather(w_qkv), gather(w_out), gather(w_in), gather(w_back)
    batch, rows = tokens.shape[:2]
    flat = (batch * rows, D)
    offset = lax.axis_index("seq") * rows
    cos_part, sin_part = rotary_tables(segment_ids, offset, rows)
    own_ids = lax.dynamic_slice_in_dim(segment_ids, offset, rows, 1)
    same_doc = own_ids[:, :, None] == segment_ids[:, None, :]

    tok = tokens.reshape(flat)
    joined = (mm(tok, w_qkv) + b_qkv).reshape(batch, rows, 3 * D)
    query = rotate(joined[..., :D], cos_part, sin_part).astype(BF)
    key = rotate(joined[..., D : 2 * D], cos_part, sin_part).astype(BF)
    value = joined[..., 2 * D :].astype(BF)
    key_all = lax.all_gather(key, "seq", axis=1, tiled=True)
    value_all = lax.all_gather(value, "seq", axis=1, tiled=True)
    keys = key_all.shape[1]
    scores = scores_of(query, key_all, same_doc)
    highest = jnp.max(scores, axis=-1, keepdims=True)
    exponent = jnp.exp(scores - highest)
    total = jnp.sum(exponent, axis=-1, keepdims=True)
    log_total = highest + jnp.log(total)
    mixed = jnp.einsum(
        "bhqk,bkhd->bqhd", (exponent / total).astype(BF), heads(value_all),
        preferred_element_type=F32,
    ).astype(BF).reshape(flat)
    first_sum = tok.astype(F32) + mm(mixed, w_out) + b_out
    normed = layer_norm(first_sum, gain_one, shift_one)
    normed_low = normed.astype(BF)
    inner = mm(normed_low, w_in) + b_in
    active = gelu_exact(inner).astype(BF)
    second_sum = normed + mm(active, w_back) + b_back
    result, pull_two = jax.vjp(layer_norm, second_sum, gain_two, shift_two)
    layer_out = result.astype(BF).reshape(tokens.shape)

    d_second_sum, d_gain_two, d_shift_two = pull_two(out_grad.reshape(flat).astype(F32))
    d_second = d_second_sum.astype(BF)
    d_b_back = jnp.sum(d_second.astype(F32), axis=0)
    d_w_back = scatter(jnp.einsum("qf,qd->fd", active, d_second, preferred_element_type=F32))
    d_active = jnp.einsum("qd,fd->qf", d_second, w_back, preferred_element_type=F32)
    d_inner = jax.vjp(gelu_exact, inner)[1](d_active)[0].astype(BF)
    d_b_in = jnp.sum(d_inner.astype(F32), axis=0)
    d_w_in = scatter(jnp.einsum("qd,qf->df", normed_low, d_inner, preferred_element_type=F32))
    d_normed = d_second_sum + jnp.einsum("qf,df->qd", d_inner, w_in, preferred_element_type=F32)
    d_first_sum, d_gain_one, d_shift_one = jax.vjp(layer_norm, first_sum, gain_one, shift_one)[1](
        d_normed
    )
    d_branch = d_first_sum.astype(BF)
    d_b_out = jnp.sum(d_branch.astype(F32), axis=0)
    d_w_out = scatter(jnp.einsum("qd,qe->de", mixed, d_branch, preferred_element_type=F32))
    d_mixed = jnp.einsum("qe,de->qd", d_branch, w_out, preferred_element_type=F32).astype(BF)
    d_mixed = d_mixed.reshape(batch, rows, D)

    attention = jnp.exp(scores_of(query, key_all, same_doc) - log_total)
    d_attention = jnp.einsum(
        "bqhd,bkhd->bhqk", heads(d_mixed), heads(value_all), preferred_element_type=F32
    )
    inner_sum = jnp.sum(d_attention * attention, axis=-1, keepdims=True)
    d_scores = (attention * (d_attention - inner_sum) * HD ** (-0.5)).astype(BF)
    d_query = jnp.einsum(
        "bhqk,bkhd->bqhd", d_scores, heads(key_all), preferred_element_type=F32
    ).reshape(batch, rows, D)
    d_value = jnp.einsum(
        "bhqk,bqhd->bkhd", attention.astype(BF), heads(d_mixed), preferred_element_type=F32
    ).reshape(batch, keys, D)
    d_key = jnp.einsum(
        "bhqk,bqhd->bkhd", d_scores, heads(query), preferred_element_type=F32
    ).reshape(batch, keys, D)
    d_key = lax.psum_scatter(d_key.astype(BF), "seq", scatter_dimension=1, tiled=True).astype(F32)
    d_value = lax.psum_scatter(d_value.astype(BF), "seq", scatter_dimension=1, tiled=True)
    d_joined = jnp.concatenate(
        [
            rotate(d_query, cos_part, -sin_part).astype(BF),
            rotate(d_key, cos_part, -sin_part).astype(BF),
            d_value,
        ],
        axis=-1,
    ).reshape(batch * rows, 3 * D)
    d_b_qkv = jnp.sum(d_joined.astype(F32), axis=0)
    d_w_qkv = scatter(jnp.einsum("qd,qe->de", tok, d_joined, preferred_element_type=F32))
    d_tokens = (
        jnp.einsum("qe,de->qd", d_joined, w_qkv, preferred_element_type=F32) + d_first_sum
    ).reshape(tokens.shape)
    small = scatter_small(
        [d_b_qkv, d_b_out, d_gain_one, d_shift_one, d_b_in, d_b_back, d_gain_two, d_shift_two],
        devices,
    )
    return (
        layer_out, d_tokens, d_w_qkv, small[0], d_w_out, small[1], small[2], small[3],
        d_w_in, small[4], d_w_back, small[5], small[6], small[7],
    )


HBM = pl.BlockSpec(memory_space=pl.ANY)
VMEM = pl.BlockSpec(memory_space=pltpu.VMEM)
MESH = pl.DeviceIdType.MESH
NEVER = -1e30
BOTH, LINE = pl.ds(0, 2), pl.ds(0, 4)
PAIRS = HEADS // 2


def place():
    dp, seq = lax.axis_index("dp"), lax.axis_index("seq")
    return dp // 2, dp % 2, seq // 2, seq % 2


def device(z, y, x, c):
    return (z * 2 + y, x * 2 + c)


def other_z(k, z):
    return lax.rem(z + k, 4)


def greet():
    z, y, x, c = place()
    barrier = pltpu.get_barrier_semaphore()
    partners = [device(z, y, x, 1 - c), device(z, y, 1 - x, c), device(z, 1 - y, x, c)]
    partners += [device(other_z(k, z), y, x, c) for k in (1, 2, 3)]
    for partner in partners:
        pl.semaphore_signal(barrier, inc=1, device_id=partner, device_id_type=MESH)
    pl.semaphore_wait(barrier, len(partners))


class Mail:
    def __init__(self, send_sems, recv_sems):
        self.send_sems, self.recv_sems = send_sems, recv_sems
        self.sent, self.sends, self.slots, self.tag = [], 0, 0, None

    def slot(self, count=1):
        at = self.slots
        self.slots += count
        return at

    def send(self, src, dst, slot, target):
        copy = pltpu.make_async_remote_copy(
            src_ref=src, dst_ref=dst, send_sem=self.send_sems.at[self.sends],
            recv_sem=self.recv_sems.at[slot], device_id=target, device_id_type=MESH,
        )
        self.sent.append((self.tag, copy))
        self.sends += 1
        copy.start()

    def arrived(self, dst, slot):
        z, y, x, c = place()
        pltpu.make_async_remote_copy(
            src_ref=dst, dst_ref=dst, send_sem=self.send_sems.at[0],
            recv_sem=self.recv_sems.at[slot], device_id=device(z, y, x, 1 - c),
            device_id_type=MESH,
        ).wait_recv()

    def finish(self, tags=None):
        for tag, copy in self.sent:
            if tags is None or tag in tags:
                copy.wait_send()
        self.sent = [s for s in self.sent if tags is not None and s[0] not in tags]


def gather_unit(mail, order, at):
    z, y, x, c = place()
    to_x, to_y, to_core = device(z, y, 1 - x, c), device(z, 1 - y, x, c), device(z, y, x, 1 - c)

    def copy(ref, slot, target):
        mail.send(ref, ref, slot, target)

    if order == "xyz":
        s_x, s_y, s_z, s_c = mail.slot(), mail.slot(), mail.slot(4), mail.slot()
        copy(at(z, y, x, c), s_x, to_x)
        yield
        mail.arrived(at(z, y, 1 - x, c), s_x)
        copy(at(z, y, BOTH, c), s_y, to_y)
        yield
        mail.arrived(at(z, 1 - y, BOTH, c), s_y)
        for k in (1, 2, 3):
            copy(at(z, BOTH, BOTH, c), s_z + z, device(other_z(k, z), y, x, c))
        yield
        for k in (1, 2, 3):
            zz = other_z(4 - k, z)
            mail.arrived(at(zz, BOTH, BOTH, c), s_z + zz)
        copy(at(LINE, BOTH, BOTH, c), s_c, to_core)
        yield
        mail.arrived(at(LINE, BOTH, BOTH, 1 - c), s_c)
        return
    s_z, s_one, s_two, s_c = mail.slot(4), mail.slot(), mail.slot(2), mail.slot(2)
    for k in (1, 2, 3):
        copy(at(z, y, x, c), s_z + z, device(other_z(k, z), y, x, c))
    yield
    for k in (1, 2, 3):
        zz = other_z(4 - k, z)
        mail.arrived(at(zz, y, x, c), s_z + zz)
    flip = order == "zxy"
    first, last = (to_x, to_y) if flip else (to_y, to_x)

    def pick(one, two, part):
        here = (x, y) if flip else (y, x)
        one, two = [BOTH if s is None else (1 - h if s else h) for s, h in zip((one, two), here)]
        return at(LINE, two, one, part) if flip else at(LINE, one, two, part)

    copy(pick(0, 0, c), s_one, first)
    copy(pick(0, 0, c), s_two, last)
    yield
    mail.arrived(pick(1, 0, c), s_one)
    copy(pick(1, 0, c), s_two + 1, last)
    copy(pick(None, 0, c), s_c, to_core)
    yield
    mail.arrived(pick(0, 1, c), s_two)
    mail.arrived(pick(1, 1, c), s_two + 1)
    copy(pick(None, 1, c), s_c + 1, to_core)
    yield
    mail.arrived(pick(None, 0, 1 - c), s_c)
    mail.arrived(pick(None, 1, 1 - c), s_c + 1)


def add_into(acc, *landed):
    def one(i, _):
        terms = [acc[i]] + [ref[i] for ref in landed]
        acc[i] = sum(t.astype(F32) for t in terms).astype(acc.dtype)
        return 0

    lax.fori_loop(0, acc.shape[0], one, 0)


def reduce_unit(mail, order, at, landing, done):
    from_core, from_far, from_near, from_z = landing
    z, y, x, c = place()
    to_x, to_y, to_core = device(z, y, 1 - x, c), device(z, 1 - y, x, c), device(z, y, x, 1 - c)
    if order == "xyz":
        s_c, s_z, s_y, s_x = mail.slot(), mail.slot(3), mail.slot(), mail.slot()
        mail.send(at(LINE, BOTH, BOTH, 1 - c), from_core, s_c, to_core)
        yield
        mail.arrived(from_core, s_c)
        add_into(at(LINE, BOTH, BOTH, c), from_core)
        for k in (1, 2, 3):
            zz = other_z(k, z)
            mail.send(at(zz, BOTH, BOTH, c), from_far.at[k - 1], s_z + k - 1, device(zz, y, x, c))
        yield
        for k in (1, 2, 3):
            mail.arrived(from_far.at[k - 1], s_z + k - 1)
        add_into(at(z, BOTH, BOTH, c), *(from_far.at[k] for k in range(3)))
        mail.send(at(z, 1 - y, BOTH, c), from_near, s_y, to_y)
        yield
        mail.arrived(from_near, s_y)
        add_into(at(z, y, BOTH, c), from_near)
        mail.send(at(z, y, 1 - x, c), from_z, s_x, to_x)
        yield
        mail.arrived(from_z, s_x)
        done(at(z, y, x, c)[...].astype(F32) + from_z[...].astype(F32))
        return
    flip = order == "zxy"
    near_link, far_link = (to_x, to_y) if flip else (to_y, to_x)

    def pick(one, two):
        here = (x, y) if flip else (y, x)
        one, two = [BOTH if s is None else (1 - h if s else h) for s, h in zip((one, two), here)]
        return at(LINE, two, one, c) if flip else at(LINE, one, two, c)

    s_c, s_far, s_near, s_z = mail.slot(), mail.slot(), mail.slot(), mail.slot(3)
    mail.send(at(LINE, BOTH, BOTH, 1 - c), from_core, s_c, to_core)
    yield
    mail.arrived(from_core, s_c)
    add_into(at(LINE, BOTH, BOTH, c), from_core)
    mail.send(pick(None, 1), from_far, s_far, far_link)
    yield
    mail.arrived(from_far, s_far)
    add_into(pick(None, 0), from_far)
    mail.send(pick(1, 0), from_near, s_near, near_link)
    yield
    mail.arrived(from_near, s_near)
    add_into(pick(0, 0), from_near)
    for k in (1, 2, 3):
        zz = other_z(k, z)
        mail.send(at(zz, y, x, c), from_z.at[k - 1], s_z + k - 1, device(zz, y, x, c))
    yield
    total = at(z, y, x, c)[...].astype(F32)
    for k in (1, 2, 3):
        mail.arrived(from_z.at[k - 1], s_z + k - 1)
        total = total + from_z[k - 1].astype(F32)
    done(total)


class Plan:
    def __init__(self, mail, gaps, routines):
        self.mail, self.gaps, self.routines, self.at, self.ended = mail, gaps, routines, 0, None

    def gap(self):
        for unit in self.gaps[self.at]:
            self.mail.tag = unit
            if next(self.routines[unit], "end") == "end" and self.ended is not None:
                self.ended(unit)
        self.mail.tag = None
        self.at += 1


def lanes(shape):
    return lax.broadcasted_iota(jnp.int32, shape, len(shape) - 1)


def nt(a, b):
    return lax.dot_general(a, b, (((1,), (1,)), ((), ())), preferred_element_type=F32)


def tn(a, b):
    return lax.dot_general(a, b, (((0,), (0,)), ((), ())), preferred_element_type=F32)


def turn(values, cos_wide, sin_wide):
    count = values.shape[-1]
    even = lanes(values.shape) % 2 == 0
    partner = jnp.where(
        even, pltpu.roll(values, count - 1, axis=1), pltpu.roll(values, 1, axis=1)
    )
    return values * cos_wide + partner * sin_wide


def spread_vector(packed, row, step, lane):
    total = 32 * step
    device_row = lax.broadcasted_iota(jnp.int32, (32, 512), 0) * 16 + row
    pick = (lanes((32, 512)) == device_row).astype(BF)
    slices = mm(pick, packed).astype(BF)
    within = lax.rem(lanes((128, total)), step) + lane
    place_at = (lax.broadcasted_iota(jnp.int32, (128, total), 0) == within).astype(BF)
    placed = mm(slices, place_at)
    owner = lanes((32, total)) // step == lax.broadcasted_iota(jnp.int32, (32, total), 0)
    return jnp.sum(jnp.where(owner, placed, 0.0), axis=0, keepdims=True)


def collect_vector(vector, row, step, lane):
    total = 32 * step
    owner = lanes((32, total)) // step == lax.broadcasted_iota(jnp.int32, (32, total), 0)
    owned = jnp.where(owner, jnp.broadcast_to(vector, (32, total)), 0.0).astype(BF)
    within = lax.rem(lanes((128, total)), step) + lane
    place_at = (lax.broadcasted_iota(jnp.int32, (128, total), 0) == within).astype(BF)
    slices = nt(owned, place_at).astype(BF)
    at = lax.broadcasted_iota(jnp.int32, (512, 32), 0)
    pick = (at == lanes((512, 32)) * 16 + row).astype(BF)
    return mm(pick, slices)


PLACES = (
    ("b_qkv", 0, 72, 0), ("b_in", 1, 96, 0), ("b_out", 2, 24, 0), ("gain_one", 2, 24, 24),
    ("shift_one", 2, 24, 48), ("gain_two", 2, 24, 72), ("shift_two", 2, 24, 96),
    ("b_back", 3, 24, 0),
)
ROW_OF = {name: i for i, (name, _, _, _) in enumerate(PLACES)}


def norm_parts(values):
    center = values - jnp.mean(values, axis=-1, keepdims=True)
    inverse = lax.rsqrt(jnp.mean(center * center, axis=-1, keepdims=True) + EPSILON)
    return center * inverse, inverse


def norm_back(normal, inverse, scaled):
    mean_one = jnp.mean(scaled, axis=-1, keepdims=True)
    mean_two = jnp.mean(scaled * normal, axis=-1, keepdims=True)
    return (scaled - mean_one - normal * mean_two) * inverse


GATHER = (
    ("vec", 0, "zyx"),
    ("qkv", 0, "zxy"),
    ("qkv", 2, "zyx"),
    ("qkv", 1, "zyx"),
    ("out", 0, "xyz"),
    ("in", 0, "zxy"),
    ("in", 1, "zyx"),
    ("in", 2, "zxy"),
    ("in", 3, "zxy"),
    ("back", 0, "zxy"),
    ("back", 1, "xyz"),
    ("back", 2, "zyx"),
    ("back", 3, "zyx"),
)
REDUCE = (
    ("back", 0, "zxy"),
    ("back", 1, "zyx"),
    ("back", 2, "xyz"),
    ("back", 3, "zxy"),
    ("in", 0, "zyx"),
    ("in", 1, "zyx"),
    ("in", 2, "zxy"),
    ("in", 3, "zxy"),
    ("out", 0, "xyz"),
    ("qkv", 0, "zyx"),
    ("qkv", 1, "xyz"),
    ("qkv", 2, "zxy"),
    ("vec", 0, "zyx"),
)
GATHER_GAPS = (
    (),
    (0, 1, 2,),
    (),
    (),
    (0, 3, 0, 0, 1, 2, 4, 0,),
    (3, 4, 5, 6, 7,),
    (),
    (2, 1, 4, 3, 2, 1, 5, 8, 6, 7, 2, 9, 10, 1,),
    (3,),
    (3, 10, 11,),
    (),
    (),
    (5,),
    (7, 8, 6, 10, 9, 12,),
    (5, 11,),
    (5,),
    (4, 12, 7,),
    (8, 6, 9, 11, 7, 4,),
    (12,),
    (),
    (10, 6, 11, 8,),
    (),
    (9,),
    (11, 12, 8, 10,),
    (9, 12,),
    (),
    (),
    (),
)
REDUCE_GAPS = (
    (0, 1, 2, 3,),
    (),
    (),
    (4,),
    (5, 0, 1, 2, 3,),
    (4, 5, 6,),
    (7,),
    (8,),
    (6, 7, 8, 0, 3, 1,),
    (2,),
    (),
    (4, 5, 0, 3, 2, 1, 8,),
    (2, 6,),
    (7, 8,),
    (0, 6, 4, 5, 3, 1,),
    (8,),
    (),
    (9,),
    (7, 10,),
    (11,),
    (9,),
    (),
    (10, 11, 6, 4, 5, 7, 12,),
    (12, 12, 9, 11,),
    (12, 12, 9, 11, 10, 10, 9, 10, 11,),
    (),
)
OUT_GRAD_AFTER = 5


def unit_at(buffers, which, cut):
    buf = buffers[which]
    if which == "vec":
        return lambda z, y, x, part: buf.at[z, y, x, part]
    rows, half = buf.shape[3], buf.shape[4] // 2
    if which == "back":
        return lambda z, y, x, part: buf.at[
            z, y, x, pl.ds(cut * 48, 48), pl.ds(pl.multiple_of(part * half, 128), half)
        ]
    return lambda z, y, x, part: buf.at[
        z, y, x, pl.ds(0, 48), pl.ds(pl.multiple_of(part * half + cut * 384, 128), 384)
    ]


def layer_kernel(rows, *refs):
    refs = iter(refs)
    take = lambda n: [next(refs) for _ in range(n)]
    tokens, out_grad, s_qkv, s_out, s_in, s_back, s_vec, segments, powers = take(9)
    o_layer, o_grad, o_qkv, o_out, o_in, o_back, o_vec = take(7)
    w_qkv, w_out, w_in, w_back, vec = take(5)
    sw_qkv, sw_out, sw_in = take(3)
    landings = take(4 * 12)
    v_core, v_far, v_near, v_z = take(4)
    tok_ref, og_ref, query, keys, values, mixed, normal, inverse, total, normed_low = take(10)
    active, slope, low, lse, layer, sums, dkv, ig_own, ig_send, ig_got, vectors, d_vectors = take(12)
    n_qkv, n_out, n_in, n_back = take(4)
    cos_ref, sin_ref, key_ids, own_ids = take(4)
    send_sems, recv_sems, own_sems = take(3)
    z, y, x, c = place()
    count = 2 * rows
    sibling, partner = device(z, y, x, 1 - c), device(z, y, 1 - x, c)
    wide = lambda start, size: pl.ds(pl.multiple_of(start, 128), size)
    vector = lambda name, cols: vectors[pl.ds(ROW_OF[name], 1), cols]
    all_d = pl.ds(0, D)

    own_copies = [
        pltpu.make_async_copy(tokens.at[x], tok_ref.at[x], own_sems.at[0]),
        pltpu.make_async_copy(out_grad.at[x], og_ref.at[x], own_sems.at[1]),
        pltpu.make_async_copy(s_vec, vec.at[z, y, x, c], own_sems.at[2]),
    ]
    for copy in own_copies:
        copy.start()
    greet()
    mail = Mail(send_sems, recv_sems)

    first_slots = []
    for shard, landing in ((s_qkv, sw_qkv), (s_in, sw_in), (s_out, sw_out)):
        half = landing.shape[1]
        first_slots.append(mail.slot())
        mail.send(shard.at[:, wide((1 - c) * half, half)], landing, first_slots[-1], sibling)
    back_slot = mail.slot()
    back_part = lambda core, part: w_back.at[
        z, y, x, pl.ds(pl.multiple_of(core * 96, 32), 96), wide(part * 384, 384)
    ]
    mail.send(s_back.at[:, wide((1 - c) * 384, 384)], back_part(c, 1 - c), back_slot, sibling)
    tok_slot, og_slot = mail.slot(), mail.slot()
    mail.send(tokens.at[1 - x], tok_ref.at[x], tok_slot, partner)

    def merge(shard, landing, target, slot):
        half = landing.shape[1]
        mail.arrived(landing, slot)
        own = shard[:, wide(c * half, half)].astype(F32)
        other = landing[...].astype(F32)
        first = jnp.where(c == 0, own, other)
        second = jnp.where(c == 0, other, own)
        target[z, y, x, :, wide(c * half, half)] = jnp.concatenate([first, second], 0).astype(BF)

    own_copies[2].wait()
    buffers = {"qkv": w_qkv, "out": w_out, "in": w_in, "back": w_back, "vec": vec}
    plan = Plan(mail, GATHER_GAPS, [
        gather_unit(mail, order, unit_at(buffers, which, cut)) for which, cut, order in GATHER
    ])
    plan.gap()
    merge(s_qkv, sw_qkv, w_qkv, first_slots[0])
    plan.gap()
    plan.gap()
    mail.arrived(back_part(1 - c, c), back_slot)
    back_part(c, c)[...] = s_back[:, wide(c * 384, 384)]
    merge(s_out, sw_out, w_out, first_slots[2])
    merge(s_in, sw_in, w_in, first_slots[1])
    plan.gap()

    ids = segments[pl.ds(x, 1), :].astype(F32)
    quarter = [ids[:, i * rows : (i + 1) * rows] for i in range(4)]
    by_core = [jnp.concatenate([quarter[i], quarter[2 + i]], axis=1) for i in (0, 1)]
    own = jnp.where(c == 0, by_core[0], by_core[1])
    own_ids[...] = own
    for i in (0, 1):
        key_ids[pl.ds(i * count, count), :] = jnp.broadcast_to(by_core[i], (128, count)).T
    own_wide = jnp.broadcast_to(own, (128, count)).T
    lower = jnp.zeros((count, 128), F32)
    for i in range(2 * count // 128):
        lower = lower + (ids[:, i * 128 : (i + 1) * 128] < own_wide).astype(F32)
    start_at = jnp.sum(lower, axis=1, keepdims=True)
    row = lax.broadcasted_iota(jnp.int32, (count, 1), 0)
    token = jnp.where(row < rows, row, row + rows) + c * rows
    angles = (token.astype(F32) - start_at) * powers[...]
    cos_ref[...] = jnp.cos(angles)
    sines = jnp.sin(angles)
    sin_ref[...] = jnp.where(lanes(sines.shape) % 2 == 0, -sines, sines)

    plan.gap()
    packed = vec[...].reshape(512, 128)
    for name, row_, step, lane in PLACES:
        vectors[pl.ds(ROW_OF[name], 1), pl.ds(0, 32 * step)] = spread_vector(packed, row_, step, lane)
    plan.gap()
    plan.gap()
    own_copies[0].wait()
    mail.arrived(tok_ref.at[1 - x], tok_slot)

    def project(start):
        cols = wide(start, 384)
        weight = w_qkv[:, :, :, :, cols].reshape(D, 384)
        return mm(tok_ref[...].reshape(count, D), weight) + vector("b_qkv", cols)

    def turned(start):
        cos = jnp.concatenate([cos_ref[...]] * 3, axis=1)
        sin = jnp.concatenate([sin_ref[...]] * 3, axis=1)
        return turn(project(start), cos, sin).astype(BF)

    def query_part(start):
        query[:, pl.ds(start, 384)] = turned(start) * jnp.asarray(HD ** (-0.5), BF)

    def key_part(start):
        keys[c, :, pl.ds(start - D, 384)] = turned(start)

    def value_part(start):
        values[c, :, pl.ds(start - 2 * D, 384)] = project(start).astype(BF)

    key_slot, value_slot = mail.slot(), mail.slot()
    plan.gap()
    query_part(0)
    key_part(3 * D // 2)
    plan.gap()
    key_part(D)
    value_part(5 * D // 2)
    mail.send(keys.at[c], keys.at[c], key_slot, sibling)
    plan.gap()
    query_part(D // 2)
    value_part(2 * D)
    mail.send(values.at[c], values.at[c], value_slot, sibling)
    plan.gap()
    plan.gap()
    mail.arrived(keys.at[1 - c], key_slot)
    plan.gap()
    mail.arrived(values.at[1 - c], value_slot)

    block = min(256, rows)
    all_keys = 2 * count

    def head_of(values_, s):
        return jnp.where(lanes(values_.shape) // HD == s, values_, jnp.zeros_like(values_))

    def same_doc(at):
        per_key = jnp.concatenate([key_ids[...]] * (block // 128), axis=1)
        return per_key == own_ids[:, at]

    for pair in range(PAIRS):
        cols = pl.ds(pair * 128, 128)
        key = keys[:, :, cols].reshape(all_keys, 128)
        value_t = values[:, :, cols].reshape(all_keys, 128).T

        def attend(i, _, key=key, value_t=value_t, cols=cols, pair=pair):
            at = wide(i * block, block)
            q = query[at, cols]
            same = same_doc(at)
            outs = []
            for s in (0, 1):
                scores = jnp.where(same, nt(key, head_of(q, s)), NEVER)
                highest = jnp.max(scores, axis=0, keepdims=True)
                exponent = jnp.exp(scores - highest)
                row_total = jnp.sum(exponent, axis=0, keepdims=True)
                out = mm(value_t[s * HD : (s + 1) * HD], exponent.astype(BF))
                outs.append(out / row_total)
                lse[pl.ds(2 * pair + s, 1), at] = highest + jnp.log(row_total)
            mixed[at, cols] = jnp.concatenate(outs, axis=0).T.astype(BF)
            return 0

        lax.fori_loop(0, count // block, attend, 0)
        plan.gap()
        if pair == OUT_GRAD_AFTER:
            mail.send(out_grad.at[1 - x], og_ref.at[x], og_slot, partner)

    plan.gap()
    chunk = 128
    chunks = count // chunk
    per_slot = rows // chunk

    def rows_of(ref, i):
        return ref.at[i // per_slot, pl.ds(pl.multiple_of(lax.rem(i, per_slot) * chunk, chunk), chunk)]

    def span(i):
        return pl.ds(pl.multiple_of(i * chunk, chunk), chunk)

    def first_norm(i, _):
        at = span(i)
        branch = mm(mixed[at], w_out[...].reshape(D, D)) + vector("b_out", all_d)
        normal_part, inverse_part = norm_parts(rows_of(tok_ref, i)[...].astype(F32) + branch)
        normal[at] = normal_part
        inverse[at] = inverse_part
        normed = normal_part * vector("gain_one", all_d) + vector("shift_one", all_d)
        normed_low[at] = normed.astype(BF)
        return 0

    lax.fori_loop(0, chunks, first_norm, 0)
    plan.gap()
    for cut in range(4):
        plan.gap()

        def feed(i, _, cut=cut):
            at = pl.ds(pl.multiple_of((i % 2) * rows, rows), rows)
            cols = wide((i // 2) * (FF // 2) + cut * 384, 384)
            weight = w_in[:, :, :, :, cols].reshape(D, 384)
            inner = mm(normed_low[at], weight) + vector("b_in", cols)
            phi = 0.5 + 0.5 * lax.erf(inner * (0.5**0.5))
            density = jnp.exp(-0.5 * inner * inner) * 0.3989422804014327
            active[at, cols] = (inner * phi).astype(BF)
            slope[at, cols] = (phi + inner * density).astype(BF)
            return 0

        lax.fori_loop(0, 4, feed, 0)
    plan.gap()

    def second(i, _):
        cols = wide(i * 256, 256)
        total[:, cols] = mm(active[...], w_back[:, :, :, :, cols].reshape(FF, 256))
        return 0

    lax.fori_loop(0, D // 256, second, 0)
    plan.gap()
    own_copies[1].wait()
    mail.arrived(og_ref.at[1 - x], og_slot)

    def second_norm(i, carry):
        at = span(i)
        normed = normal[at] * vector("gain_one", all_d) + vector("shift_one", all_d)
        part, root = norm_parts(normed + total[at] + vector("b_back", all_d))
        gain = vector("gain_two", all_d)
        rows_of(layer, i)[...] = (part * gain + vector("shift_two", all_d)).astype(BF)
        grad = rows_of(og_ref, i)[...].astype(F32)
        d_sum = norm_back(part, root, grad * gain)
        total[at] = d_sum
        d_low = d_sum.astype(BF)
        low[at] = d_low
        terms = (grad * part, grad, d_low.astype(F32))
        return tuple(k + jnp.sum(t, axis=0, keepdims=True) for k, t in zip(carry, terms))

    zero = jnp.zeros((1, D), F32)
    grads = lax.fori_loop(0, chunks, second_norm, (zero, zero, zero))
    for name, grad in zip(("gain_two", "shift_two", "b_back"), grads):
        d_vectors[pl.ds(ROW_OF[name], 1), all_d] = grad
    mail.finish()
    layer_slot = mail.slot()
    mail.send(layer.at[1 - x], o_layer.at[x], layer_slot, partner)
    layer_own = pltpu.make_async_copy(layer.at[x], o_layer.at[x], own_sems.at[3])
    layer_own.start()


    def inner_grad(i, _):
        cols = wide(i * 384, 384)
        weight = w_back[i // 2, i % 2].reshape(384, D)
        d_inner = (nt(low[...], weight) * slope[:, cols].astype(F32)).astype(BF)
        slope[:, cols] = d_inner
        d_vectors[pl.ds(ROW_OF["b_in"], 1), cols] = jnp.sum(
            d_inner.astype(F32), axis=0, keepdims=True
        )
        return 0

    lax.fori_loop(0, FF // 384, inner_grad, 0)

    def back_grad(i, _):
        grad = tn(active[:, wide(i * 384, 384)], low[...])
        w_back[i // 2, i % 2] = grad.astype(BF).reshape(2, 192, D)
        return 0

    lax.fori_loop(0, FF // 384, back_grad, 0)

    reducers = []
    news = {"qkv": n_qkv, "out": n_out, "in": n_in, "back": n_back}
    for number, (which, cut, order) in enumerate(REDUCE):
        if which == "vec":
            landing = (v_core, v_far, v_near, v_z)

            def done(sum_):
                o_vec[...] = sum_
        else:
            landing = tuple(landings[4 * number : 4 * number + 4])

            def done(sum_, which=which, cut=cut):
                if which == "back":
                    n_back[pl.ds(cut * 48, 48), :] = sum_
                else:
                    news[which][:, pl.ds(cut * 384, 384)] = sum_

        place_of = "back" if which == "qkv" else which
        reducers.append(
            reduce_unit(mail, order, unit_at(buffers, place_of, cut), landing, done)
        )
    finals = []

    def finish_weight(which, out):
        part = news[which]
        half, own_rows = part.shape[1], part.shape[0] // 2
        mine = pl.ds(pl.multiple_of(c * own_rows, 8), own_rows)
        theirs = pl.ds(pl.multiple_of((1 - c) * own_rows, 8), own_rows)
        slot = mail.slot()
        mail.send(part.at[theirs], out.at[:, wide(c * half, half)], slot, sibling)
        own = pltpu.make_async_copy(
            part.at[mine], out.at[:, wide(c * half, half)], own_sems.at[4 + len(finals)]
        )
        own.start()
        finals.append((own, out.at[:, wide((1 - c) * half, half)], slot))

    left = {"back": 4, "in": 4, "out": 1, "qkv": 3, "vec": 1}
    outs = {"qkv": o_qkv, "out": o_out, "in": o_in, "back": o_back}

    def ended(number):
        which = REDUCE[number][0]
        left[which] -= 1
        if which != "vec" and not left[which]:
            finish_weight(which, outs[which])

    plan = Plan(mail, REDUCE_GAPS, reducers)
    plan.ended = ended
    plan.gap()

    def normed_grad(i, _):
        cols = wide(i * 512, 512)
        weight = w_in[:, :, :, :, cols].reshape(D, 512)
        total[...] = total[...] + nt(slope[:, cols], weight)
        return 0

    lax.fori_loop(0, FF // 512, normed_grad, 0)
    plan.gap()

    def first_back(i, carry):
        at = span(i)
        part = normal[at]
        grad = total[at]
        d_sum = norm_back(part, inverse[at], grad * vector("gain_one", all_d))
        total[at] = d_sum
        d_low = d_sum.astype(BF)
        low[at] = d_low
        terms = (grad * part, grad, d_low.astype(F32))
        return tuple(k + jnp.sum(t, axis=0, keepdims=True) for k, t in zip(carry, terms))

    grads = lax.fori_loop(0, chunks, first_back, (zero, zero, zero))
    for name, grad in zip(("gain_one", "shift_one", "b_out"), grads):
        d_vectors[pl.ds(ROW_OF[name], 1), all_d] = grad
    plan.gap()

    for cut in range(4):

        def in_grad(h, _, cut=cut):
            cols = wide(h * (FF // 2) + cut * 384, 384)
            grad = tn(normed_low[...], slope[:, cols])
            w_in[:, :, :, :, cols] = grad.astype(BF).reshape(4, 2, 2, 48, 384)
            return 0

        lax.fori_loop(0, 2, in_grad, 0)
        plan.gap()

    def mixed_grad(i, _):
        at = span(i)
        active[at, pl.ds(3 * D, D)] = nt(low[at], w_out[...].reshape(D, D)).astype(BF)
        return 0

    lax.fori_loop(0, chunks, mixed_grad, 0)

    def out_grad_tile(h, _):
        cols = wide(h * 384, 384)
        grad = tn(mixed[...], low[:, cols])
        w_out[:, :, :, :, cols] = grad.astype(BF).reshape(4, 2, 2, 48, 384)
        return 0

    lax.fori_loop(0, 2, out_grad_tile, 0)
    plan.gap()

    d_slots = []
    for pair in range(PAIRS):
        cols = pl.ds(pair * 128, 128)
        key = keys[:, :, cols].reshape(all_keys, 128)
        key_t = key.T
        value = values[:, :, cols].reshape(all_keys, 128)

        def attend_back(i, _, key=key, key_t=key_t, value=value, cols=cols, pair=pair):
            at = wide(i * block, block)
            q = query[at, cols]
            d_out = active[at, pl.ds(3 * D + pair * 128, 128)]
            product = (d_out.astype(F32) * mixed[at, cols].astype(F32)).T
            same = same_doc(at)
            d_queries = []
            d_key, d_value = sums[0], sums[1]
            for s in (0, 1):
                q_s, d_s = head_of(q, s), head_of(d_out, s)
                delta = jnp.sum(product[s * HD : (s + 1) * HD], axis=0, keepdims=True)
                scores = jnp.where(same, nt(key, q_s), NEVER)
                attention = jnp.exp(scores - lse[pl.ds(2 * pair + s, 1), at])
                d_value = d_value + mm(attention.astype(BF), d_s)
                d_scores = (attention * (nt(value, d_s) - delta)).astype(BF)
                d_key = d_key + mm(d_scores, q_s)
                d_queries.append(mm(key_t[s * HD : (s + 1) * HD], d_scores))
            sums[0], sums[1] = d_key, d_value
            d_query = jnp.concatenate(d_queries, axis=0).T * HD ** (-0.5)
            active[at, cols] = turn(d_query, cos_ref[at], -sin_ref[at]).astype(BF)
            return 0

        sums[...] = jnp.zeros_like(sums)
        lax.fori_loop(0, count // block, attend_back, 0)
        for which in (0, 1):
            for core in (0, 1):
                slope[:, pl.ds(which * 2 * D + core * D + pair * 128, 128)] = sums[
                    which, pl.ds(core * count, count)
                ].astype(BF)
            d_slots.append(mail.slot())
            mail.send(
                slope.at[:, wide(which * 2 * D + (1 - c) * D + pair * 128, 128)],
                dkv.at[which, :, cols], d_slots[-1], sibling,
            )
        plan.gap()

    plan.gap()
    for pair in range(PAIRS):
        for which in (0, 1):
            mail.arrived(dkv.at[which, :, pl.ds(pair * 128, 128)], d_slots[2 * pair + which])

    def own_key_grads(i, _):
        cols = wide(i * 128, 128)
        d_key = slope[:, wide(c * D + i * 128, 128)].astype(F32) + dkv[0, :, cols].astype(F32)
        d_key = turn(d_key, cos_ref[...], -sin_ref[...])
        d_value = slope[:, wide(2 * D + c * D + i * 128, 128)].astype(F32)
        d_value = d_value + dkv[1, :, cols].astype(F32)
        active[:, wide(D + i * 128, 128)] = d_key.astype(BF)
        active[:, wide(2 * D + i * 128, 128)] = d_value.astype(BF)
        return 0

    lax.fori_loop(0, PAIRS, own_key_grads, 0)
    plan.gap()
    plan.gap()
    mail.finish((0, 1, 2, 3))
    for cut in range(3):

        def qkv_grad(h, _, cut=cut):
            grad = tn(tok_ref[...].reshape(count, D), active[:, wide(h * (3 * D // 2) + cut * 384, 384)])
            w_back[:, :, :, pl.ds(cut * 48, 48), wide(h * 384, 384)] = grad.astype(BF).reshape(
                4, 2, 2, 48, 384
            )
            return 0

        lax.fori_loop(0, 2, qkv_grad, 0)
        plan.gap()

    def token_grad(i):
        at = span(i)
        return nt(active[at, pl.ds(0, 3 * D)], w_qkv[...].reshape(D, 3 * D)) + total[at]

    def token_there(i, _):
        ig_send[span(i)] = token_grad((1 - x) * per_slot + i).astype(BF)
        return 0

    lax.fori_loop(0, per_slot, token_there, 0)
    ig_slot = mail.slot()
    mail.send(ig_send, ig_got, ig_slot, partner)
    plan.gap()

    def token_here(i, _):
        ig_own[0, span(i)] = token_grad(x * per_slot + i)
        return 0

    lax.fori_loop(0, per_slot, token_here, 0)
    ig_here = pltpu.make_async_copy(ig_own.at[0], o_grad.at[x], own_sems.at[8])
    ig_here.start()
    plan.gap()
    for i in range(3 * D // 256):
        cols = pl.ds(i * 256, 256)
        d_vectors[pl.ds(ROW_OF["b_qkv"], 1), cols] = jnp.sum(
            active[:, cols].astype(F32), axis=0, keepdims=True
        )
    packed = jnp.zeros((512, 128), F32)
    for name, row, step, lane in PLACES:
        packed = packed + collect_vector(
            d_vectors[pl.ds(ROW_OF[name], 1), pl.ds(0, 32 * step)], row, step, lane
        )
    vec[...] = packed.astype(BF).reshape(4, 2, 2, 2, 16, 128)
    plan.gap()
    plan.gap()
    mail.arrived(ig_got, ig_slot)
    ig_own[1] = ig_got[...].astype(F32)
    ig_there = pltpu.make_async_copy(ig_own.at[1], o_grad.at[1 - x], own_sems.at[9])
    ig_there.start()
    plan.gap()
    for own, landed, slot in finals:
        own.wait()
        mail.arrived(landed, slot)
    mail.arrived(o_layer.at[1 - x], layer_slot)
    layer_own.wait()
    ig_here.wait()
    ig_there.wait()
    mail.finish()


def pack_vectors(parts):
    by_name = dict(zip(("b_qkv", "b_out", "gain_one", "shift_one", "b_in", "b_back", "gain_two", "shift_two"), parts))
    packed = jnp.zeros((2048,), BF)
    for name, row, step, lane in PLACES:
        first = 128 * row + lane
        packed = packed + jnp.pad(by_name[name], (first, 2048 - first - step))
    return packed.reshape(16, 128)


def landing_shapes(order, block):
    far = {"xyz": (3, 2, 2), "zyx": (4, 2), "zxy": (4, 2)}[order]
    near = {"xyz": (2,), "zyx": (4,), "zxy": (4,)}[order]
    last = {"xyz": (), "zyx": (3,), "zxy": (3,)}[order]
    return [pltpu.VMEM(lead + block, BF) for lead in ((4, 2, 2), far, near, last)]


def fast_device(*args):
    (tokens, segment_ids, w_qkv, b_qkv, w_out, b_out, gain_one, shift_one) = args[:8]
    (w_in, b_in, w_back, b_back, gain_two, shift_two, out_grad) = args[8:]
    rows = tokens.shape[1]
    count = 2 * rows
    packed = pack_vectors([b_qkv, b_out, gain_one, shift_one, b_in, b_back, gain_two, shift_two])
    inverse = 10000.0 ** (-2.0 * np.arange(HD // 2, dtype=np.float64) / HD)
    powers = np.tile(np.repeat(inverse, 2), 2).astype(np.float32)[None]
    shape = jax.ShapeDtypeStruct
    landings = [s for _, _, order in REDUCE[:12] for s in landing_shapes(order, (48, 384))]
    vm = pltpu.VMEM
    outs = pl.pallas_call(
        functools.partial(layer_kernel, rows),
        out_shape=[
            shape((2, rows, D), BF), shape((2, rows, D), F32), shape((24, 3 * D), F32),
            shape((24, D), F32), shape((24, FF), F32), shape((96, D), F32), shape((16, 128), F32),
        ],
        in_specs=[HBM, HBM] + [VMEM] * 7,
        out_specs=[HBM] * 6 + [VMEM],
        scratch_shapes=[
            vm((4, 2, 2, 48, 3 * D), BF), vm((4, 2, 2, 48, D), BF), vm((4, 2, 2, 48, FF), BF),
            vm((4, 2, 2, 192, D), BF), vm((4, 2, 2, 2, 16, 128), BF),
            vm((24, 3 * D // 2), BF), vm((24, D // 2), BF), vm((24, FF // 2), BF),
            *landings, *landing_shapes(REDUCE[12][2], (16, 128)),
            vm((2, rows, D), BF), vm((2, rows, D), BF), vm((count, D), BF), vm((2, count, D), BF),
            vm((2, count, D), BF), vm((count, D), BF), vm((count, D), F32), vm((count, 1), F32),
            vm((count, D), F32), vm((count, D), BF),
            vm((count, FF), BF), vm((count, FF), BF), vm((count, D), BF), vm((16, count), F32),
            vm((2, rows, D), BF), vm((2, 2 * count, 128), F32), vm((2, count, D), BF),
            vm((2, rows, D), F32), vm((rows, D), BF), vm((rows, D), BF), vm((8, FF), F32),
            vm((8, FF), F32),
            vm((48, 3 * D // 2), F32), vm((48, D // 2), F32), vm((48, FF // 2), F32),
            vm((192, D // 2), F32),
            vm((count, 128), F32), vm((count, 128), F32), vm((2 * count, 128), F32),
            vm((1, count), F32),
            pltpu.SemaphoreType.DMA((240,)), pltpu.SemaphoreType.DMA((240,)),
            pltpu.SemaphoreType.DMA((10,)),
        ],
        compiler_params=pltpu.CompilerParams(
            collective_id=0, has_side_effects=True, vmem_limit_bytes=63 << 20
        ),
        cost_estimate=pl.CostEstimate(
            flops=28_000_000_000, bytes_accessed=8_000_000, transcendentals=16_000_000
        ),
    )(tokens, out_grad, w_qkv, w_out, w_in, w_back, packed, segment_ids, powers)
    layer_out, input_grad, d_qkv, d_out, d_in, d_back, small = outs
    small = {name: small[row, lane : lane + step] for name, row, step, lane in PLACES}
    return (
        layer_out, input_grad, d_qkv, small["b_qkv"], d_out, small["b_out"], small["gain_one"],
        small["shift_one"], d_in, small["b_in"], d_back, small["b_back"], small["gain_two"],
        small["shift_two"],
    )


def solution(mesh):
    devices = mesh.shape["dp"] * mesh.shape["seq"]
    fast = mesh.shape["dp"] == 8 and mesh.shape["seq"] == 4
    rows3 = P("dp", "seq", None)
    mat, vec = P(ALL, None), P(ALL)
    params = (mat, vec, mat, vec, vec, vec, mat, vec, mat, vec, vec, vec)
    return jax.shard_map(
        fast_device if fast else (lambda *args: on_device(devices, *args)),
        mesh=mesh,
        in_specs=(rows3, P("dp", None)) + params + (rows3,),
        out_specs=(rows3, rows3) + params,
        check_vma=False,
    )
```

```python
import functools
import jax
import jax.numpy as jnp
import numpy as np
from jax import lax
from jax.experimental import pallas as pl
from jax.experimental.pallas import tpu as pltpu
from jax.sharding import PartitionSpec as P

D = 768
HEADS = 12
HD = 64
FF = 3072
EPSILON = 1e-06
ALL = ("dp", "seq")
BF = jnp.bfloat16
F32 = jnp.float32


def mm(a, b):
    return jnp.dot(a, b, preferred_element_type=F32)


def layer_norm(values, gain_vec, shift_vec):
    center = values - jnp.mean(values, axis=-1, keepdims=True)
    spread = jnp.mean(center * center, axis=-1, keepdims=True)
    return center * lax.rsqrt(spread + EPSILON) * gain_vec + shift_vec


def gelu_exact(values):
    return jax.nn.gelu(values, approximate=False)


def rotary_tables(segments, offset, row_count):
    length = segments.shape[-1]
    places = jnp.arange(length, dtype=jnp.int32)[None]
    change = jnp.concatenate(
        [jnp.ones((segments.shape[0], 1), dtype=bool), segments[:, 1:] != segments[:, :-1]], axis=1
    )
    starts = lax.cummax(jnp.where(change, places, 0), axis=1)
    position = lax.dynamic_slice_in_dim(places - starts, offset, row_count, 1).astype(F32)
    inverse = 10000.0 ** (-2.0 * jnp.arange(HD // 2, dtype=F32) / HD)
    angles = position[..., None] * inverse
    return jnp.cos(angles), jnp.sin(angles)


def rotate(values, cos_part, sin_part):
    paired = values.reshape(values.shape[:-1] + (HEADS, HD // 2, 2))
    even, odd = paired[..., 0], paired[..., 1]
    cos_wide, sin_wide = cos_part[..., None, :], sin_part[..., None, :]
    turned = jnp.stack(
        [even * cos_wide - odd * sin_wide, even * sin_wide + odd * cos_wide], axis=-1
    )
    return turned.reshape(values.shape)


def gather(local):
    return lax.all_gather(local, ALL, axis=0, tiled=True)


def gather_small(parts):
    joined = gather(jnp.concatenate(parts)[None])
    out, at = [], 0
    for part in parts:
        n = part.shape[0]
        out.append(joined[:, at : at + n].reshape(-1))
        at += n
    return out


def scatter_small(sums, devices):
    joined = jnp.concatenate([s.reshape(devices, -1) for s in sums], axis=1)
    own = lax.psum_scatter(joined, ALL, scatter_dimension=0, tiled=True)[0]
    out, at = [], 0
    for s in sums:
        n = s.shape[0] // devices
        out.append(own[at : at + n])
        at += n
    return out


def scatter(grad):
    return lax.psum_scatter(grad.astype(BF), ALL, scatter_dimension=0, tiled=True).astype(F32)


def heads(values):
    return values.reshape(values.shape[0], values.shape[1], HEADS, HD)


def scores_of(query, key_all, same_doc):
    raw = jnp.einsum("bqhd,bkhd->bhqk", heads(query), heads(key_all), preferred_element_type=F32)
    return jnp.where(same_doc[:, None], raw * HD ** (-0.5), -1e30)


def on_device(devices, *args):
    (tokens, segment_ids, w_qkv, b_qkv, w_out, b_out, gain_one, shift_one) = args[:8]
    (w_in, b_in, w_back, b_back, gain_two, shift_two, out_grad) = args[8:]
    b_qkv, b_out, gain_one, shift_one, b_in, b_back, gain_two, shift_two = [
        v.astype(F32)
        for v in gather_small([b_qkv, b_out, gain_one, shift_one, b_in, b_back, gain_two, shift_two])
    ]
    w_qkv, w_out, w_in, w_back = gather(w_qkv), gather(w_out), gather(w_in), gather(w_back)
    batch, rows = tokens.shape[:2]
    flat = (batch * rows, D)
    offset = lax.axis_index("seq") * rows
    cos_part, sin_part = rotary_tables(segment_ids, offset, rows)
    own_ids = lax.dynamic_slice_in_dim(segment_ids, offset, rows, 1)
    same_doc = own_ids[:, :, None] == segment_ids[:, None, :]

    tok = tokens.reshape(flat)
    joined = (mm(tok, w_qkv) + b_qkv).reshape(batch, rows, 3 * D)
    query = rotate(joined[..., :D], cos_part, sin_part).astype(BF)
    key = rotate(joined[..., D : 2 * D], cos_part, sin_part).astype(BF)
    value = joined[..., 2 * D :].astype(BF)
    key_all = lax.all_gather(key, "seq", axis=1, tiled=True)
    value_all = lax.all_gather(value, "seq", axis=1, tiled=True)
    keys = key_all.shape[1]
    scores = scores_of(query, key_all, same_doc)
    highest = jnp.max(scores, axis=-1, keepdims=True)
    exponent = jnp.exp(scores - highest)
    total = jnp.sum(exponent, axis=-1, keepdims=True)
    log_total = highest + jnp.log(total)
    mixed = jnp.einsum(
        "bhqk,bkhd->bqhd", (exponent / total).astype(BF), heads(value_all),
        preferred_element_type=F32,
    ).astype(BF).reshape(flat)
    first_sum = tok.astype(F32) + mm(mixed, w_out) + b_out
    normed = layer_norm(first_sum, gain_one, shift_one)
    normed_low = normed.astype(BF)
    inner = mm(normed_low, w_in) + b_in
    active = gelu_exact(inner).astype(BF)
    second_sum = normed + mm(active, w_back) + b_back
    result, pull_two = jax.vjp(layer_norm, second_sum, gain_two, shift_two)
    layer_out = result.astype(BF).reshape(tokens.shape)

    d_second_sum, d_gain_two, d_shift_two = pull_two(out_grad.reshape(flat).astype(F32))
    d_second = d_second_sum.astype(BF)
    d_b_back = jnp.sum(d_second.astype(F32), axis=0)
    d_w_back = scatter(jnp.einsum("qf,qd->fd", active, d_second, preferred_element_type=F32))
    d_active = jnp.einsum("qd,fd->qf", d_second, w_back, preferred_element_type=F32)
    d_inner = jax.vjp(gelu_exact, inner)[1](d_active)[0].astype(BF)
    d_b_in = jnp.sum(d_inner.astype(F32), axis=0)
    d_w_in = scatter(jnp.einsum("qd,qf->df", normed_low, d_inner, preferred_element_type=F32))
    d_normed = d_second_sum + jnp.einsum("qf,df->qd", d_inner, w_in, preferred_element_type=F32)
    d_first_sum, d_gain_one, d_shift_one = jax.vjp(layer_norm, first_sum, gain_one, shift_one)[1](
        d_normed
    )
    d_branch = d_first_sum.astype(BF)
    d_b_out = jnp.sum(d_branch.astype(F32), axis=0)
    d_w_out = scatter(jnp.einsum("qd,qe->de", mixed, d_branch, preferred_element_type=F32))
    d_mixed = jnp.einsum("qe,de->qd", d_branch, w_out, preferred_element_type=F32).astype(BF)
    d_mixed = d_mixed.reshape(batch, rows, D)

    attention = jnp.exp(scores_of(query, key_all, same_doc) - log_total)
    d_attention = jnp.einsum(
        "bqhd,bkhd->bhqk", heads(d_mixed), heads(value_all), preferred_element_type=F32
    )
    inner_sum = jnp.sum(d_attention * attention, axis=-1, keepdims=True)
    d_scores = (attention * (d_attention - inner_sum) * HD ** (-0.5)).astype(BF)
    d_query = jnp.einsum(
        "bhqk,bkhd->bqhd", d_scores, heads(key_all), preferred_element_type=F32
    ).reshape(batch, rows, D)
    d_value = jnp.einsum(
        "bhqk,bqhd->bkhd", attention.astype(BF), heads(d_mixed), preferred_element_type=F32
    ).reshape(batch, keys, D)
    d_key = jnp.einsum(
        "bhqk,bqhd->bkhd", d_scores, heads(query), preferred_element_type=F32
    ).reshape(batch, keys, D)
    d_key = lax.psum_scatter(d_key.astype(BF), "seq", scatter_dimension=1, tiled=True).astype(F32)
    d_value = lax.psum_scatter(d_value.astype(BF), "seq", scatter_dimension=1, tiled=True)
    d_joined = jnp.concatenate(
        [
            rotate(d_query, cos_part, -sin_part).astype(BF),
            rotate(d_key, cos_part, -sin_part).astype(BF),
            d_value,
        ],
        axis=-1,
    ).reshape(batch * rows, 3 * D)
    d_b_qkv = jnp.sum(d_joined.astype(F32), axis=0)
    d_w_qkv = scatter(jnp.einsum("qd,qe->de", tok, d_joined, preferred_element_type=F32))
    d_tokens = (
        jnp.einsum("qe,de->qd", d_joined, w_qkv, preferred_element_type=F32) + d_first_sum
    ).reshape(tokens.shape)
    small = scatter_small(
        [d_b_qkv, d_b_out, d_gain_one, d_shift_one, d_b_in, d_b_back, d_gain_two, d_shift_two],
        devices,
    )
    return (
        layer_out, d_tokens, d_w_qkv, small[0], d_w_out, small[1], small[2], small[3],
        d_w_in, small[4], d_w_back, small[5], small[6], small[7],
    )


HBM = pl.BlockSpec(memory_space=pl.ANY)
VMEM = pl.BlockSpec(memory_space=pltpu.VMEM)
MESH = pl.DeviceIdType.MESH
NEVER = -1e30
BOTH, LINE = pl.ds(0, 2), pl.ds(0, 4)
PAIRS = HEADS // 2


def place():
    dp, seq = lax.axis_index("dp"), lax.axis_index("seq")
    return dp // 2, dp % 2, seq // 2, seq % 2


def device(z, y, x, c):
    return (z * 2 + y, x * 2 + c)


def other_z(k, z):
    return lax.rem(z + k, 4)


def greet():
    z, y, x, c = place()
    barrier = pltpu.get_barrier_semaphore()
    partners = [device(z, y, x, 1 - c), device(z, y, 1 - x, c), device(z, 1 - y, x, c)]
    partners += [device(other_z(k, z), y, x, c) for k in (1, 2, 3)]
    for partner in partners:
        pl.semaphore_signal(barrier, inc=1, device_id=partner, device_id_type=MESH)
    pl.semaphore_wait(barrier, len(partners))


class Mail:
    def __init__(self, send_sems, recv_sems):
        self.send_sems, self.recv_sems = send_sems, recv_sems
        self.sent, self.sends, self.slots, self.tag = [], 0, 0, None

    def slot(self, count=1):
        at = self.slots
        self.slots += count
        return at

    def send(self, src, dst, slot, target):
        copy = pltpu.make_async_remote_copy(
            src_ref=src, dst_ref=dst, send_sem=self.send_sems.at[self.sends],
            recv_sem=self.recv_sems.at[slot], device_id=target, device_id_type=MESH,
        )
        self.sent.append((self.tag, copy))
        self.sends += 1
        copy.start()

    def arrived(self, dst, slot):
        z, y, x, c = place()
        pltpu.make_async_remote_copy(
            src_ref=dst, dst_ref=dst, send_sem=self.send_sems.at[0],
            recv_sem=self.recv_sems.at[slot], device_id=device(z, y, x, 1 - c),
            device_id_type=MESH,
        ).wait_recv()

    def finish(self, tags=None):
        for tag, copy in self.sent:
            if tags is None or tag in tags:
                copy.wait_send()
        self.sent = [s for s in self.sent if tags is not None and s[0] not in tags]


def gather_unit(mail, order, at):
    z, y, x, c = place()
    to_x, to_y, to_core = device(z, y, 1 - x, c), device(z, 1 - y, x, c), device(z, y, x, 1 - c)

    def copy(ref, slot, target):
        mail.send(ref, ref, slot, target)

    if order == "xyz":
        s_x, s_y, s_z, s_c = mail.slot(), mail.slot(), mail.slot(4), mail.slot()
        copy(at(z, y, x, c), s_x, to_x)
        yield
        mail.arrived(at(z, y, 1 - x, c), s_x)
        copy(at(z, y, BOTH, c), s_y, to_y)
        yield
        mail.arrived(at(z, 1 - y, BOTH, c), s_y)
        for k in (1, 2, 3):
            copy(at(z, BOTH, BOTH, c), s_z + z, device(other_z(k, z), y, x, c))
        yield
        for k in (1, 2, 3):
            zz = other_z(4 - k, z)
            mail.arrived(at(zz, BOTH, BOTH, c), s_z + zz)
        copy(at(LINE, BOTH, BOTH, c), s_c, to_core)
        yield
        mail.arrived(at(LINE, BOTH, BOTH, 1 - c), s_c)
        return
    s_z, s_one, s_two, s_c = mail.slot(4), mail.slot(), mail.slot(2), mail.slot(2)
    for k in (1, 2, 3):
        copy(at(z, y, x, c), s_z + z, device(other_z(k, z), y, x, c))
    yield
    for k in (1, 2, 3):
        zz = other_z(4 - k, z)
        mail.arrived(at(zz, y, x, c), s_z + zz)
    flip = order == "zxy"
    first, last = (to_x, to_y) if flip else (to_y, to_x)

    def pick(one, two, part):
        here = (x, y) if flip else (y, x)
        one, two = [BOTH if s is None else (1 - h if s else h) for s, h in zip((one, two), here)]
        return at(LINE, two, one, part) if flip else at(LINE, one, two, part)

    copy(pick(0, 0, c), s_one, first)
    copy(pick(0, 0, c), s_two, last)
    yield
    mail.arrived(pick(1, 0, c), s_one)
    copy(pick(1, 0, c), s_two + 1, last)
    copy(pick(None, 0, c), s_c, to_core)
    yield
    mail.arrived(pick(0, 1, c), s_two)
    mail.arrived(pick(1, 1, c), s_two + 1)
    copy(pick(None, 1, c), s_c + 1, to_core)
    yield
    mail.arrived(pick(None, 0, 1 - c), s_c)
    mail.arrived(pick(None, 1, 1 - c), s_c + 1)


def add_into(acc, *landed):
    def one(i, _):
        terms = [acc[i]] + [ref[i] for ref in landed]
        acc[i] = sum(t.astype(F32) for t in terms).astype(acc.dtype)
        return 0

    lax.fori_loop(0, acc.shape[0], one, 0)


def reduce_unit(mail, order, at, landing, done):
    from_core, from_far, from_near, from_z = landing
    z, y, x, c = place()
    to_x, to_y, to_core = device(z, y, 1 - x, c), device(z, 1 - y, x, c), device(z, y, x, 1 - c)
    if order == "xyz":
        s_c, s_z, s_y, s_x = mail.slot(), mail.slot(3), mail.slot(), mail.slot()
        mail.send(at(LINE, BOTH, BOTH, 1 - c), from_core, s_c, to_core)
        yield
        mail.arrived(from_core, s_c)
        add_into(at(LINE, BOTH, BOTH, c), from_core)
        for k in (1, 2, 3):
            zz = other_z(k, z)
            mail.send(at(zz, BOTH, BOTH, c), from_far.at[k - 1], s_z + k - 1, device(zz, y, x, c))
        yield
        for k in (1, 2, 3):
            mail.arrived(from_far.at[k - 1], s_z + k - 1)
        add_into(at(z, BOTH, BOTH, c), *(from_far.at[k] for k in range(3)))
        mail.send(at(z, 1 - y, BOTH, c), from_near, s_y, to_y)
        yield
        mail.arrived(from_near, s_y)
        add_into(at(z, y, BOTH, c), from_near)
        mail.send(at(z, y, 1 - x, c), from_z, s_x, to_x)
        yield
        mail.arrived(from_z, s_x)
        done(at(z, y, x, c)[...].astype(F32) + from_z[...].astype(F32))
        return
    flip = order == "zxy"
    near_link, far_link = (to_x, to_y) if flip else (to_y, to_x)

    def pick(one, two):
        here = (x, y) if flip else (y, x)
        one, two = [BOTH if s is None else (1 - h if s else h) for s, h in zip((one, two), here)]
        return at(LINE, two, one, c) if flip else at(LINE, one, two, c)

    s_c, s_far, s_near, s_z = mail.slot(), mail.slot(), mail.slot(), mail.slot(3)
    mail.send(at(LINE, BOTH, BOTH, 1 - c), from_core, s_c, to_core)
    yield
    mail.arrived(from_core, s_c)
    add_into(at(LINE, BOTH, BOTH, c), from_core)
    mail.send(pick(None, 1), from_far, s_far, far_link)
    yield
    mail.arrived(from_far, s_far)
    add_into(pick(None, 0), from_far)
    mail.send(pick(1, 0), from_near, s_near, near_link)
    yield
    mail.arrived(from_near, s_near)
    add_into(pick(0, 0), from_near)
    for k in (1, 2, 3):
        zz = other_z(k, z)
        mail.send(at(zz, y, x, c), from_z.at[k - 1], s_z + k - 1, device(zz, y, x, c))
    yield
    total = at(z, y, x, c)[...].astype(F32)
    for k in (1, 2, 3):
        mail.arrived(from_z.at[k - 1], s_z + k - 1)
        total = total + from_z[k - 1].astype(F32)
    done(total)


class Plan:
    def __init__(self, mail, gaps, routines):
        self.mail, self.gaps, self.routines, self.at, self.ended = mail, gaps, routines, 0, None

    def gap(self):
        for unit in self.gaps[self.at]:
            self.mail.tag = unit
            if next(self.routines[unit], "end") == "end" and self.ended is not None:
                self.ended(unit)
        self.mail.tag = None
        self.at += 1


def lanes(shape):
    return lax.broadcasted_iota(jnp.int32, shape, len(shape) - 1)


def nt(a, b):
    return lax.dot_general(a, b, (((1,), (1,)), ((), ())), preferred_element_type=F32)


def tn(a, b):
    return lax.dot_general(a, b, (((0,), (0,)), ((), ())), preferred_element_type=F32)


def turn(values, cos_wide, sin_wide):
    count = values.shape[-1]
    even = lanes(values.shape) % 2 == 0
    partner = jnp.where(
        even, pltpu.roll(values, count - 1, axis=1), pltpu.roll(values, 1, axis=1)
    )
    return values * cos_wide + partner * sin_wide


def spread_vector(packed, row, step, lane):
    total = 32 * step
    device_row = lax.broadcasted_iota(jnp.int32, (32, 512), 0) * 16 + row
    pick = (lanes((32, 512)) == device_row).astype(BF)
    slices = mm(pick, packed).astype(BF)
    within = lax.rem(lanes((128, total)), step) + lane
    place_at = (lax.broadcasted_iota(jnp.int32, (128, total), 0) == within).astype(BF)
    placed = mm(slices, place_at)
    owner = lanes((32, total)) // step == lax.broadcasted_iota(jnp.int32, (32, total), 0)
    return jnp.sum(jnp.where(owner, placed, 0.0), axis=0, keepdims=True)


def collect_vector(vector, row, step, lane):
    total = 32 * step
    owner = lanes((32, total)) // step == lax.broadcasted_iota(jnp.int32, (32, total), 0)
    owned = jnp.where(owner, jnp.broadcast_to(vector, (32, total)), 0.0).astype(BF)
    within = lax.rem(lanes((128, total)), step) + lane
    place_at = (lax.broadcasted_iota(jnp.int32, (128, total), 0) == within).astype(BF)
    slices = nt(owned, place_at).astype(BF)
    at = lax.broadcasted_iota(jnp.int32, (512, 32), 0)
    pick = (at == lanes((512, 32)) * 16 + row).astype(BF)
    return mm(pick, slices)


PLACES = (
    ("b_qkv", 0, 72, 0), ("b_in", 1, 96, 0), ("b_out", 2, 24, 0), ("gain_one", 2, 24, 24),
    ("shift_one", 2, 24, 48), ("gain_two", 2, 24, 72), ("shift_two", 2, 24, 96),
    ("b_back", 3, 24, 0),
)
ROW_OF = {name: i for i, (name, _, _, _) in enumerate(PLACES)}


def norm_parts(values):
    center = values - jnp.mean(values, axis=-1, keepdims=True)
    inverse = lax.rsqrt(jnp.mean(center * center, axis=-1, keepdims=True) + EPSILON)
    return center * inverse, inverse


def norm_back(normal, inverse, scaled):
    mean_one = jnp.mean(scaled, axis=-1, keepdims=True)
    mean_two = jnp.mean(scaled * normal, axis=-1, keepdims=True)
    return (scaled - mean_one - normal * mean_two) * inverse


GATHER = (
    ("vec", 0, "zyx"),
    ("qkv", 0, "zyx"),
    ("qkv", 2, "zxy"),
    ("qkv", 1, "zyx"),
    ("out", 0, "zxy"),
    ("in", 0, "zyx"),
    ("in", 1, "xyz"),
    ("in", 2, "zxy"),
    ("in", 3, "zxy"),
    ("back", 0, "zyx"),
    ("back", 1, "zyx"),
    ("back", 2, "xyz"),
    ("back", 3, "zxy"),
)
REDUCE = (
    ("back", 0, "zxy"),
    ("back", 1, "xyz"),
    ("back", 2, "zyx"),
    ("back", 3, "zyx"),
    ("in", 0, "xyz"),
    ("in", 1, "zxy"),
    ("in", 2, "zyx"),
    ("in", 3, "zyx"),
    ("out", 0, "zxy"),
    ("qkv", 0, "xyz"),
    ("qkv", 1, "zyx"),
    ("qkv", 2, "zxy"),
    ("vec", 0, "zyx"),
)
GATHER_GAPS = (
    (),
    (0, 1,),
    (),
    (),
    (0, 2, 1, 3, 0, 2, 4, 0, 1, 3, 5, 0,),
    (),
    (),
    (4, 6, 2, 3, 5, 7, 6, 8, 1, 7, 9, 1,),
    (2, 8, 10, 6, 4, 5, 9, 11, 3, 2,),
    (3,),
    (7, 10, 12,),
    (11,),
    (4, 8, 9,),
    (5, 4,),
    (11, 12,),
    (),
    (5, 9, 7, 6, 10,),
    (8, 12,),
    (),
    (),
    (9, 10, 7,),
    (),
    (12, 8, 6,),
    (11, 10,),
    (12,),
    (11,),
    (),
    (),
)
REDUCE_GAPS = (
    (0, 1, 2, 3,),
    (),
    (),
    (4,),
    (5,),
    (6,),
    (7,),
    (8,),
    (0, 1, 2, 3,),
    (),
    (4,),
    (0, 5,),
    (),
    (2, 6, 3, 7, 0, 5, 8, 1, 2, 0,),
    (9, 3,),
    (1, 4, 5,),
    (8, 9, 6, 2, 7,),
    (1,),
    (4, 3, 10,),
    (),
    (11,),
    (8,),
    (),
    (4, 5, 6, 10, 7, 11, 12,),
    (12, 8, 12, 11,),
    (12, 6, 7, 10, 11, 12, 9, 10, 9, 11, 9, 10,),
    (),
)
OUT_GRAD_AFTER = 5


def unit_at(buffers, which, cut):
    buf = buffers[which]
    if which == "vec":
        return lambda z, y, x, part: buf.at[z, y, x, part]
    rows, half = buf.shape[3], buf.shape[4] // 2
    if which == "back":
        return lambda z, y, x, part: buf.at[
            z, y, x, pl.ds(cut * 48, 48), pl.ds(pl.multiple_of(part * half, 128), half)
        ]
    return lambda z, y, x, part: buf.at[
        z, y, x, pl.ds(0, 48), pl.ds(pl.multiple_of(part * half + cut * 384, 128), 384)
    ]


QKV_COLUMNS = ((0, D), (2 * D, 5 * D // 2), (D // 2, 3 * D // 2))


def layer_kernel(rows, *refs):
    refs = iter(refs)
    take = lambda n: [next(refs) for _ in range(n)]
    tokens, out_grad, s_qkv, s_out, s_in, s_back, s_vec, segments, powers = take(9)
    o_layer, o_grad, o_qkv, o_out, o_in, o_back, o_vec = take(7)
    w_qkv, w_out, w_in, w_back, vec = take(5)
    sw_qkv, sw_out, sw_in = take(3)
    landings = take(4 * 9 + 3 * 3)
    v_core, v_far, v_near, v_z = take(4)
    tok_ref, og_ref, query, keys, values, mixed, normal, total, normed_low = take(9)
    active, slope, low, lse, dkv, ig_got, vectors, d_vectors = take(8)
    n_qkv, n_out, n_in, n_back = take(4)
    cos_ref, sin_ref, key_wide, own_wide, key_row, own_row = take(6)
    send_sems, recv_sems, own_sems = take(3)
    z, y, x, c = place()
    count = 2 * rows
    sibling, partner = device(z, y, x, 1 - c), device(z, y, 1 - x, c)
    wide = lambda start, size: pl.ds(pl.multiple_of(start, 128), size)
    vector = lambda name, cols: vectors[pl.ds(ROW_OF[name], 1), cols]
    all_d = pl.ds(0, D)

    own_copies = [
        pltpu.make_async_copy(tokens.at[x], tok_ref.at[x], own_sems.at[0]),
        pltpu.make_async_copy(out_grad.at[x], og_ref.at[x], own_sems.at[1]),
        pltpu.make_async_copy(s_vec, vec.at[z, y, x, c], own_sems.at[2]),
    ]
    for copy in own_copies:
        copy.start()
    greet()
    mail = Mail(send_sems, recv_sems)

    first_slots = []
    for shard, landing in ((s_qkv, sw_qkv), (s_in, sw_in), (s_out, sw_out)):
        half = landing.shape[1]
        first_slots.append(mail.slot())
        mail.send(shard.at[:, wide((1 - c) * half, half)], landing, first_slots[-1], sibling)
    back_slot = mail.slot()
    back_part = lambda core, part: w_back.at[
        z, y, x, pl.ds(pl.multiple_of(core * 96, 32), 96), wide(part * 384, 384)
    ]
    mail.send(s_back.at[:, wide((1 - c) * 384, 384)], back_part(c, 1 - c), back_slot, sibling)
    tok_slot, og_slot = mail.slot(), mail.slot()
    mail.send(tokens.at[1 - x], tok_ref.at[x], tok_slot, partner)

    def merge(shard, landing, target, slot):
        half = landing.shape[1]
        mail.arrived(landing, slot)
        own = shard[:, wide(c * half, half)].astype(F32)
        other = landing[...].astype(F32)
        first = jnp.where(c == 0, own, other)
        second = jnp.where(c == 0, other, own)
        target[z, y, x, :, wide(c * half, half)] = jnp.concatenate([first, second], 0).astype(BF)

    own_copies[2].wait()
    buffers = {"qkv": w_qkv, "out": w_out, "in": w_in, "back": w_back, "vec": vec}
    plan = Plan(mail, GATHER_GAPS, [
        gather_unit(mail, order, unit_at(buffers, which, cut)) for which, cut, order in GATHER
    ])
    plan.gap()
    merge(s_qkv, sw_qkv, w_qkv, first_slots[0])
    plan.gap()
    plan.gap()
    mail.arrived(back_part(1 - c, c), back_slot)
    back_part(c, c)[...] = s_back[:, wide(c * 384, 384)]
    merge(s_out, sw_out, w_out, first_slots[2])
    merge(s_in, sw_in, w_in, first_slots[1])
    plan.gap()

    ids = segments[pl.ds(x, 1), :].astype(F32)
    quarter = [ids[:, i * rows : (i + 1) * rows] for i in range(4)]
    by_core = [jnp.concatenate([quarter[i], quarter[2 + i]], axis=1) for i in (0, 1)]
    own = jnp.where(c == 0, by_core[0], by_core[1])
    own_row[...] = own
    key_row[...] = jnp.concatenate(by_core, axis=1)
    for i in (0, 1):
        key_wide[pl.ds(i * count, count), :] = jnp.broadcast_to(by_core[i], (128, count)).T
    own_wide[...] = jnp.broadcast_to(own, (128, count)).T
    lower = jnp.zeros((count, 128), F32)
    for i in range(2 * count // 128):
        lower = lower + (ids[:, i * 128 : (i + 1) * 128] < own_wide[...]).astype(F32)
    start_at = jnp.sum(lower, axis=1, keepdims=True)
    row = lax.broadcasted_iota(jnp.int32, (count, 1), 0)
    token = jnp.where(row < rows, row, row + rows) + c * rows
    angles = (token.astype(F32) - start_at) * powers[...]
    cos_ref[...] = jnp.cos(angles)
    sines = jnp.sin(angles)
    sin_ref[...] = jnp.where(lanes(sines.shape) % 2 == 0, -sines, sines)

    plan.gap()
    packed = vec[...].reshape(512, 128)
    for name, row_, step, lane in PLACES:
        vectors[pl.ds(ROW_OF[name], 1), pl.ds(0, 32 * step)] = spread_vector(packed, row_, step, lane)
    plan.gap()
    plan.gap()
    own_copies[0].wait()
    mail.arrived(tok_ref.at[1 - x], tok_slot)

    def project(start):
        cols = wide(start, 384)
        weight = w_qkv[:, :, :, :, cols].reshape(D, 384)
        return mm(tok_ref[...].reshape(count, D), weight) + vector("b_qkv", cols)

    def turned(start):
        cos = jnp.concatenate([cos_ref[...]] * 3, axis=1)
        sin = jnp.concatenate([sin_ref[...]] * 3, axis=1)
        return turn(project(start), cos, sin).astype(BF)

    def query_part(start):
        query[:, pl.ds(start, 384)] = turned(start) * jnp.asarray(HD ** (-0.5), BF)

    def key_part(start):
        keys[c, :, pl.ds(start - D, 384)] = turned(start)

    def value_part(start):
        values[c, :, pl.ds(start - 2 * D, 384)] = project(start).astype(BF)

    key_slot, value_slot = mail.slot(), mail.slot()
    plan.gap()
    query_part(0)
    key_part(3 * D // 2)
    plan.gap()
    key_part(D)
    value_part(5 * D // 2)
    mail.send(keys.at[c], keys.at[c], key_slot, sibling)
    plan.gap()
    query_part(D // 2)
    value_part(2 * D)
    mail.send(values.at[c], values.at[c], value_slot, sibling)
    plan.gap()
    plan.gap()
    mail.arrived(keys.at[1 - c], key_slot)
    plan.gap()
    mail.arrived(values.at[1 - c], value_slot)

    all_keys = 2 * count

    def head_of(values_, s):
        return jnp.where(lanes(values_.shape) // HD == s, values_, jnp.zeros_like(values_))

    for pair in range(PAIRS):
        cols = pl.ds(pair * 128, 128)
        key = keys[:, :, cols].reshape(all_keys, 128)
        value = values[:, :, cols].reshape(all_keys, 128)
        q = query[:, cols]
        same = jnp.concatenate([own_wide[...]] * (all_keys // 128), axis=1) == key_row[...]
        outs = []
        for s in (0, 1):
            scores = jnp.where(same, nt(head_of(q, s), key), NEVER)
            highest = jnp.max(scores, axis=1, keepdims=True)
            exponent = jnp.exp(scores - highest)
            row_total = jnp.sum(exponent, axis=1, keepdims=True)
            outs.append(mm(exponent.astype(BF), value) / row_total)
            lse[:, pl.ds(2 * pair + s, 1)] = highest + jnp.log(row_total)
        mixed[:, cols] = jnp.where(lanes((count, 128)) < HD, outs[0], outs[1]).astype(BF)
        plan.gap()
        if pair == OUT_GRAD_AFTER:
            mail.send(out_grad.at[1 - x], og_ref.at[x], og_slot, partner)

    plan.gap()
    chunk = rows
    chunks = count // chunk
    per_slot = rows // chunk

    def rows_of(ref, i):
        return ref.at[i // per_slot, pl.ds(pl.multiple_of(lax.rem(i, per_slot) * chunk, chunk), chunk)]

    def span(i):
        return pl.ds(pl.multiple_of(i * chunk, chunk), chunk)

    def branch(h, _):
        cols = wide(h * 384, 384)
        weight = w_out[:, :, :, :, cols].reshape(D, 384)
        total[:, cols] = mm(mixed[...], weight) + vector("b_out", cols)
        return 0

    lax.fori_loop(0, 2, branch, 0, unroll=True)
    for i in range(chunks):
        at = span(i)
        normal_part, inverse_part = norm_parts(rows_of(tok_ref, i)[...].astype(F32) + total[at])
        normal[at] = normal_part
        lse[at, pl.ds(127, 1)] = inverse_part
        normed = normal_part * vector("gain_one", all_d) + vector("shift_one", all_d)
        normed_low[at] = normed.astype(BF)
    plan.gap()
    for cut in range(4):
        plan.gap()

        def feed(h, _, cut=cut):
            cols = wide(h * (FF // 2) + cut * 384, 384)
            weight = w_in[:, :, :, :, cols].reshape(D, 384)
            inner = mm(normed_low[...], weight) + vector("b_in", cols)
            phi = 0.5 + 0.5 * lax.erf(inner * (0.5**0.5))
            density = jnp.exp(-0.5 * inner * inner) * 0.3989422804014327
            active[:, cols] = (inner * phi).astype(BF)
            slope[:, cols] = (phi + inner * density).astype(BF)
            return 0

        lax.fori_loop(0, 2, feed, 0, unroll=True)
    plan.gap()

    def second(i, _):
        cols = wide(i * 384, 384)
        total[:, cols] = mm(active[...], w_back[:, :, :, :, cols].reshape(FF, 384))
        return 0

    lax.fori_loop(0, 2, second, 0)
    plan.gap()
    own_copies[1].wait()
    mail.arrived(og_ref.at[1 - x], og_slot)

    def second_norm(i, carry):
        at = span(i)
        normed = normal[at] * vector("gain_one", all_d) + vector("shift_one", all_d)
        part, root = norm_parts(normed + total[at] + vector("b_back", all_d))
        gain = vector("gain_two", all_d)
        grad = rows_of(og_ref, i)[...].astype(F32)
        rows_of(og_ref, i)[...] = (part * gain + vector("shift_two", all_d)).astype(BF)
        d_sum = norm_back(part, root, grad * gain)
        total[at] = d_sum
        d_low = d_sum.astype(BF)
        low[at] = d_low
        terms = (grad * part, grad, d_low.astype(F32))
        return tuple(k + jnp.sum(t, axis=0, keepdims=True) for k, t in zip(carry, terms))

    zero = jnp.zeros((1, D), F32)
    grads = lax.fori_loop(0, chunks, second_norm, (zero, zero, zero), unroll=True)
    for name, grad in zip(("gain_two", "shift_two", "b_back"), grads):
        d_vectors[pl.ds(ROW_OF[name], 1), all_d] = grad
    mail.finish()
    layer_slot = mail.slot()
    mail.send(og_ref.at[1 - x], o_layer.at[x], layer_slot, partner)
    layer_own = pltpu.make_async_copy(og_ref.at[x], o_layer.at[x], own_sems.at[3])
    layer_own.start()


    def inner_grad(i, _):
        cols = wide(i * 384, 384)
        weight = w_back[i // 2, i % 2].reshape(384, D)
        d_inner = (nt(low[...], weight) * slope[:, cols].astype(F32)).astype(BF)
        slope[:, cols] = d_inner
        d_vectors[pl.ds(ROW_OF["b_in"], 1), cols] = jnp.sum(
            d_inner.astype(F32), axis=0, keepdims=True
        )
        return 0

    lax.fori_loop(0, FF // 384, inner_grad, 0, unroll=2)

    def back_grad(i, _):
        grad = tn(active[:, wide(i * 768, 768)], low[...])
        w_back[i] = grad.astype(BF).reshape(2, 2, 192, D)
        return 0

    lax.fori_loop(0, FF // 768, back_grad, 0)

    reducers = []
    news = {"qkv": n_qkv, "out": n_out, "in": n_in, "back": n_back}
    for number, (which, cut, order) in enumerate(REDUCE):
        if which == "vec":
            landing = (v_core, v_far, v_near, v_z)

            def done(sum_):
                o_vec[...] = sum_
        else:
            rest = 36 + 3 * (number - 9)
            if number < 9:
                landing = landings[4 * number : 4 * number + 4]
            else:
                landing = [landings[4 * (number - 9)]] + landings[rest : rest + 3]

            def done(sum_, which=which, cut=cut):
                if which == "back":
                    n_back[pl.ds(cut * 48, 48), :] = sum_
                else:
                    news[which][:, pl.ds(cut * 384, 384)] = sum_

        place_of = "back" if which == "qkv" else which
        reducers.append(
            reduce_unit(mail, order, unit_at(buffers, place_of, cut), landing, done)
        )
    finals = []

    def finish_part(part, out, columns):
        own_rows = part.shape[0] // 2
        mine = pl.ds(pl.multiple_of(c * own_rows, 8), own_rows)
        theirs = pl.ds(pl.multiple_of((1 - c) * own_rows, 8), own_rows)
        here, there = [
            wide(jnp.where(core == 0, columns[0], columns[1]), part.shape[1]) for core in (c, 1 - c)
        ]
        slot = mail.slot()
        mail.send(part.at[theirs], out.at[:, here], slot, sibling)
        own = pltpu.make_async_copy(part.at[mine], out.at[:, here], own_sems.at[4 + len(finals)])
        own.start()
        finals.append((own, out.at[:, there], slot))

    left = {"back": 4, "in": 4, "out": 1, "qkv": 3, "vec": 1}
    outs = {"qkv": o_qkv, "out": o_out, "in": o_in, "back": o_back}

    def ended(number):
        which, cut, _ = REDUCE[number]
        left[which] -= 1
        if which == "qkv":
            finish_part(n_qkv.at[:, pl.ds(cut * 384, 384)], o_qkv, QKV_COLUMNS[cut])
        elif which != "vec" and not left[which]:
            finish_part(news[which], outs[which], (0, news[which].shape[1]))

    plan = Plan(mail, REDUCE_GAPS, reducers)
    plan.ended = ended
    plan.gap()

    def normed_grad(i, _):
        cols = wide(i * 384, 384)
        weight = w_in[pl.ds(2 * i, 2)].reshape(384, FF)
        total[:, cols] = total[:, cols] + nt(slope[...], weight)
        return 0

    lax.fori_loop(0, 2, normed_grad, 0)
    plan.gap()

    def first_back(i, carry):
        at = span(i)
        part = normal[at]
        grad = total[at]
        d_sum = norm_back(part, lse[at, pl.ds(127, 1)], grad * vector("gain_one", all_d))
        total[at] = d_sum
        d_low = d_sum.astype(BF)
        low[at] = d_low
        terms = (grad * part, grad, d_low.astype(F32))
        return tuple(k + jnp.sum(t, axis=0, keepdims=True) for k, t in zip(carry, terms))

    grads = lax.fori_loop(0, chunks, first_back, (zero, zero, zero), unroll=True)
    for name, grad in zip(("gain_one", "shift_one", "b_out"), grads):
        d_vectors[pl.ds(ROW_OF[name], 1), all_d] = grad
    plan.gap()

    for cut in range(4):

        halves = [pl.ds(h * (FF // 2) + cut * 384, 384) for h in (0, 1)]
        both_halves = jnp.concatenate([slope[:, cols] for cols in halves], axis=1)
        grad = tn(normed_low[...], both_halves).astype(BF)
        for h, cols in enumerate(halves):
            w_in[:, :, :, :, cols] = grad[:, h * 384 : (h + 1) * 384].reshape(4, 2, 2, 48, 384)
        plan.gap()

    def mixed_grad(i, _):
        weight = w_out[pl.ds(2 * i, 2)].reshape(384, D)
        active[:, wide(3 * D + i * 384, 384)] = nt(low[...], weight).astype(BF)
        return 0

    lax.fori_loop(0, 2, mixed_grad, 0, unroll=True)
    w_out[...] = tn(mixed[...], low[...]).astype(BF).reshape(4, 2, 2, 48, D)
    plan.gap()

    d_slots = []
    lse_t = lse[...].T

    def own_key_grads(pairs):
        for pair in pairs:
            cols = pl.ds(pair * 128, 128)
            for which in (0, 1):
                mail.arrived(dkv.at[which, :, cols], d_slots[2 * pair + which])
            d_key = slope[:, wide(c * D + pair * 128, 128)].astype(F32) + dkv[0, :, cols].astype(F32)
            d_key = turn(d_key, cos_ref[...], -sin_ref[...])
            d_value = slope[:, wide(2 * D + c * D + pair * 128, 128)].astype(F32)
            d_value = d_value + dkv[1, :, cols].astype(F32)
            active[:, pl.ds(D + pair * 128, 128)] = d_key.astype(BF)
            active[:, pl.ds(2 * D + pair * 128, 128)] = d_value.astype(BF)

    def qkv_grad(cut):
        mail.finish((cut,))
        starts = QKV_COLUMNS[cut]
        both_halves = jnp.concatenate([active[:, pl.ds(k, 384)] for k in starts], axis=1)
        grad = tn(tok_ref[...].reshape(count, D), both_halves).astype(BF)
        for h in (0, 1):
            w_back[:, :, :, pl.ds(cut * 48, 48), pl.ds(h * 384, 384)] = grad[
                :, h * 384 : (h + 1) * 384
            ].reshape(4, 2, 2, 48, 384)

    for pair in range(PAIRS):
        cols = pl.ds(pair * 128, 128)
        key = keys[:, :, cols].reshape(all_keys, 128)
        key_t = key.T
        value = values[:, :, cols].reshape(all_keys, 128)
        q, d_out = query[:, cols], active[:, pl.ds(3 * D + pair * 128, 128)]
        product = (d_out.astype(F32) * mixed[:, cols].astype(F32)).T
        same = jnp.concatenate([key_wide[...]] * (count // 128), axis=1) == own_row[...]
        d_queries = []
        d_key, d_value = 0.0, 0.0
        for s in (0, 1):
            q_s, d_s = head_of(q, s), head_of(d_out, s)
            delta = jnp.sum(product[s * HD : (s + 1) * HD], axis=0, keepdims=True)
            scores = jnp.where(same, nt(key, q_s), NEVER)
            attention = jnp.exp(scores - lse_t[2 * pair + s : 2 * pair + s + 1])
            d_value = d_value + mm(attention.astype(BF), d_s)
            d_scores = (attention * (nt(value, d_s) - delta)).astype(BF)
            d_key = d_key + mm(d_scores, q_s)
            d_queries.append(mm(key_t[s * HD : (s + 1) * HD], d_scores))
        for which, grad in enumerate((d_key, d_value)):
            for core in (0, 1):
                slope[:, pl.ds(which * 2 * D + core * D + pair * 128, 128)] = grad[
                    core * count : (core + 1) * count
                ].astype(BF)
            d_slots.append(mail.slot())
            mail.send(
                slope.at[:, wide(which * 2 * D + (1 - c) * D + pair * 128, 128)],
                dkv.at[which, :, cols], d_slots[-1], sibling,
            )
        d_query = jnp.concatenate(d_queries, axis=0).T * HD ** (-0.5)
        active[:, cols] = turn(d_query, cos_ref[...], -sin_ref[...]).astype(BF)
        plan.gap()
        if pair == 4:
            own_key_grads((0, 1, 2))
            plan.gap()
            qkv_grad(0)
            plan.gap()

    plan.gap()
    own_key_grads((3, 4, 5))
    for cut in (1, 2):
        plan.gap()
        qkv_grad(cut)
        plan.gap()

    def token_grad(slot, i):
        at = pl.ds(pl.multiple_of(slot * rows, rows), rows)
        weight = w_qkv[pl.ds(2 * i, 2)].reshape(384, 3 * D)
        cols = wide(i * 384, 384)
        return nt(active[at, pl.ds(0, 3 * D)], weight) + total[at, cols]

    def token_there(i, _):
        normed_low[pl.ds(0, rows), wide(i * 384, 384)] = token_grad(1 - x, i).astype(BF)
        return 0

    lax.fori_loop(0, 2, token_there, 0, unroll=True)
    ig_slot = mail.slot()
    mail.send(normed_low.at[pl.ds(0, rows)], ig_got, ig_slot, partner)
    plan.gap()

    def token_here(i, _):
        normal[pl.ds(0, rows), wide(i * 384, 384)] = token_grad(x, i)
        return 0

    lax.fori_loop(0, 2, token_here, 0, unroll=True)
    ig_here = pltpu.make_async_copy(normal.at[pl.ds(0, rows)], o_grad.at[x], own_sems.at[14])
    ig_here.start()
    plan.gap()
    for i in range(3 * D // 256):
        cols = pl.ds(i * 256, 256)
        d_vectors[pl.ds(ROW_OF["b_qkv"], 1), cols] = jnp.sum(
            active[:, cols].astype(F32), axis=0, keepdims=True
        )
    packed = jnp.zeros((512, 128), F32)
    for name, row, step, lane in PLACES:
        packed = packed + collect_vector(
            d_vectors[pl.ds(ROW_OF[name], 1), pl.ds(0, 32 * step)], row, step, lane
        )
    vec[...] = packed.astype(BF).reshape(4, 2, 2, 2, 16, 128)
    plan.gap()
    plan.gap()
    mail.arrived(ig_got, ig_slot)
    normal[pl.ds(rows, rows)] = ig_got[...].astype(F32)
    ig_there = pltpu.make_async_copy(normal.at[pl.ds(rows, rows)], o_grad.at[1 - x], own_sems.at[15])
    ig_there.start()
    plan.gap()
    for own, landed, slot in finals:
        own.wait()
        mail.arrived(landed, slot)
    mail.arrived(o_layer.at[1 - x], layer_slot)
    layer_own.wait()
    ig_here.wait()
    ig_there.wait()
    mail.finish()


def pack_vectors(parts):
    by_name = dict(zip(("b_qkv", "b_out", "gain_one", "shift_one", "b_in", "b_back", "gain_two", "shift_two"), parts))
    packed = jnp.zeros((2048,), BF)
    for name, row, step, lane in PLACES:
        first = 128 * row + lane
        packed = packed + jnp.pad(by_name[name], (first, 2048 - first - step))
    return packed.reshape(16, 128)


def landing_shapes(order, block):
    far = {"xyz": (3, 2, 2), "zyx": (4, 2), "zxy": (4, 2)}[order]
    near = {"xyz": (2,), "zyx": (4,), "zxy": (4,)}[order]
    last = {"xyz": (), "zyx": (3,), "zxy": (3,)}[order]
    return [pltpu.VMEM(lead + block, BF) for lead in ((4, 2, 2), far, near, last)]


def fast_device(*args):
    (tokens, segment_ids, w_qkv, b_qkv, w_out, b_out, gain_one, shift_one) = args[:8]
    (w_in, b_in, w_back, b_back, gain_two, shift_two, out_grad) = args[8:]
    rows = tokens.shape[1]
    count = 2 * rows
    packed = pack_vectors([b_qkv, b_out, gain_one, shift_one, b_in, b_back, gain_two, shift_two])
    inverse = 10000.0 ** (-2.0 * np.arange(HD // 2, dtype=np.float64) / HD)
    powers = np.tile(np.repeat(inverse, 2), 2).astype(np.float32)[None]
    shape = jax.ShapeDtypeStruct
    landings = []
    for number, (_, _, order) in enumerate(REDUCE[:12]):
        landings += landing_shapes(order, (48, 384))[0 if number < 9 else 1 :]
    vm = pltpu.VMEM
    outs = pl.pallas_call(
        functools.partial(layer_kernel, rows),
        out_shape=[
            shape((2, rows, D), BF), shape((2, rows, D), F32), shape((24, 3 * D), F32),
            shape((24, D), F32), shape((24, FF), F32), shape((96, D), F32), shape((16, 128), F32),
        ],
        in_specs=[HBM, HBM] + [VMEM] * 7,
        out_specs=[HBM] * 6 + [VMEM],
        scratch_shapes=[
            vm((4, 2, 2, 48, 3 * D), BF), vm((4, 2, 2, 48, D), BF), vm((4, 2, 2, 48, FF), BF),
            vm((4, 2, 2, 192, D), BF), vm((4, 2, 2, 2, 16, 128), BF),
            vm((24, 3 * D // 2), BF), vm((24, D // 2), BF), vm((24, FF // 2), BF),
            *landings, *landing_shapes(REDUCE[12][2], (16, 128)),
            vm((2, rows, D), BF), vm((2, rows, D), BF), vm((count, D), BF), vm((2, count, D), BF),
            vm((2, count, D), BF), vm((count, D), BF), vm((count, D), F32),
            vm((count, D), F32), vm((count, D), BF),
            vm((count, FF), BF), vm((count, FF), BF), vm((count, D), BF), vm((count, 128), F32),
            vm((2, count, D), BF), vm((rows, D), BF), vm((8, FF), F32),
            vm((8, FF), F32),
            vm((48, 3 * D // 2), F32), vm((48, D // 2), F32), vm((48, FF // 2), F32),
            vm((192, D // 2), F32),
            vm((count, 128), F32), vm((count, 128), F32), vm((2 * count, 128), F32),
            vm((count, 128), F32), vm((1, 2 * count), F32), vm((1, count), F32),
            pltpu.SemaphoreType.DMA((240,)), pltpu.SemaphoreType.DMA((240,)),
            pltpu.SemaphoreType.DMA((16,)),
        ],
        compiler_params=pltpu.CompilerParams(
            collective_id=0, has_side_effects=True, vmem_limit_bytes=63 << 20
        ),
        cost_estimate=pl.CostEstimate(
            flops=28_000_000_000, bytes_accessed=8_000_000, transcendentals=16_000_000
        ),
    )(tokens, out_grad, w_qkv, w_out, w_in, w_back, packed, segment_ids, powers)
    return hand_out(outs)


def hand_out_kernel(*refs):
    sources, packed = refs[:6], refs[6]
    targets, vectors = refs[7:13], refs[13:]
    for source, target in zip(sources, targets):
        target[...] = source[...]
    for (_, row, step, lane), out in zip(PLACES, vectors):
        out[...] = packed[row, pl.ds(lane, step)]


def hand_out(outs):
    shape = jax.ShapeDtypeStruct
    results = pl.pallas_call(
        hand_out_kernel,
        out_shape=[shape(o.shape, o.dtype) for o in outs[:6]]
        + [shape((step,), F32) for _, _, step, _ in PLACES],
        in_specs=[VMEM] * 7,
        out_specs=[VMEM] * (6 + len(PLACES)),
    )(*outs)
    layer_out, input_grad, d_qkv, d_out, d_in, d_back = results[:6]
    small = {name: value for (name, _, _, _), value in zip(PLACES, results[6:])}
    return (
        layer_out, input_grad, d_qkv, small["b_qkv"], d_out, small["b_out"], small["gain_one"],
        small["shift_one"], d_in, small["b_in"], d_back, small["b_back"], small["gain_two"],
        small["shift_two"],
    )


def solution(mesh):
    devices = mesh.shape["dp"] * mesh.shape["seq"]
    fast = mesh.shape["dp"] == 8 and mesh.shape["seq"] == 4
    rows3 = P("dp", "seq", None)
    mat, vec = P(ALL, None), P(ALL)
    params = (mat, vec, mat, vec, vec, vec, mat, vec, mat, vec, vec, vec)
    return jax.shard_map(
        fast_device if fast else (lambda *args: on_device(devices, *args)),
        mesh=mesh,
        in_specs=(rows3, P("dp", None)) + params + (rows3,),
        out_specs=(rows3, rows3) + params,
        check_vma=False,
    )
```
